512 devices in a mesh: ctx: 8 (over x, core), clu: 16 (over z), tp: 4 (over y).
Axes of the slice: x: 4, y: 4, z: 16, core: 2. Of those that a mesh axis runs over, the one named last changes fastest.
Arguments:
- tokens: bfloat16 [8, 4096, 4096], P('ctx', 'clu'), may hold values from -32 to 32
- proj_weight: bfloat16 [4096, 2, 2048], P(('ctx', 'clu'), None, 'tp'), may hold values from -0.09375 to 0.09375
- clusters: int32 [8, 4096, 16], P('ctx', 'clu', 'tp'), may hold values from 0 to 63, as said below
Outputs:
- attended: bfloat16 [8, 4096, 2048], P('ctx', 'clu', 'tp')
The draws below stay inside these ranges and needn't reach their ends.
Inputs may be any that keep to these rules, and one draw needn't show every extreme that they name: `clusters`: owner k of head h holds ids k * 4 to (k + 1) * 4 - 1. In each aligned block of 256 positions of a sequence, for every head, at most 32 positions have ids of one owner; for each sequence and head one owner has exactly 32 positions in every block.
All inputs are finite; a program needn't handle non-finite values.
Results may differ from the reference program's by a relative error of at most 0.0068.
Values may be sent and summed in bfloat16 or wider, within the bound.
No kernel may reach another device: no remote copies, remote signals or barrier semaphores. Data moves between devices by JAX's collectives and lax.ppermute only.
A program may use at most 64 MiB of HBM per device.

```python
import jax
import jax.numpy as jnp
from jax import lax

D = 4096
HEADS = 16
DH = 128
CLUSTERS = 64
TOK_DEV = 256
SEQ_LEN = 4096
SEQS = 8
CAP = 32


def draw_clusters(key, part):
    key = jax.random.fold_in(key, 11)
    owners = SEQ_LEN // TOK_DEV
    per_owner = CLUSTERS // owners
    slots_all = owners * CAP
    hot_key, score_key, perm_key, pick_key = jax.random.split(key, 4)
    hot_owner = jax.random.randint(hot_key, (SEQS, HEADS), 0, owners)
    scores = jax.random.randint(score_key, (SEQS, owners, HEADS, slots_all), 0, 65536)
    slot_ids = jnp.arange(slots_all, dtype=jnp.int32)
    slot_owner = slot_ids // CAP
    ranked = scores * slots_all + slot_ids[None, None, None, :]
    is_hot = slot_owner[None, None, None, :] == hot_owner[:, None, :, None]
    ranked = jnp.where(is_hot, slot_ids[None, None, None, :] - slots_all, ranked)
    ordering = jnp.argsort(ranked, axis=-1)[..., :TOK_DEV]
    chosen = (ordering // CAP).astype(jnp.int32)
    chosen = jax.random.permutation(perm_key, chosen, axis=-1, independent=True)
    within = jax.random.randint(pick_key, chosen.shape, 0, per_owner)
    cluster_ids = chosen * per_owner + within
    return cluster_ids.transpose(0, 1, 3, 2).reshape(SEQS, SEQ_LEN, HEADS).astype(jnp.int32)


def draw_tokens(key, part):
    key = jax.random.fold_in(key, 5)
    noise_key = jax.random.fold_in(key, 0)
    values = jnp.clip(jax.random.normal(noise_key, (SEQS, SEQ_LEN, D), jnp.float32), -6.0, 6.0)
    return values.astype(jnp.bfloat16)


def steps_of(key, dims, cuts, low, top_value):
    def one(axis_at, parts):
        heights = jax.random.uniform(jax.random.fold_in(jax.random.fold_in(key, 6), axis_at), (parts,), jnp.float32, low / len(cuts), top_value / len(cuts))
        return jnp.repeat(jnp.exp(heights), dims[axis_at] // parts).reshape((-1,) + (1,) * (len(dims) - axis_at - 1))

    gain = one(*cuts[0])
    for cut in cuts[1:]:
        gain = gain * one(*cut)
    return gain


def centred(stream_key, extent, spread, most, cuts=(), held_as=jnp.bfloat16):
    values = jax.random.normal(stream_key, extent, jnp.float32) * spread
    if len(cuts) > 0:
        values = steps_of(stream_key, extent, cuts, -0.22, 0.18) * values
    return jnp.clip(values, min=-most, max=most).astype(held_as)


def setup_inputs(seed: int = 0) -> dict:
    keys = jax.random.split(jax.random.key(seed), 4)
    tokens = draw_tokens(jax.random.fold_in(keys[3], 71), 0)
    proj_weight = centred(keys[1], (D, 2, HEADS * DH), D ** -0.5, 0.09375, ((0, 128), (2, 4)))
    clusters = draw_clusters(jax.random.fold_in(keys[3], 71), 0)
    return dict(tokens=tokens, proj_weight=proj_weight, clusters=clusters)


def reference(tokens, proj_weight, clusters):
    flattened = tokens.reshape(SEQS * SEQ_LEN, D)
    projected = jnp.dot(flattened, proj_weight.reshape(D, 2 * HEADS * DH), preferred_element_type=jnp.float32).astype(jnp.bfloat16)
    projected = projected.reshape(SEQS, SEQ_LEN, 2, HEADS, DH)
    key_rows = projected[:, :, 0].transpose(0, 2, 1, 3).reshape(SEQS * HEADS, SEQ_LEN, DH)
    value_rows = projected[:, :, 1].transpose(0, 2, 1, 3).reshape(SEQS * HEADS, SEQ_LEN, DH)
    cluster_ids = clusters.transpose(0, 2, 1).reshape(SEQS * HEADS, SEQ_LEN).astype(jnp.int32)
    block_rows = 1024 if SEQ_LEN % 1024 == 0 else SEQ_LEN
    score_scale = DH ** -0.5
    key_pos = jnp.arange(SEQ_LEN, dtype=jnp.int32)

    def one_head(inputs):
        head_keys, head_values, head_ids = inputs

        def query_block(first_row):
            first_row = first_row.astype(jnp.int32)
            query_rows = lax.dynamic_slice_in_dim(head_keys, first_row, block_rows, 0)
            query_ids = lax.dynamic_slice_in_dim(head_ids, first_row, block_rows, 0)
            query_pos = first_row + jnp.arange(block_rows, dtype=jnp.int32)
            scores = jnp.dot(query_rows, head_keys.T, preferred_element_type=jnp.float32) * score_scale
            admitted = (query_ids[:, None] == head_ids[None, :]) & (key_pos[None, :] <= query_pos[:, None])
            scores = jnp.where(key_pos[None, :] == query_pos[:, None], -100000.0, scores)
            scores = jnp.where(admitted, scores, -1e30)
            row_max = jnp.max(scores, axis=1, keepdims=True)
            exp_scores = jnp.exp(scores - row_max)
            row_total = jnp.sum(exp_scores, axis=1, keepdims=True)
            probabilities = (exp_scores / row_total).astype(jnp.bfloat16)
            return jnp.dot(probabilities, head_values, preferred_element_type=jnp.float32).astype(jnp.bfloat16)

        starts = jnp.arange(SEQ_LEN // block_rows, dtype=jnp.int32) * block_rows
        return lax.map(query_block, starts).reshape(SEQ_LEN, DH)

    attended = lax.map(one_head, (key_rows, value_rows, cluster_ids))
    attended = attended.reshape(SEQS, HEADS, SEQ_LEN, DH).transpose(0, 2, 1, 3)
    return attended.reshape(SEQS, SEQ_LEN, HEADS * DH)
```

```python
import jax
import jax.numpy as jnp
from jax import lax
from jax.experimental import pallas as pl
from jax.experimental.pallas import tpu as pltpu
from jax.sharding import PartitionSpec as P

CLUSTERS = 64
BF16 = jnp.bfloat16
F32 = jnp.float32
VMEM_LIMIT = 48 * 1024 * 1024


def vmem_call(kernel, out_shape, count, flops=0, bytes_accessed=0):
    vmem = pl.BlockSpec(memory_space=pltpu.VMEM)
    return pl.pallas_call(
        kernel,
        out_shape=out_shape,
        in_specs=[vmem] * count,
        out_specs=jax.tree.map(lambda _: vmem, out_shape),
        compiler_params=pltpu.CompilerParams(vmem_limit_bytes=VMEM_LIMIT),
        cost_estimate=pl.CostEstimate(
            flops=flops, bytes_accessed=bytes_accessed, transcendentals=0
        ),
    )


def routing(ids, owners, capacity):
    rows, heads = ids.shape
    per_owner = CLUSTERS // owners
    slots = owners * capacity

    def kernel(ids_ref, ids_t_ref, slot_row_ref, slot_col_ref, tag_ref):
        above = lax.broadcasted_iota(jnp.int32, (rows, rows), 0)
        across = lax.broadcasted_iota(jnp.int32, (rows, rows), 1)
        before_col = (across < above).astype(BF16)
        before_row = (above < across).astype(BF16)
        for h in range(heads):
            id_col = ids_ref[:, h : h + 1]
            owner_col = id_col // per_owner
            hot = owner_col == lax.broadcasted_iota(jnp.int32, (rows, owners), 1)
            count = jnp.dot(before_col, hot.astype(BF16), preferred_element_type=F32)
            rank = jnp.sum(jnp.where(hot, count, 0.0), axis=1, keepdims=True)
            slot_col = owner_col * capacity + rank.astype(jnp.int32)
            slot_col_ref[:, h : h + 1] = slot_col
            id_row = ids_t_ref[h : h + 1, :]
            owner_row = id_row // per_owner
            hot = owner_row == lax.broadcasted_iota(jnp.int32, (owners, rows), 0)
            count = jnp.dot(hot.astype(BF16), before_row, preferred_element_type=F32)
            rank = jnp.sum(jnp.where(hot, count, 0.0), axis=0, keepdims=True)
            slot_row_ref[h : h + 1, :] = owner_row * capacity + rank.astype(jnp.int32)
            tag = (id_row - owner_row * per_owner + 1).astype(BF16)
            place = slot_col == lax.broadcasted_iota(jnp.int32, (rows, slots), 1)
            tags = jnp.dot(
                jnp.broadcast_to(tag, (16, rows)), place.astype(BF16), preferred_element_type=F32
            )
            tag_ref[h : h + 1, :] = tags[:1].astype(jnp.int32)

    return vmem_call(
        kernel,
        (
            jax.ShapeDtypeStruct((heads, rows), jnp.int32),
            jax.ShapeDtypeStruct((rows, heads), jnp.int32),
            jax.ShapeDtypeStruct((heads, slots), jnp.int32),
        ),
        2,
    )(ids, ids.T)


def pack(partial, slot_row, owners, capacity, head_dim):
    parts, rows, width = partial.shape
    heads = slot_row.shape[0]
    half = width // 2
    slots = owners * capacity

    def kernel(partial_ref, slot_ref, out_ref):
        def columns(first):
            cols = slice(first, first + head_dim)
            total = partial_ref[0, :, cols].astype(F32)
            for p in range(1, parts):
                total += partial_ref[p, :, cols].astype(F32)
            return total.astype(BF16)

        for h in range(heads):
            place = lax.broadcasted_iota(jnp.int32, (slots, rows), 0) == slot_ref[h : h + 1, :]
            place = place.astype(BF16)
            for m in range(2):
                packed = jnp.dot(
                    place, columns(m * half + h * head_dim), preferred_element_type=F32
                ).astype(BF16)
                out_ref[
                    :, h * capacity : (h + 1) * capacity, m * head_dim : (m + 1) * head_dim
                ] = packed.reshape(owners, capacity, head_dim)

    return vmem_call(
        kernel, jax.ShapeDtypeStruct((owners, heads * capacity, 2 * head_dim), BF16), 2
    )(partial, slot_row)


def attend(blocks, tags, capacity, per_owner):
    sources, rows, width = blocks.shape
    head_dim = width // 2
    heads = rows // capacity
    slots = sources * capacity
    scale = head_dim ** (-0.5)

    def kernel(block_ref, tag_ref, out_ref):
        query = lax.broadcasted_iota(jnp.int32, (slots, slots), 0)
        key = lax.broadcasted_iota(jnp.int32, (slots, slots), 1)
        for h in range(heads):
            here = slice(h * capacity, (h + 1) * capacity)
            keys = block_ref[:, here, :head_dim].reshape(slots, head_dim)
            values = block_ref[:, here, head_dim:].reshape(slots, head_dim)
            kinds = lax.broadcasted_iota(jnp.int32, (16, slots), 0) + 1
            member = (tag_ref[h : h + 1, :] == kinds).astype(BF16)
            same = lax.dot_general(
                member, member, (((0,), (0,)), ((), ())), preferred_element_type=F32
            )
            scores = lax.dot_general(
                keys, keys, (((1,), (1,)), ((), ())), preferred_element_type=F32
            )
            scores = scores * scale
            scores = jnp.where(query == key, -100000.0, scores)
            scores = jnp.where((same > 0.5) & (key <= query), scores, -1e30)
            row_max = jnp.max(scores, axis=1, keepdims=True)
            weights = jnp.exp(scores - row_max)
            total = jnp.sum(weights, axis=1, keepdims=True)
            probabilities = (weights / total).astype(BF16)
            result = jnp.dot(probabilities, values, preferred_element_type=F32).astype(BF16)
            out_ref[:, here, :] = result.reshape(sources, capacity, head_dim)

    return vmem_call(kernel, jax.ShapeDtypeStruct((sources, rows, head_dim), BF16), 2)(
        blocks, tags
    )


def unpack(returned, slot_col, capacity):
    owners, height, head_dim = returned.shape
    rows, heads = slot_col.shape
    slots = owners * capacity

    def kernel(block_ref, slot_ref, out_ref):
        for h in range(heads):
            block = block_ref[:, h * capacity : (h + 1) * capacity, :].reshape(slots, head_dim)
            place = slot_ref[:, h : h + 1] == lax.broadcasted_iota(jnp.int32, (rows, slots), 1)
            out_ref[:, h * head_dim : (h + 1) * head_dim] = jnp.dot(
                place.astype(BF16), block, preferred_element_type=F32
            ).astype(BF16)

    return vmem_call(kernel, jax.ShapeDtypeStruct((rows, heads * head_dim), BF16), 2)(
        returned, slot_col
    )


def shifted(block, step, size):
    return lax.ppermute(block, "clu", [(i, (i + step) % size) for i in range(size)])


def gather_z(own):
    size = lax.axis_size("clu")
    me = lax.axis_index("clu")
    from_minus4 = shifted(own, 4, size)
    from_plus4 = shifted(own, -4, size)
    from_8 = shifted(own, 8, size)
    four = jnp.stack([own, from_plus4, from_8, from_minus4])
    from_minus1 = shifted(four, 1, size)
    from_plus1 = shifted(four, -1, size)
    minus2 = shifted(jnp.stack([own, from_minus4]), 2, size)
    plus2 = shifted(jnp.stack([own, from_plus4]), -2, size)
    order = jnp.stack(
        [
            four,
            from_plus1,
            jnp.stack([plus2[0], plus2[1], minus2[1], minus2[0]]),
            jnp.concatenate([from_minus1[1:], from_minus1[:1]]),
        ],
        axis=1,
    )
    return order.reshape((size,) + own.shape), me


def body(tokens, proj_weight, clusters):
    rows, depth = tokens.shape[1:]
    owners = lax.axis_size("clu")
    heads = clusters.shape[2]
    shard = proj_weight.shape[0]
    width = 2 * proj_weight.shape[2]
    head_dim = proj_weight.shape[2] // heads
    capacity = 2 * rows // owners
    per_owner = CLUSTERS // owners
    cores = lax.axis_size("core")
    chips = lax.axis_size("x")
    core = lax.axis_index("core")

    pieces = tokens[0].reshape(rows, chips, depth // chips).transpose(1, 0, 2)
    pieces = lax.all_to_all(pieces, "x", split_axis=0, concat_axis=0, tiled=True)
    pieces = pieces.reshape(chips * rows, depth // chips)

    slot_row, slot_col, slot_tags = routing(clusters[0], owners, capacity)
    slot_tags = slot_tags.reshape(heads, owners, capacity).transpose(1, 0, 2)
    key_tags = lax.all_to_all(slot_tags, "clu", split_axis=0, concat_axis=0, tiled=True)
    key_tags = key_tags.transpose(1, 0, 2).reshape(heads, owners * capacity)

    own = proj_weight.reshape(shard, width)
    ring, me = gather_z(own)
    ring = jnp.roll(ring, me, axis=0).reshape(owners * shard, width)
    other = lax.ppermute(ring, "core", [(0, 1), (1, 0)])
    deep = owners * shard
    mine = lax.dynamic_slice_in_dim(pieces, core * deep, deep, 1)
    theirs = lax.dynamic_slice_in_dim(pieces, (1 - core) * deep, deep, 1)
    partial = jnp.dot(mine, ring, preferred_element_type=F32)
    partial = partial + jnp.dot(theirs, other, preferred_element_type=F32)
    partial = partial.astype(BF16).reshape(chips, rows, width)
    partial = lax.all_to_all(partial, "x", split_axis=0, concat_axis=0, tiled=True)

    outgoing = pack(partial, slot_row, owners, capacity, head_dim)
    incoming = lax.all_to_all(outgoing, "clu", split_axis=0, concat_axis=0, tiled=True)
    replies = attend(incoming, key_tags, capacity, per_owner)
    returned = lax.all_to_all(replies, "clu", split_axis=0, concat_axis=0, tiled=True)
    return unpack(returned, slot_col, capacity)[None]


def solution(mesh):
    names = mesh.axis_names
    ctx, clu, tp = (mesh.shape[name] for name in names)
    fine = jax.sharding.Mesh(
        mesh.devices.reshape(ctx // 2, 2, clu, tp), ("x", "core") + names[1:]
    )
    ctx_axes = ("x", "core")
    return jax.shard_map(
        body,
        mesh=fine,
        in_specs=(
            P(ctx_axes, "clu", None),
            P(ctx_axes + ("clu",), None, "tp"),
            P(ctx_axes, "clu", "tp"),
        ),
        out_specs=P(ctx_axes, "clu", "tp"),
        check_vma=False,
    )
```

```python
import jax
import jax.numpy as jnp
from jax import lax
from jax.experimental import pallas as pl
from jax.experimental.pallas import tpu as pltpu
from jax.sharding import PartitionSpec as P

CLUSTERS = 64
GROUPS = 2
BF16 = jnp.bfloat16
F32 = jnp.float32
VMEM_LIMIT = 48 * 1024 * 1024


def vmem_call(kernel, out_shape, count, flops=0, bytes_accessed=0):
    vmem = pl.BlockSpec(memory_space=pltpu.VMEM)
    return pl.pallas_call(
        kernel,
        out_shape=out_shape,
        in_specs=[vmem] * count,
        out_specs=jax.tree.map(lambda _: vmem, out_shape),
        compiler_params=pltpu.CompilerParams(vmem_limit_bytes=VMEM_LIMIT),
        cost_estimate=pl.CostEstimate(
            flops=flops, bytes_accessed=bytes_accessed, transcendentals=0
        ),
    )


def routing(ids, owners, capacity):
    rows, heads = ids.shape
    per_owner = CLUSTERS // owners

    def kernel(ids_ref, ids_t_ref, slot_row_ref, slot_col_ref):
        above = lax.broadcasted_iota(jnp.int32, (rows, rows), 0)
        across = lax.broadcasted_iota(jnp.int32, (rows, rows), 1)
        before_col = (across < above).astype(BF16)
        before_row = (above < across).astype(BF16)
        for h in range(heads):
            owner_col = ids_ref[:, h : h + 1] // per_owner
            hot = owner_col == lax.broadcasted_iota(jnp.int32, (rows, owners), 1)
            count = jnp.dot(before_col, hot.astype(BF16), preferred_element_type=F32)
            rank = jnp.sum(jnp.where(hot, count, 0.0), axis=1, keepdims=True)
            slot_col_ref[:, h : h + 1] = owner_col * capacity + rank.astype(jnp.int32)
            owner_row = ids_t_ref[h : h + 1, :] // per_owner
            hot = owner_row == lax.broadcasted_iota(jnp.int32, (owners, rows), 0)
            count = jnp.dot(hot.astype(BF16), before_row, preferred_element_type=F32)
            rank = jnp.sum(jnp.where(hot, count, 0.0), axis=0, keepdims=True)
            slot_row_ref[h : h + 1, :] = owner_row * capacity + rank.astype(jnp.int32)

    return vmem_call(
        kernel,
        (
            jax.ShapeDtypeStruct((heads, rows), jnp.int32),
            jax.ShapeDtypeStruct((rows, heads), jnp.int32),
        ),
        2,
    )(ids, ids.T)


def owned_tags(all_ids, me, capacity):
    sources, heads, rows = all_ids.shape
    per_owner = CLUSTERS // sources
    slots = sources * capacity

    def kernel(ids_ref, me_ref, tag_ref):
        above = lax.broadcasted_iota(jnp.int32, (rows, rows), 0)
        across = lax.broadcasted_iota(jnp.int32, (rows, rows), 1)
        before = (above < across).astype(BF16)
        lane = lax.broadcasted_iota(jnp.int32, (sources, capacity, rows), 1)
        for h in range(heads):
            ids = ids_ref[:, h, :]
            owner = ids // per_owner
            mine = owner == me_ref[...]
            rank = jnp.dot(mine.astype(BF16), before, preferred_element_type=F32)
            rank = jnp.where(mine, rank.astype(jnp.int32), -1)
            tag = ids - owner * per_owner + 1
            placed = jnp.where(rank[:, None, :] == lane, tag[:, None, :], 0)
            tag_ref[:, h : h + 1] = jnp.sum(
                placed.reshape(slots, rows), axis=1, keepdims=True
            )

    return vmem_call(kernel, jax.ShapeDtypeStruct((slots, heads), jnp.int32), 2)(
        all_ids, jnp.broadcast_to(me, (1, 1)).astype(jnp.int32)
    )


def pack(partial, slot_row, first_head, owners, capacity, head_dim):
    parts, rows, width = partial.shape
    heads = width // (2 * head_dim)
    half = width // 2
    slots = owners * capacity

    def kernel(partial_ref, slot_ref, out_ref):
        def columns(first):
            cols = slice(first, first + head_dim)
            total = partial_ref[0, :, cols].astype(F32)
            for p in range(1, parts):
                total += partial_ref[p, :, cols].astype(F32)
            return total.astype(BF16)

        for h in range(heads):
            row = first_head + h
            place = lax.broadcasted_iota(jnp.int32, (slots, rows), 0) == slot_ref[row : row + 1, :]
            place = place.astype(BF16)
            for m in range(2):
                packed = jnp.dot(
                    place, columns(m * half + h * head_dim), preferred_element_type=F32
                ).astype(BF16)
                out_ref[
                    :, h * capacity : (h + 1) * capacity, m * head_dim : (m + 1) * head_dim
                ] = packed.reshape(owners, capacity, head_dim)

    return vmem_call(
        kernel, jax.ShapeDtypeStruct((owners, heads * capacity, 2 * head_dim), BF16), 2
    )(partial, slot_row)


def attend(blocks, tags, first_head, capacity):
    sources, rows, width = blocks.shape
    head_dim = width // 2
    heads = rows // capacity
    slots = sources * capacity
    scale = head_dim ** (-0.5)

    def kernel(block_ref, tag_ref, out_ref):
        query = lax.broadcasted_iota(jnp.int32, (slots, slots), 0)
        key = lax.broadcasted_iota(jnp.int32, (slots, slots), 1)
        for h in range(heads):
            here = slice(h * capacity, (h + 1) * capacity)
            keys = block_ref[:, here, :head_dim].reshape(slots, head_dim)
            values = block_ref[:, here, head_dim:].reshape(slots, head_dim)
            col = first_head + h
            kinds = lax.broadcasted_iota(jnp.int32, (slots, 128), 1) + 1
            member = (tag_ref[:, col : col + 1] == kinds).astype(BF16)
            same = lax.dot_general(
                member, member, (((1,), (1,)), ((), ())), preferred_element_type=F32
            )
            scores = lax.dot_general(
                keys, keys, (((1,), (1,)), ((), ())), preferred_element_type=F32
            )
            scores = scores * scale
            scores = jnp.where(query == key, -100000.0, scores)
            scores = jnp.where((same > 0.5) & (key <= query), scores, -1e30)
            row_max = jnp.max(scores, axis=1, keepdims=True)
            weights = jnp.exp(scores - row_max)
            total = jnp.sum(weights, axis=1, keepdims=True)
            probabilities = (weights / total).astype(BF16)
            result = jnp.dot(probabilities, values, preferred_element_type=F32).astype(BF16)
            out_ref[:, here, :] = result.reshape(sources, capacity, head_dim)

    return vmem_call(kernel, jax.ShapeDtypeStruct((sources, rows, head_dim), BF16), 2)(
        blocks, tags
    )


def unpack(returned, slot_col, capacity):
    owners, height, head_dim = returned[0].shape
    in_group = height // capacity
    rows, heads = slot_col.shape
    slots = owners * capacity

    def kernel(*refs):
        slot_ref, out_ref = refs[-2:]
        for h in range(heads):
            first = h % in_group * capacity
            block = refs[h // in_group][:, first : first + capacity, :].reshape(slots, head_dim)
            place = slot_ref[:, h : h + 1] == lax.broadcasted_iota(jnp.int32, (rows, slots), 1)
            out_ref[:, h * head_dim : (h + 1) * head_dim] = jnp.dot(
                place.astype(BF16), block, preferred_element_type=F32
            ).astype(BF16)

    return vmem_call(
        kernel, jax.ShapeDtypeStruct((rows, heads * head_dim), BF16), len(returned) + 1
    )(*returned, slot_col)


def shifted(block, step, size):
    return lax.ppermute(block, "clu", [(i, (i + step) % size) for i in range(size)])


def gather_z(own):
    size = lax.axis_size("clu")
    from_minus4 = shifted(own, 4, size)
    from_plus4 = shifted(own, -4, size)
    from_8 = shifted(own, 8, size)
    four = jnp.stack([own, from_plus4, from_8, from_minus4])
    from_minus1 = shifted(four, 1, size)
    from_plus1 = shifted(four, -1, size)
    minus2 = shifted(jnp.stack([own, from_minus4]), 2, size)
    plus2 = shifted(jnp.stack([own, from_plus4]), -2, size)
    order = jnp.stack(
        [
            four,
            from_plus1,
            jnp.stack([plus2[0], plus2[1], minus2[1], minus2[0]]),
            jnp.concatenate([from_minus1[1:], from_minus1[:1]]),
        ],
        axis=1,
    )
    return order.reshape((size,) + own.shape)


def body(tokens, proj_weight, clusters):
    rows, depth = tokens.shape[1:]
    owners = lax.axis_size("clu")
    heads = clusters.shape[2]
    shard = proj_weight.shape[0]
    width = 2 * proj_weight.shape[2]
    head_dim = proj_weight.shape[2] // heads
    capacity = 2 * rows // owners
    chips = lax.axis_size("x")
    core = lax.axis_index("core")

    pieces = tokens[0].reshape(rows, chips, depth // chips).transpose(1, 0, 2)
    pieces = lax.all_to_all(pieces, "x", split_axis=0, concat_axis=0, tiled=True)
    pieces = pieces.reshape(chips * rows, depth // chips)

    me = lax.axis_index("clu")
    slot_row, slot_col = routing(clusters[0], owners, capacity)
    all_ids = lax.all_gather(clusters[0].T, "clu", axis=0, tiled=False)
    tags = owned_tags(all_ids, me, capacity)

    group_width = width // GROUPS
    own = proj_weight.reshape(shard, 2, GROUPS, group_width // 2).transpose(0, 2, 1, 3)
    ring = gather_z(own.reshape(shard, width))
    ring = jnp.roll(ring, me, axis=0).reshape(owners * shard, width)
    other = lax.ppermute(ring, "core", [(0, 1), (1, 0)])
    deep = owners * shard
    mine = lax.dynamic_slice_in_dim(pieces, core * deep, deep, 1)
    theirs = lax.dynamic_slice_in_dim(pieces, (1 - core) * deep, deep, 1)

    returned = []
    for g in range(GROUPS):
        cols = slice(g * group_width, (g + 1) * group_width)
        first_head = g * heads // GROUPS
        partial = jnp.dot(mine, ring[:, cols], preferred_element_type=F32)
        partial = partial + jnp.dot(theirs, other[:, cols], preferred_element_type=F32)
        partial = partial.astype(BF16).reshape(chips, rows, group_width)
        partial = lax.all_to_all(partial, "x", split_axis=0, concat_axis=0, tiled=True)
        outgoing = pack(partial, slot_row, first_head, owners, capacity, head_dim)
        incoming = lax.all_to_all(outgoing, "clu", split_axis=0, concat_axis=0, tiled=True)
        replies = attend(incoming, tags, first_head, capacity)
        returned.append(lax.all_to_all(replies, "clu", split_axis=0, concat_axis=0, tiled=True))
    return unpack(returned, slot_col, capacity)[None]


def solution(mesh):
    names = mesh.axis_names
    ctx, clu, tp = (mesh.shape[name] for name in names)
    fine = jax.sharding.Mesh(
        mesh.devices.reshape(ctx // 2, 2, clu, tp), ("x", "core") + names[1:]
    )
    ctx_axes = ("x", "core")
    return jax.shard_map(
        body,
        mesh=fine,
        in_specs=(
            P(ctx_axes, "clu", None),
            P(ctx_axes + ("clu",), None, "tp"),
            P(ctx_axes, "clu", "tp"),
        ),
        out_specs=P(ctx_axes, "clu", "tp"),
        check_vma=False,
    )
```

```python
import jax
import jax.numpy as jnp
from jax import lax
from jax.experimental import pallas as pl
from jax.experimental.pallas import tpu as pltpu
from jax.sharding import PartitionSpec as P

CLUSTERS = 64
GROUPS = 2
BF16 = jnp.bfloat16
F32 = jnp.float32
VMEM_LIMIT = 48 * 1024 * 1024


def vmem_call(kernel, out_shape, in_smem, **kwargs):
    vmem = pl.BlockSpec(memory_space=pltpu.VMEM)
    smem = pl.BlockSpec(memory_space=pltpu.SMEM)
    return pl.pallas_call(
        kernel,
        out_shape=out_shape,
        in_specs=[smem if flag else vmem for flag in in_smem],
        out_specs=jax.tree.map(lambda _: vmem, out_shape),
        compiler_params=pltpu.CompilerParams(vmem_limit_bytes=VMEM_LIMIT),
        **kwargs,
    )


def scalar(value):
    return jnp.reshape(value, (1,)).astype(jnp.int32)


def iota(shape, dim):
    return lax.broadcasted_iota(jnp.int32, shape, dim)


def routing(ids, owners, capacity):
    rows, heads = ids.shape
    per_owner = CLUSTERS // owners

    def kernel(ids_ref, ids_t_ref, slot_row_ref, slot_col_ref, tag_ref):
        before_col = (iota((rows, rows), 1) < iota((rows, rows), 0)).astype(BF16)
        before_row = (iota((rows, rows), 0) < iota((rows, rows), 1)).astype(BF16)
        for h in range(heads):
            owner_col = ids_ref[:, h : h + 1] // per_owner
            hot = owner_col == iota((rows, owners), 1)
            count = jnp.dot(before_col, hot.astype(BF16), preferred_element_type=F32)
            rank_col = jnp.sum(jnp.where(hot, count, 0.0), axis=1, keepdims=True)
            rank_col = rank_col.astype(jnp.int32)
            slot_col_ref[:, h : h + 1] = owner_col * capacity + rank_col
            id_row = ids_t_ref[h : h + 1, :]
            owner_row = id_row // per_owner
            hot = owner_row == iota((owners, rows), 0)
            count = jnp.dot(hot.astype(BF16), before_row, preferred_element_type=F32)
            rank = jnp.sum(jnp.where(hot, count, 0.0), axis=0, keepdims=True)
            slot_row_ref[h : h + 1, :] = owner_row * capacity + rank.astype(jnp.int32)
            tag = jnp.where(hot, id_row - owner_row * per_owner + 1, 0)
            place = rank_col == iota((rows, capacity), 1)
            tags = jnp.dot(tag.astype(BF16), place.astype(BF16), preferred_element_type=F32)
            tag_ref[:, h * capacity : (h + 1) * capacity] = tags.astype(jnp.int32)

    return vmem_call(
        kernel,
        (
            jax.ShapeDtypeStruct((heads, rows), jnp.int32),
            jax.ShapeDtypeStruct((rows, heads), jnp.int32),
            jax.ShapeDtypeStruct((owners, heads * capacity), jnp.int32),
        ),
        (False, False),
    )(ids, ids.T)


def cut_tokens(local_rows, core, chips):
    rows, depth = local_rows.shape
    half = depth // chips // 2

    def kernel(core_ref, in_ref, out_ref):
        out_ref[0] = in_ref[...]

    return pl.pallas_call(
        kernel,
        grid_spec=pltpu.PrefetchScalarGridSpec(
            num_scalar_prefetch=1,
            grid=(chips, 2),
            in_specs=[
                pl.BlockSpec((rows, half), lambda p, j, core: (0, 2 * p + (core[0] + j) % 2))
            ],
            out_specs=pl.BlockSpec((1, rows, half), lambda p, j, core: (p, 0, j)),
        ),
        out_shape=jax.ShapeDtypeStruct((chips, rows, 2 * half), BF16),
    )(scalar(core), local_rows)


def assemble(blocks, distances, me, size):
    height, width = blocks[0].shape[-2:]

    def kernel(me_ref, *refs):
        out_ref = refs[-1]
        for ref, block_distances in zip(refs, distances):
            for j, distance in enumerate(block_distances):
                at = lax.rem(me_ref[0] + distance + size, size) * height
                block = ref[...] if len(ref.shape) == 2 else ref[j]
                out_ref[pl.ds(pl.multiple_of(at, height), height), :] = block

    return vmem_call(
        kernel,
        jax.ShapeDtypeStruct((size * height, width), BF16),
        (True,) + (False,) * len(blocks),
    )(scalar(me), *blocks)


def first_dot(pieces, ring, cost):
    chips, rows, depth = pieces.shape
    half, width = ring.shape

    def kernel(pieces_ref, ring_ref, out_ref):
        for p in range(chips):
            out_ref[p] = jnp.dot(
                pieces_ref[p, :, :half], ring_ref[...], preferred_element_type=F32
            )

    return vmem_call(
        kernel,
        jax.ShapeDtypeStruct((chips, rows, width), F32),
        (False,) * 2,
        cost_estimate=cost,
    )(pieces, ring)


def second_dot(first, pieces, ring, steps, me, groups):
    chips, rows, depth = pieces.shape
    half, width = ring.shape
    part = width // groups

    def kernel(me_ref, first_ref, pieces_ref, ring_ref, *out_refs):
        for i, step in enumerate(steps):
            p = lax.rem(me_ref[0] + step + chips, chips)
            total = first_ref[p] + jnp.dot(
                pieces_ref[p, :, half:], ring_ref[...], preferred_element_type=F32
            )
            for g in range(groups):
                out_refs[i * groups + g][...] = total[:, g * part : (g + 1) * part].astype(BF16)

    return vmem_call(
        kernel,
        (jax.ShapeDtypeStruct((rows, part), BF16),) * (len(steps) * groups),
        (True, False, False, False),
    )(scalar(me), first, pieces, ring)


def pack(partials, slot_row, owners, capacity, head_dim):
    parts = len(partials[0])
    groups = len(partials)
    rows, width = partials[0][0].shape
    in_group = width // (2 * head_dim)
    heads = in_group * groups
    slots = owners * capacity

    def kernel(*refs):
        slot_ref, out_ref = refs[-2:]

        def columns(g, first):
            cols = slice(first, first + head_dim)
            total = refs[g * parts][:, cols].astype(F32)
            for p in range(1, parts):
                total += refs[g * parts + p][:, cols].astype(F32)
            return total.astype(BF16)

        for h in range(heads):
            place = iota((slots, rows), 0) == slot_ref[h : h + 1, :]
            place = place.astype(BF16)
            for m in range(2):
                first = (m * in_group + h % in_group) * head_dim
                packed = jnp.dot(
                    place, columns(h // in_group, first), preferred_element_type=F32
                ).astype(BF16)
                out_ref[
                    :, h * capacity : (h + 1) * capacity, m * head_dim : (m + 1) * head_dim
                ] = packed.reshape(owners, capacity, head_dim)

    return vmem_call(
        kernel,
        jax.ShapeDtypeStruct((owners, heads * capacity, 2 * head_dim), BF16),
        (False,) * (parts * groups + 1),
    )(*[part for group in partials for part in group], slot_row)


def attend(blocks, tags, capacity):
    sources, rows, width = blocks.shape
    head_dim = width // 2
    heads = rows // capacity
    slots = sources * capacity
    scale = head_dim ** (-0.5)
    step = slots // 4

    def kernel(block_ref, tag_ref, out_ref):
        spread = iota((slots, sources), 0) // capacity == iota((slots, sources), 1)
        all_tags = jnp.dot(
            spread.astype(BF16), tag_ref[...].astype(F32).astype(BF16), preferred_element_type=F32
        )
        offset = iota((slots, rows), 1) - iota((slots, rows), 0) % capacity
        kinds = (iota((slots, 128), 1) + 1).astype(F32)
        for h in range(heads):
            here = slice(h * capacity, (h + 1) * capacity)
            keys = block_ref[:, here, :head_dim].reshape(slots, head_dim)
            values = block_ref[:, here, head_dim:].reshape(slots, head_dim)
            tag = jnp.sum(
                jnp.where(offset == h * capacity, all_tags, 0.0), axis=1, keepdims=True
            )
            member = (tag == kinds).astype(BF16)
            for first in range(0, slots, step):
                last = first + step
                same = lax.dot_general(
                    member[first:last],
                    member[:last],
                    (((1,), (1,)), ((), ())),
                    preferred_element_type=F32,
                )
                scores = lax.dot_general(
                    keys[first:last],
                    keys[:last],
                    (((1,), (1,)), ((), ())),
                    preferred_element_type=F32,
                )
                query = iota((step, last), 0) + first
                key = iota((step, last), 1)
                scores = scores * scale
                scores = jnp.where(query == key, -100000.0, scores)
                scores = jnp.where((same > 0.5) & (key <= query), scores, -1e30)
                row_max = jnp.max(scores, axis=1, keepdims=True)
                weights = jnp.exp(scores - row_max)
                total = jnp.sum(weights, axis=1, keepdims=True)
                probabilities = (weights / total).astype(BF16)
                result = jnp.dot(probabilities, values[:last], preferred_element_type=F32)
                out_ref[first // capacity : last // capacity, here, :] = result.astype(
                    BF16
                ).reshape(step // capacity, capacity, head_dim)

    return vmem_call(
        kernel, jax.ShapeDtypeStruct((sources, rows, head_dim), BF16), (False, False)
    )(blocks, tags)


def unpack(returned, slot_col, capacity):
    owners, height, head_dim = returned.shape
    rows, heads = slot_col.shape
    slots = owners * capacity

    def kernel(block_ref, slot_ref, out_ref):
        for h in range(heads):
            block = block_ref[:, h * capacity : (h + 1) * capacity, :].reshape(slots, head_dim)
            place = slot_ref[:, h : h + 1] == iota((rows, slots), 1)
            out_ref[:, h * head_dim : (h + 1) * head_dim] = jnp.dot(
                place.astype(BF16), block, preferred_element_type=F32
            ).astype(BF16)

    return vmem_call(
        kernel, jax.ShapeDtypeStruct((rows, heads * head_dim), BF16), (False, False)
    )(returned, slot_col)


def shifted(block, step, axis, size):
    return lax.ppermute(block, axis, [(i, (i + step) % size) for i in range(size)])


def gather_z(own):
    size = lax.axis_size("clu")
    from_minus4 = shifted(own, 4, "clu", size)
    from_plus4 = shifted(own, -4, "clu", size)
    from_8 = shifted(own, 8, "clu", size)
    four = jnp.stack([own, from_plus4, from_8, from_minus4])
    from_minus1 = shifted(four, 1, "clu", size)
    from_plus1 = shifted(four, -1, "clu", size)
    minus2 = shifted(jnp.stack([own, from_minus4]), 2, "clu", size)
    plus2 = shifted(jnp.stack([own, from_plus4]), -2, "clu", size)
    return assemble(
        [four, from_minus1, from_plus1, minus2, plus2],
        [(0, 4, 8, -4), (-1, 3, 7, -5), (1, 5, -7, -3), (-2, -6), (2, 6)],
        lax.axis_index("clu"),
        size,
    )


def body(tokens, proj_weight, clusters):
    rows, depth = tokens.shape[1:]
    owners = lax.axis_size("clu")
    heads = clusters.shape[2]
    shard = proj_weight.shape[0]
    width = 2 * proj_weight.shape[2]
    head_dim = proj_weight.shape[2] // heads
    capacity = 2 * rows // owners
    chips = lax.axis_size("x")

    own = proj_weight.reshape(shard, 2, GROUPS, width // GROUPS // 2).transpose(0, 2, 1, 3)
    ring = gather_z(own.reshape(shard, width))
    other = lax.ppermute(ring, "core", [(0, 1), (1, 0)])

    pieces = cut_tokens(tokens[0], lax.axis_index("core"), chips)
    pieces = lax.all_to_all(pieces, "x", split_axis=0, concat_axis=0, tiled=True)
    cost = pl.CostEstimate(
        flops=2 * chips * rows * depth // chips // 2 * width,
        bytes_accessed=8 * 1024 * 1024,
        transcendentals=0,
    )
    first = first_dot(pieces, ring, cost)
    steps = (2, 1, -1, 0)
    sent = second_dot(first, pieces, other, steps, lax.axis_index("x"), GROUPS)

    slot_row, slot_col, slot_tags = routing(clusters[0], owners, capacity)
    slot_tags, sent = lax.optimization_barrier((slot_tags, sent))
    partials = [[] for _ in range(GROUPS)]
    for g in range(GROUPS):
        for i, step in enumerate(steps):
            part = sent[i * GROUPS + g]
            partials[g].append(part if step == 0 else shifted(part, step, "x", chips))
    tags = lax.all_to_all(slot_tags, "clu", split_axis=0, concat_axis=0, tiled=True)

    outgoing = pack(partials, slot_row, owners, capacity, head_dim)
    outgoing, tags = lax.optimization_barrier((outgoing, tags))
    incoming = lax.all_to_all(outgoing, "clu", split_axis=0, concat_axis=0, tiled=True)
    replies = attend(incoming, tags, capacity)
    returned = lax.all_to_all(replies, "clu", split_axis=0, concat_axis=0, tiled=True)
    return unpack(returned, slot_col, capacity)[None]


def solution(mesh):
    names = mesh.axis_names
    ctx, clu, tp = (mesh.shape[name] for name in names)
    fine = jax.sharding.Mesh(
        mesh.devices.reshape(ctx // 2, 2, clu, tp), ("x", "core") + names[1:]
    )
    ctx_axes = ("x", "core")
    return jax.shard_map(
        body,
        mesh=fine,
        in_specs=(
            P(ctx_axes, "clu", None),
            P(ctx_axes + ("clu",), None, "tp"),
            P(ctx_axes, "clu", "tp"),
        ),
        out_specs=P(ctx_axes, "clu", "tp"),
        check_vma=False,
    )
```

```python
import jax
import jax.numpy as jnp
from jax import lax
from jax.experimental import pallas as pl
from jax.experimental.pallas import tpu as pltpu
from jax.sharding import PartitionSpec as P

CLUSTERS = 64
GROUPS = 2
BF16 = jnp.bfloat16
F32 = jnp.float32
VMEM_LIMIT = 48 * 1024 * 1024


def vmem_call(kernel, out_shape, in_smem, **kwargs):
    vmem = pl.BlockSpec(memory_space=pltpu.VMEM)
    smem = pl.BlockSpec(memory_space=pltpu.SMEM)
    return pl.pallas_call(
        kernel,
        out_shape=out_shape,
        in_specs=[smem if flag else vmem for flag in in_smem],
        out_specs=jax.tree.map(lambda _: vmem, out_shape),
        compiler_params=pltpu.CompilerParams(vmem_limit_bytes=VMEM_LIMIT),
        **kwargs,
    )


def scalar(value):
    return jnp.reshape(value, (1,)).astype(jnp.int32)


def iota(shape, dim):
    return lax.broadcasted_iota(jnp.int32, shape, dim)


def routing(ids, owners, capacity):
    rows, heads = ids.shape
    per_owner = CLUSTERS // owners

    def kernel(ids_ref, ids_t_ref, slot_row_ref, slot_col_ref):
        before_col = (iota((rows, rows), 1) < iota((rows, rows), 0)).astype(BF16)
        before_row = (iota((rows, rows), 0) < iota((rows, rows), 1)).astype(BF16)
        for h in range(heads):
            owner_col = ids_ref[:, h : h + 1] // per_owner
            hot = owner_col == iota((rows, owners), 1)
            count = jnp.dot(before_col, hot.astype(BF16), preferred_element_type=F32)
            rank = jnp.sum(jnp.where(hot, count, 0.0), axis=1, keepdims=True)
            slot_col_ref[:, h : h + 1] = owner_col * capacity + rank.astype(jnp.int32)
            owner_row = ids_t_ref[h : h + 1, :] // per_owner
            hot = owner_row == iota((owners, rows), 0)
            count = jnp.dot(hot.astype(BF16), before_row, preferred_element_type=F32)
            rank = jnp.sum(jnp.where(hot, count, 0.0), axis=0, keepdims=True)
            slot_row_ref[h : h + 1, :] = owner_row * capacity + rank.astype(jnp.int32)

    return vmem_call(
        kernel,
        (
            jax.ShapeDtypeStruct((heads, rows), jnp.int32),
            jax.ShapeDtypeStruct((rows, heads), jnp.int32),
        ),
        (False, False),
    )(ids, ids.T)


def owned_mask(all_ids, me, heads, capacity):
    sources, id_rows, lanes = all_ids.shape
    per_head = 2 * sources * capacity // 4 // lanes
    rows = per_head * lanes
    per_owner = CLUSTERS // sources
    slots = sources * capacity

    def kernel(me_ref, ids_ref, out_ref):
        before = (iota((rows, rows), 0) < iota((rows, rows), 1)).astype(BF16)
        place = iota((sources, capacity, rows), 1)
        kinds = iota((slots, 128), 1) + 1
        query = iota((slots, slots), 0)
        key = iota((slots, slots), 1)
        outside = jnp.where(query == key, -100000.0, 0.0)
        for h in range(heads):
            ids = jnp.concatenate(
                [ids_ref[:, h * per_head + j, :] for j in range(per_head)], axis=1
            )
            ids = ids.astype(F32).astype(jnp.int32)
            owner = ids // per_owner
            mine = owner == me_ref[0]
            rank = jnp.dot(mine.astype(BF16), before, preferred_element_type=F32)
            rank = jnp.where(mine, rank.astype(jnp.int32), -1)
            tag = ids - owner * per_owner + 1
            placed = jnp.where(rank[:, None, :] == place, tag[:, None, :], 0)
            tag = jnp.sum(placed.reshape(slots, rows), axis=1, keepdims=True)
            member = (tag == kinds).astype(BF16)
            same = lax.dot_general(
                member, member, (((1,), (1,)), ((), ())), preferred_element_type=F32
            )
            out_ref[h] = jnp.where((same > 0.5) & (key <= query), outside, -1e30)

    return vmem_call(kernel, jax.ShapeDtypeStruct((heads, slots, slots), F32), (True, False))(
        scalar(me), all_ids
    )


def cut_tokens(local_rows, x, core, steps, chips):
    rows, depth = local_rows.shape
    half = depth // chips // 2

    def kernel(x_ref, core_ref, in_ref, *refs):
        out_refs, sems = refs[:-1], refs[-1]
        copies = []
        for i, step in enumerate(steps):
            chip = lax.rem(x_ref[0] + step + chips, chips)
            for j in range(2):
                first = (2 * chip + lax.rem(core_ref[0] + j, 2)) * half
                copies.append(
                    pltpu.make_async_copy(
                        in_ref.at[:, pl.ds(pl.multiple_of(first, half), half)],
                        out_refs[i].at[:, j * half : (j + 1) * half],
                        sems.at[2 * i + j],
                    )
                )
        for copy in copies:
            copy.start()
        for copy in copies:
            copy.wait()

    smem = pl.BlockSpec(memory_space=pltpu.SMEM)
    whole = pl.BlockSpec(memory_space=pl.ANY)
    return pl.pallas_call(
        kernel,
        out_shape=(jax.ShapeDtypeStruct((rows, 2 * half), BF16),) * len(steps),
        in_specs=[smem, smem, whole],
        out_specs=(whole,) * len(steps),
        scratch_shapes=[pltpu.SemaphoreType.DMA((2 * len(steps),))],
    )(scalar(x), scalar(core), local_rows)


def assemble(parts, starts, me, size, width):
    height, wide = parts[0].shape[1:]
    classes = 4
    id_rows = 16

    def kernel(me_ref, *refs):
        part_refs = refs[: len(parts)]
        weight_ref, id_ref, sems = refs[len(parts) :]
        copies = []
        for ref, (step, first) in zip(part_refs, starts):
            kind = lax.rem(me_ref[0] + step + size, classes)
            for j in range(ref.shape[0]):
                device = kind + classes * (first + j)
                at = pl.multiple_of(device * height, height)
                copies.append((ref.at[j, :, :width], weight_ref.at[pl.ds(at, height), :]))
                copies.append((ref.at[j, :id_rows, width:], id_ref.at[device]))
        copies = [
            pltpu.make_async_copy(source, target, sems.at[i])
            for i, (source, target) in enumerate(copies)
        ]
        for copy in copies:
            copy.start()
        for copy in copies:
            copy.wait()

    whole = pl.BlockSpec(memory_space=pl.ANY)
    return pl.pallas_call(
        kernel,
        out_shape=(
            jax.ShapeDtypeStruct((size * height, width), BF16),
            jax.ShapeDtypeStruct((size, id_rows, wide - width), BF16),
        ),
        in_specs=[pl.BlockSpec(memory_space=pltpu.SMEM)] + [whole] * len(parts),
        out_specs=(whole, whole),
        scratch_shapes=[pltpu.SemaphoreType.DMA((2 * size,))],
    )(scalar(me), *parts)


def project(pieces, ring, other, groups):
    rows, depth = pieces[0].shape
    half, width = ring.shape
    part = width // groups

    def kernel(*refs):
        piece_refs = refs[: len(pieces)]
        ring_ref, other_ref = refs[len(pieces) : len(pieces) + 2]
        out_refs = refs[len(pieces) + 2 :]
        for i, piece_ref in enumerate(piece_refs):
            for g in range(groups):
                cols = slice(g * part, (g + 1) * part)
                total = jnp.dot(
                    piece_ref[:, :half], ring_ref[:, cols], preferred_element_type=F32
                ) + jnp.dot(piece_ref[:, half:], other_ref[:, cols], preferred_element_type=F32)
                out_refs[i * groups + g][...] = total.astype(BF16)

    return vmem_call(
        kernel,
        (jax.ShapeDtypeStruct((rows, part), BF16),) * (len(pieces) * groups),
        (False,) * (len(pieces) + 2),
    )(*pieces, ring, other)


def pack(partials, slot_row, owners, capacity, head_dim):
    parts = len(partials[0])
    groups = len(partials)
    rows, width = partials[0][0].shape
    in_group = width // (2 * head_dim)
    heads = in_group * groups
    slots = owners * capacity

    def kernel(*refs):
        slot_ref, out_ref = refs[-2:]

        def columns(g, first):
            cols = slice(first, first + head_dim)
            total = refs[g * parts][:, cols].astype(F32)
            for p in range(1, parts):
                total += refs[g * parts + p][:, cols].astype(F32)
            return total.astype(BF16)

        for h in range(heads):
            place = iota((slots, rows), 0) == slot_ref[h : h + 1, :]
            place = place.astype(BF16)
            for m in range(2):
                first = (m * in_group + h % in_group) * head_dim
                packed = jnp.dot(
                    place, columns(h // in_group, first), preferred_element_type=F32
                ).astype(BF16)
                out_ref[
                    :, h * capacity : (h + 1) * capacity, m * head_dim : (m + 1) * head_dim
                ] = packed.reshape(owners, capacity, head_dim)

    return vmem_call(
        kernel,
        jax.ShapeDtypeStruct((owners, heads * capacity, 2 * head_dim), BF16),
        (False,) * (parts * groups + 1),
    )(*[part for group in partials for part in group], slot_row)


def attend(blocks, mask, capacity):
    sources, rows, width = blocks.shape
    head_dim = width // 2
    heads = rows // capacity
    slots = sources * capacity
    scale = head_dim ** (-0.5)

    def kernel(block_ref, mask_ref, out_ref):
        for h in range(heads):
            here = slice(h * capacity, (h + 1) * capacity)
            keys = block_ref[:, here, :head_dim].reshape(slots, head_dim)
            values = block_ref[:, here, head_dim:].reshape(slots, head_dim)
            scores = lax.dot_general(
                keys, keys, (((1,), (1,)), ((), ())), preferred_element_type=F32
            )
            mask = mask_ref[h]
            scores = jnp.where(mask == 0.0, scores * scale, mask)
            row_max = jnp.max(scores, axis=1, keepdims=True)
            weights = jnp.exp(scores - row_max)
            total = jnp.sum(weights, axis=1, keepdims=True)
            probabilities = (weights / total).astype(BF16)
            result = jnp.dot(probabilities, values, preferred_element_type=F32).astype(BF16)
            out_ref[:, here, :] = result.reshape(sources, capacity, head_dim)

    return vmem_call(
        kernel, jax.ShapeDtypeStruct((sources, rows, head_dim), BF16), (False, False)
    )(blocks, mask)


def unpack(returned, slot_col, capacity):
    owners, height, head_dim = returned.shape
    rows, heads = slot_col.shape
    slots = owners * capacity

    def kernel(block_ref, slot_ref, out_ref):
        for h in range(heads):
            block = block_ref[:, h * capacity : (h + 1) * capacity, :].reshape(slots, head_dim)
            place = slot_ref[:, h : h + 1] == iota((rows, slots), 1)
            out_ref[:, h * head_dim : (h + 1) * head_dim] = jnp.dot(
                place.astype(BF16), block, preferred_element_type=F32
            ).astype(BF16)

    return vmem_call(
        kernel, jax.ShapeDtypeStruct((rows, heads * head_dim), BF16), (False, False)
    )(returned, slot_col)


CLU = ("zq", "zr")


def shifted(block, step, axis):
    size = lax.axis_size(axis)
    return lax.ppermute(block, axis, [(i, (i + step) % size) for i in range(size)])


def body(tokens, proj_weight, clusters):
    rows, depth = tokens.shape[1:]
    owners = lax.axis_size(CLU)
    me = lax.axis_index(CLU)
    heads = clusters.shape[2]
    shard = proj_weight.shape[0]
    width = 2 * proj_weight.shape[2]
    head_dim = proj_weight.shape[2] // heads
    capacity = 2 * rows // owners
    chips = lax.axis_size("x")

    own = proj_weight.reshape(shard, 2, GROUPS, width // GROUPS // 2).transpose(0, 2, 1, 3)
    ids = clusters[0].T.astype(BF16).reshape(-1, 128)
    ids = jnp.pad(ids, ((0, shard - ids.shape[0]), (0, 0)))
    own = jnp.concatenate([own.reshape(shard, width), ids], axis=1)
    four = lax.all_to_all(
        jnp.broadcast_to(own, (4,) + own.shape), "zq", split_axis=0, concat_axis=0, tiled=True
    )
    steps = (2, 1, -1, 0)
    pieces = cut_tokens(tokens[0], lax.axis_index("x"), lax.axis_index("core"), steps, chips)
    pieces = [p if s == 0 else shifted(p, s, "x") for p, s in zip(pieces, steps)]

    parts = [
        four,
        shifted(four, 1, CLU),
        shifted(four, -1, CLU),
        shifted(four[:2], 2, CLU),
        shifted(four[2:], -2, CLU),
    ]
    starts = [(0, 0), (-1, 0), (1, 0), (-2, 0), (2, 2)]
    ring, all_ids = assemble(parts, starts, me, owners, width)
    other = lax.ppermute(ring, "core", [(0, 1), (1, 0)])
    sent = project(pieces, ring, other, GROUPS)

    slot_row, slot_col = routing(clusters[0], owners, capacity)
    partials = [[] for _ in range(GROUPS)]
    for g in range(GROUPS):
        for i, step in enumerate(steps):
            part = sent[i * GROUPS + g]
            partials[g].append(part if step == 0 else shifted(part, -step, "x"))
    mask = owned_mask(all_ids, me, heads, capacity)
    outgoing = pack(partials, slot_row, owners, capacity, head_dim)
    incoming = lax.all_to_all(outgoing, CLU, split_axis=0, concat_axis=0, tiled=True)
    replies = attend(incoming, mask, capacity)
    returned = lax.all_to_all(replies, CLU, split_axis=0, concat_axis=0, tiled=True)
    return unpack(returned, slot_col, capacity)[None]


def solution(mesh):
    ctx, clu, tp = (mesh.shape[name] for name in mesh.axis_names)
    fine = jax.sharding.Mesh(
        mesh.devices.reshape(ctx // 2, 2, clu // 4, 4, tp), ("x", "core") + CLU + ("tp",)
    )
    ctx_axes = ("x", "core")
    return jax.shard_map(
        body,
        mesh=fine,
        in_specs=(
            P(ctx_axes, CLU, None),
            P(ctx_axes + CLU, None, "tp"),
            P(ctx_axes, CLU, "tp"),
        ),
        out_specs=P(ctx_axes, CLU, "tp"),
        check_vma=False,
    )
```

```python
import jax
import jax.numpy as jnp
from jax import lax
from jax.experimental import pallas as pl
from jax.experimental.pallas import tpu as pltpu
from jax.sharding import PartitionSpec as P

CLUSTERS = 64
BF16 = jnp.bfloat16
F32 = jnp.float32
VMEM_LIMIT = 48 * 1024 * 1024


def vmem_call(kernel, out_shape, in_smem, **kwargs):
    vmem = pl.BlockSpec(memory_space=pltpu.VMEM)
    smem = pl.BlockSpec(memory_space=pltpu.SMEM)
    return pl.pallas_call(
        kernel,
        out_shape=out_shape,
        in_specs=[smem if flag else vmem for flag in in_smem],
        out_specs=jax.tree.map(lambda _: vmem, out_shape),
        compiler_params=pltpu.CompilerParams(vmem_limit_bytes=VMEM_LIMIT),
        **kwargs,
    )


def scalar(value):
    return jnp.reshape(value, (1,)).astype(jnp.int32)


def iota(shape, dim):
    return lax.broadcasted_iota(jnp.int32, shape, dim)


def routing(ids, owners, capacity):
    rows, heads = ids.shape
    per_owner = CLUSTERS // owners

    def kernel(ids_ref, ids_t_ref, slot_row_ref, slot_col_ref):
        before_col = (iota((rows, rows), 1) < iota((rows, rows), 0)).astype(BF16)
        before_row = (iota((rows, rows), 0) < iota((rows, rows), 1)).astype(BF16)
        for h in range(heads):
            owner_col = ids_ref[:, h : h + 1] // per_owner
            hot = owner_col == iota((rows, owners), 1)
            count = jnp.dot(before_col, hot.astype(BF16), preferred_element_type=F32)
            rank = jnp.sum(jnp.where(hot, count, 0.0), axis=1, keepdims=True)
            slot_col_ref[:, h : h + 1] = owner_col * capacity + rank.astype(jnp.int32)
            owner_row = ids_t_ref[h : h + 1, :] // per_owner
            hot = owner_row == iota((owners, rows), 0)
            count = jnp.dot(hot.astype(BF16), before_row, preferred_element_type=F32)
            rank = jnp.sum(jnp.where(hot, count, 0.0), axis=0, keepdims=True)
            slot_row_ref[h : h + 1, :] = owner_row * capacity + rank.astype(jnp.int32)

    return vmem_call(
        kernel,
        (
            jax.ShapeDtypeStruct((heads, rows), jnp.int32),
            jax.ShapeDtypeStruct((rows, heads), jnp.int32),
        ),
        (False, False),
    )(ids, ids.T)


def owned_mask(all_ids, me, heads, capacity):
    sources, id_rows, lanes = all_ids.shape
    per_head = 2 * sources * capacity // 4 // lanes
    rows = per_head * lanes
    per_owner = CLUSTERS // sources
    slots = sources * capacity

    def kernel(me_ref, ids_ref, out_ref):
        before = (iota((rows, rows), 0) < iota((rows, rows), 1)).astype(BF16)
        place = iota((sources, capacity, rows), 1)
        kinds = iota((slots, 128), 1) + 1
        query = iota((slots, slots), 0)
        key = iota((slots, slots), 1)
        outside = jnp.where(query == key, -100000.0, 0.0)
        for h in range(heads):
            ids = jnp.concatenate(
                [ids_ref[:, h * per_head + j, :] for j in range(per_head)], axis=1
            )
            ids = ids.astype(F32).astype(jnp.int32)
            owner = ids // per_owner
            mine = owner == me_ref[0]
            rank = jnp.dot(mine.astype(BF16), before, preferred_element_type=F32)
            rank = jnp.where(mine, rank.astype(jnp.int32), -1)
            tag = ids - owner * per_owner + 1
            placed = jnp.where(rank[:, None, :] == place, tag[:, None, :], 0)
            tag = jnp.sum(placed.reshape(slots, rows), axis=1, keepdims=True)
            member = (tag == kinds).astype(BF16)
            same = lax.dot_general(
                member, member, (((1,), (1,)), ((), ())), preferred_element_type=F32
            )
            out_ref[h] = jnp.where((same > 0.5) & (key <= query), outside, -1e30)

    return vmem_call(kernel, jax.ShapeDtypeStruct((heads, slots, slots), F32), (True, False))(
        scalar(me), all_ids
    )


def cut_tokens(local_rows, core, parity, chips, owners):
    rows, depth = local_rows.shape
    half = depth // chips // 2
    shard = half // owners

    def kernel(core_ref, parity_ref, in_ref, own_ref, other_ref, order_ref):
        @pl.when(pl.program_id(0) == 0)
        def _():
            at = iota((half, half), 0)
            kind = at // shard % 2
            target = at // (2 * shard) * shard + at % shard
            target = target + jnp.where(kind == parity_ref[0], 0, half // 2)
            order_ref[...] = (target == iota((half, half), 1)).astype(BF16)

        def ordered(block):
            return jnp.dot(block, order_ref[...], preferred_element_type=F32).astype(BF16)

        first = ordered(in_ref[:, :half])
        second = ordered(in_ref[:, half:])
        mine_first = core_ref[0] == 0
        own_ref[0] = jnp.where(mine_first, first, second)
        other_ref[0] = jnp.where(mine_first, second, first)

    out_spec = pl.BlockSpec((1, rows, half), lambda p, core, parity: (p, 0, 0))
    return pl.pallas_call(
        kernel,
        grid_spec=pltpu.PrefetchScalarGridSpec(
            num_scalar_prefetch=2,
            grid=(chips,),
            in_specs=[pl.BlockSpec((rows, 2 * half), lambda p, core, parity: (0, p))],
            out_specs=(out_spec, out_spec),
            scratch_shapes=[pltpu.VMEM((half, half), BF16)],
        ),
        out_shape=(jax.ShapeDtypeStruct((chips, rows, half), BF16),) * 2,
    )(scalar(core), scalar(parity), local_rows)


def add_products(total, tokens, weights, places, x):
    chips, rows, half = tokens[0].shape
    width = weights[0].shape[1]
    given = [] if total is None else [total]

    def kernel(x_ref, *refs):
        out_ref = refs[-1]
        token_refs = refs[len(given) : len(given) + 2]
        weight_refs = refs[len(given) + 2 : -1]
        for i, token_ref in enumerate(token_refs):
            result = refs[0][i] if given else 0.0
            for weight_ref, (step, first) in zip(weight_refs, places):
                chip = lax.rem(x_ref[0] + step + chips, chips)
                depth = weight_ref.shape[0]
                result = result + jnp.dot(
                    token_ref[chip, :, first : first + depth],
                    weight_ref[...],
                    preferred_element_type=F32,
                )
            out_ref[i] = result

    operands = given + list(tokens) + list(weights)
    return vmem_call(
        kernel,
        jax.ShapeDtypeStruct((2, rows, width), F32),
        (True,) + (False,) * len(operands),
    )(scalar(x), *operands)


def last_products(total, tokens, weights, places, x):
    chips, rows, half = tokens[0].shape
    width = weights[0].shape[1]

    def kernel(x_ref, total_ref, own_ref, other_ref, *refs):
        weight_refs = refs[:-2]
        for i, (token_ref, out_ref) in enumerate(zip((own_ref, other_ref), refs[-2:])):
            result = total_ref[i]
            for weight_ref, (step, first) in zip(weight_refs, places):
                chip = lax.rem(x_ref[0] + step + chips, chips)
                depth = weight_ref.shape[0]
                result = result + jnp.dot(
                    token_ref[chip, :, first : first + depth],
                    weight_ref[...],
                    preferred_element_type=F32,
                )
            out_ref[...] = result.astype(out_ref.dtype)

    return vmem_call(
        kernel,
        (jax.ShapeDtypeStruct((rows, width), F32), jax.ShapeDtypeStruct((rows, width), BF16)),
        (True,) + (False,) * (3 + len(weights)),
    )(scalar(x), total, *tokens, *weights)


def pack(own, received, slot_row, owners, capacity, head_dim):
    rows, width = own.shape
    heads = slot_row.shape[0]
    slots = owners * capacity

    def kernel(own_ref, received_ref, slot_ref, out_ref):
        for h in range(heads):
            place = iota((slots, rows), 0) == slot_ref[h : h + 1, :]
            place = place.astype(BF16)
            for m in range(2):
                cols = slice((m * heads + h) * head_dim, (m * heads + h + 1) * head_dim)
                total = own_ref[:, cols] + received_ref[:, cols].astype(F32)
                packed = jnp.dot(
                    place, total.astype(BF16), preferred_element_type=F32
                ).astype(BF16)
                out_ref[
                    :, h * capacity : (h + 1) * capacity, m * head_dim : (m + 1) * head_dim
                ] = packed.reshape(owners, capacity, head_dim)

    return vmem_call(
        kernel,
        jax.ShapeDtypeStruct((owners, heads * capacity, 2 * head_dim), BF16),
        (False,) * 3,
    )(own, received, slot_row)


def attend(blocks, mask, capacity):
    sources, rows, width = blocks.shape
    head_dim = width // 2
    heads = rows // capacity
    slots = sources * capacity
    scale = head_dim ** (-0.5)

    def kernel(block_ref, mask_ref, out_ref):
        for h in range(heads):
            here = slice(h * capacity, (h + 1) * capacity)
            keys = block_ref[:, here, :head_dim].reshape(slots, head_dim)
            values = block_ref[:, here, head_dim:].reshape(slots, head_dim)
            scores = lax.dot_general(
                keys, keys, (((1,), (1,)), ((), ())), preferred_element_type=F32
            )
            mask = mask_ref[h]
            scores = jnp.where(mask == 0.0, scores * scale, mask)
            row_max = jnp.max(scores, axis=1, keepdims=True)
            weights = jnp.exp(scores - row_max)
            total = jnp.sum(weights, axis=1, keepdims=True)
            probabilities = (weights / total).astype(BF16)
            result = jnp.dot(probabilities, values, preferred_element_type=F32).astype(BF16)
            out_ref[:, here, :] = result.reshape(sources, capacity, head_dim)

    return vmem_call(
        kernel, jax.ShapeDtypeStruct((sources, rows, head_dim), BF16), (False, False)
    )(blocks, mask)


def unpack(returned, slot_col, capacity):
    owners, height, head_dim = returned.shape
    rows, heads = slot_col.shape
    slots = owners * capacity

    def kernel(block_ref, slot_ref, out_ref):
        for h in range(heads):
            block = block_ref[:, h * capacity : (h + 1) * capacity, :].reshape(slots, head_dim)
            place = slot_ref[:, h : h + 1] == iota((rows, slots), 1)
            out_ref[:, h * head_dim : (h + 1) * head_dim] = jnp.dot(
                place.astype(BF16), block, preferred_element_type=F32
            ).astype(BF16)

    return vmem_call(
        kernel, jax.ShapeDtypeStruct((rows, heads * head_dim), BF16), (False, False)
    )(returned, slot_col)


CLU = ("zh", "zl")


def shifted(block, step, axis):
    size = lax.axis_size(axis)
    return lax.ppermute(block, axis, [(i, (i + step) % size) for i in range(size)])


def round_x(block):
    half = block.shape[0] // 2
    below = shifted(block, 1, "x")
    above = shifted(block, -1, "x")
    return [below, above, shifted(below[:half], 1, "x"), shifted(above[half:], -1, "x")]


def body(tokens, proj_weight, clusters):
    rows, depth = tokens.shape[1:]
    owners = lax.axis_size(CLU)
    me = lax.axis_index(CLU)
    parity = lax.axis_index("zl")
    x = lax.axis_index("x")
    heads = clusters.shape[2]
    shard = proj_weight.shape[0]
    width = 2 * proj_weight.shape[2]
    head_dim = proj_weight.shape[2] // heads
    capacity = 2 * rows // owners
    chips = lax.axis_size("x")

    ids = clusters[0].T.astype(BF16).reshape(-1, 128)
    ids = jnp.pad(ids, ((0, shard - ids.shape[0]), (0, 0)))
    own = jnp.concatenate([proj_weight.reshape(shard, width), ids], axis=1)
    same = lax.all_gather(own, "zh", axis=0)
    low, high = shifted(same[:4], 1, CLU), shifted(same[4:], -1, CLU)
    rest = jnp.concatenate([low, high], axis=0)

    mine, send = cut_tokens(tokens[0], lax.axis_index("core"), parity, chips, owners)
    theirs = lax.ppermute(send, "core", [(0, 1), (1, 0)])

    first = same[:, :, :width].reshape(-1, width)
    second = rest[:, :, :width].reshape(-1, width)
    first_x, second_x = round_x(first), round_x(second)
    half = first.shape[0]
    both = (mine, theirs)
    total = add_products(
        None, both, [first] + first_x[:2], [(0, 0), (-1, 0), (1, 0)], x
    )
    total = add_products(
        total, both, [second] + second_x[:2], [(0, half), (-1, half), (1, half)], x
    )
    kept, given = last_products(
        total,
        both,
        first_x[2:] + second_x[2:],
        [(2, 0), (2, half // 2), (2, half), (2, half + half // 2)],
        x,
    )
    received = lax.ppermute(given, "core", [(0, 1), (1, 0)])

    slot_row, slot_col = routing(clusters[0], owners, capacity)
    outgoing = pack(kept, received, slot_row, owners, capacity, head_dim)
    incoming = lax.all_to_all(outgoing, CLU, split_axis=0, concat_axis=0, tiled=True)

    same_ids, rest_ids = same[:, :16, width:], rest[:, :16, width:]
    even = jnp.where(parity == 0, same_ids, rest_ids)
    odd = jnp.where(parity == 0, rest_ids, same_ids)
    all_ids = jnp.stack([even, odd], axis=1).reshape((owners,) + even.shape[1:])
    mask = owned_mask(all_ids, me, heads, capacity)
    replies = attend(incoming, mask, capacity)
    returned = lax.all_to_all(replies, CLU, split_axis=0, concat_axis=0, tiled=True)
    return unpack(returned, slot_col, capacity)[None]


def solution(mesh):
    ctx, clu, tp = (mesh.shape[name] for name in mesh.axis_names)
    fine = jax.sharding.Mesh(
        mesh.devices.reshape(ctx // 2, 2, clu // 2, 2, tp), ("x", "core") + CLU + ("tp",)
    )
    ctx_axes = ("x", "core")
    return jax.shard_map(
        body,
        mesh=fine,
        in_specs=(
            P(ctx_axes, CLU, None),
            P(ctx_axes + CLU, None, "tp"),
            P(ctx_axes, CLU, "tp"),
        ),
        out_specs=P(ctx_axes, CLU, "tp"),
        check_vma=False,
    )
```

```python
import jax
import jax.numpy as jnp
from jax import lax
from jax.experimental import pallas as pl
from jax.experimental.pallas import tpu as pltpu
from jax.sharding import PartitionSpec as P

CLUSTERS = 64
BF16 = jnp.bfloat16
F32 = jnp.float32
VMEM_LIMIT = 48 * 1024 * 1024


def vmem_call(kernel, out_shape, in_smem, **kwargs):
    vmem = pl.BlockSpec(memory_space=pltpu.VMEM)
    smem = pl.BlockSpec(memory_space=pltpu.SMEM)
    return pl.pallas_call(
        kernel,
        out_shape=out_shape,
        in_specs=[smem if flag else vmem for flag in in_smem],
        out_specs=jax.tree.map(lambda _: vmem, out_shape),
        compiler_params=pltpu.CompilerParams(vmem_limit_bytes=VMEM_LIMIT),
        **kwargs,
    )


def scalar(value):
    return jnp.reshape(value, (1,)).astype(jnp.int32)


def iota(shape, dim):
    return lax.broadcasted_iota(jnp.int32, shape, dim)


def routing(ids, owners, capacity):
    rows, heads = ids.shape
    per_owner = CLUSTERS // owners

    def kernel(ids_ref, ids_t_ref, slot_row_ref, slot_col_ref):
        before_col = (iota((rows, rows), 1) < iota((rows, rows), 0)).astype(BF16)
        before_row = (iota((rows, rows), 0) < iota((rows, rows), 1)).astype(BF16)
        for h in range(heads):
            owner_col = ids_ref[:, h : h + 1] // per_owner
            hot = owner_col == iota((rows, owners), 1)
            count = jnp.dot(before_col, hot.astype(BF16), preferred_element_type=F32)
            rank = jnp.sum(jnp.where(hot, count, 0.0), axis=1, keepdims=True)
            slot_col_ref[:, h : h + 1] = owner_col * capacity + rank.astype(jnp.int32)
            owner_row = ids_t_ref[h : h + 1, :] // per_owner
            hot = owner_row == iota((owners, rows), 0)
            count = jnp.dot(hot.astype(BF16), before_row, preferred_element_type=F32)
            rank = jnp.sum(jnp.where(hot, count, 0.0), axis=0, keepdims=True)
            slot_row_ref[h : h + 1, :] = owner_row * capacity + rank.astype(jnp.int32)

    return vmem_call(
        kernel,
        (
            jax.ShapeDtypeStruct((heads, rows), jnp.int32),
            jax.ShapeDtypeStruct((rows, heads), jnp.int32),
        ),
        (False, False),
    )(ids, ids.T)


def owned_mask(all_ids, me, chosen, capacity):
    sources, id_rows, lanes = all_ids.shape
    per_head = 2 * sources * capacity // 4 // lanes
    rows = per_head * lanes
    per_owner = CLUSTERS // sources
    slots = sources * capacity

    def kernel(me_ref, ids_ref, out_ref):
        before = (iota((rows, rows), 0) < iota((rows, rows), 1)).astype(BF16)
        place = iota((sources, capacity, rows), 1)
        kinds = iota((slots, 128), 1) + 1
        query = iota((slots, slots), 0)
        key = iota((slots, slots), 1)
        outside = jnp.where(query == key, -100000.0, 0.0)
        for i, h in enumerate(chosen):
            ids = jnp.concatenate(
                [ids_ref[:, h * per_head + j, :] for j in range(per_head)], axis=1
            )
            ids = ids.astype(F32).astype(jnp.int32)
            owner = ids // per_owner
            mine = owner == me_ref[0]
            rank = jnp.dot(mine.astype(BF16), before, preferred_element_type=F32)
            rank = jnp.where(mine, rank.astype(jnp.int32), -1)
            tag = ids - owner * per_owner + 1
            placed = jnp.where(rank[:, None, :] == place, tag[:, None, :], 0)
            tag = jnp.sum(placed.reshape(slots, rows), axis=1, keepdims=True)
            member = (tag == kinds).astype(BF16)
            same = lax.dot_general(
                member, member, (((1,), (1,)), ((), ())), preferred_element_type=F32
            )
            out_ref[i] = jnp.where((same > 0.5) & (key <= query), outside, -1e30)

    return vmem_call(kernel, jax.ShapeDtypeStruct((len(chosen), slots, slots), F32), (True, False))(
        scalar(me), all_ids
    )


def cut_tokens(local_rows, core, chips):
    rows, depth = local_rows.shape
    half = depth // chips // 2

    def kernel(core_ref, in_ref, out_ref, sems):
        copies = []
        for p in range(chips):
            for j in range(2):
                first = (2 * p + lax.rem(core_ref[0] + j, 2)) * half
                copies.append(
                    pltpu.make_async_copy(
                        in_ref.at[:, pl.ds(pl.multiple_of(first, half), half)],
                        out_ref.at[p, :, j * half : (j + 1) * half],
                        sems.at[2 * p + j],
                    )
                )
        for copy in copies:
            copy.start()
        for copy in copies:
            copy.wait()

    return pl.pallas_call(
        kernel,
        out_shape=jax.ShapeDtypeStruct((chips, rows, 2 * half), BF16),
        in_specs=[
            pl.BlockSpec(memory_space=pltpu.SMEM),
            pl.BlockSpec(memory_space=pl.ANY),
        ],
        out_specs=pl.BlockSpec(memory_space=pltpu.VMEM),
        scratch_shapes=[pltpu.SemaphoreType.DMA((2 * chips,))],
        compiler_params=pltpu.CompilerParams(vmem_limit_bytes=VMEM_LIMIT),
    )(scalar(core), local_rows)


def project(pieces, ring, other, x, steps, first, width):
    chips, rows, depth = pieces.shape
    half = ring.shape[0]
    cols = slice(first, first + width)

    def kernel(x_ref, pieces_ref, ring_ref, other_ref, *out_refs):
        for step, out_ref in zip(steps, out_refs):
            p = lax.rem(x_ref[0] + step + chips, chips)
            total = jnp.dot(
                pieces_ref[p, :, :half], ring_ref[:, cols], preferred_element_type=F32
            ) + jnp.dot(pieces_ref[p, :, half:], other_ref[:, cols], preferred_element_type=F32)
            out_ref[...] = total.astype(BF16)

    return vmem_call(
        kernel,
        (jax.ShapeDtypeStruct((rows, width), BF16),) * len(steps),
        (True, False, False, False),
    )(scalar(x), pieces, ring, other)


def add(partials):
    def kernel(*refs):
        total = refs[0][...].astype(F32)
        for ref in refs[1:-1]:
            total += ref[...].astype(F32)
        refs[-1][...] = total.astype(BF16)

    return vmem_call(
        kernel, jax.ShapeDtypeStruct(partials[0].shape, BF16), (False,) * len(partials)
    )(*partials)


def pack(partials, slot_row, chosen, owners, capacity, head_dim):
    rows, width = partials[0].shape
    heads = len(chosen)
    slots = owners * capacity

    def kernel(*refs):
        slot_ref, out_ref = refs[-2:]
        for i, h in enumerate(chosen):
            place = iota((slots, rows), 0) == slot_ref[h : h + 1, :]
            place = place.astype(BF16)
            for m in range(2):
                cols = slice((m * heads + i) * head_dim, (m * heads + i + 1) * head_dim)
                total = refs[0][:, cols].astype(F32)
                for ref in refs[1:-2]:
                    total += ref[:, cols].astype(F32)
                packed = jnp.dot(
                    place, total.astype(BF16), preferred_element_type=F32
                ).astype(BF16)
                out_ref[
                    :, i * capacity : (i + 1) * capacity, m * head_dim : (m + 1) * head_dim
                ] = packed.reshape(owners, capacity, head_dim)

    return vmem_call(
        kernel,
        jax.ShapeDtypeStruct((owners, heads * capacity, 2 * head_dim), BF16),
        (False,) * (len(partials) + 1),
    )(*partials, slot_row)


def attend(blocks, mask, capacity):
    sources, rows, width = blocks.shape
    head_dim = width // 2
    heads = rows // capacity
    slots = sources * capacity
    scale = head_dim ** (-0.5)

    def kernel(block_ref, mask_ref, out_ref):
        for h in range(heads):
            here = slice(h * capacity, (h + 1) * capacity)
            keys = block_ref[:, here, :head_dim].reshape(slots, head_dim)
            values = block_ref[:, here, head_dim:].reshape(slots, head_dim)
            scores = lax.dot_general(
                keys, keys, (((1,), (1,)), ((), ())), preferred_element_type=F32
            )
            mask = mask_ref[h]
            scores = jnp.where(mask == 0.0, scores * scale, mask)
            row_max = jnp.max(scores, axis=1, keepdims=True)
            weights = jnp.exp(scores - row_max)
            total = jnp.sum(weights, axis=1, keepdims=True)
            probabilities = (weights / total).astype(BF16)
            result = jnp.dot(probabilities, values, preferred_element_type=F32).astype(BF16)
            out_ref[:, here, :] = result.reshape(sources, capacity, head_dim)

    return vmem_call(
        kernel, jax.ShapeDtypeStruct((sources, rows, head_dim), BF16), (False, False)
    )(blocks, mask)


def attend_all(gathered, own, all_ids, ids, me, chosen):
    devices, rows, width = gathered.shape
    heads = len(chosen)
    head_dim = width // 2 // heads
    lanes = all_ids.shape[2]
    per_head = rows // lanes
    scale = head_dim ** (-0.5)

    def kernel(me_ref, gathered_ref, own_ref, all_ids_ref, ids_ref, out_ref, score_ref):
        ahead = iota((rows, rows), 1) - iota((rows, rows), 0)
        for i, h in enumerate(chosen):
            cols = slice(i * head_dim, (i + 1) * head_dim)
            values = slice((heads + i) * head_dim, (heads + i + 1) * head_dim)
            queries = own_ref[:, cols]
            query_ids = ids_ref[:, h : h + 1].astype(F32)
            row_max = jnp.full((rows, 1), -jnp.inf, F32)
            for z in range(devices):
                key_ids = jnp.concatenate(
                    [all_ids_ref[z, h * per_head + j : h * per_head + j + 1, :] for j in range(per_head)],
                    axis=1,
                ).astype(F32)
                scores = lax.dot_general(
                    queries,
                    gathered_ref[z, :, cols],
                    (((1,), (1,)), ((), ())),
                    preferred_element_type=F32,
                )
                offset = (me_ref[0] - z) * rows
                scores = jnp.where(ahead == offset, -100000.0, scores * scale)
                scores = jnp.where((query_ids == key_ids) & (ahead <= offset), scores, -1e30)
                score_ref[:, z * rows : (z + 1) * rows] = scores
                row_max = jnp.maximum(row_max, jnp.max(scores, axis=1, keepdims=True))
            total = jnp.zeros((rows, 1), F32)
            for z in range(devices):
                part = jnp.exp(score_ref[:, z * rows : (z + 1) * rows] - row_max)
                score_ref[:, z * rows : (z + 1) * rows] = part
                total += jnp.sum(part, axis=1, keepdims=True)
            inverse = 1.0 / total
            result = jnp.zeros((rows, head_dim), F32)
            for z in range(devices):
                part = (score_ref[:, z * rows : (z + 1) * rows] * inverse).astype(BF16)
                result += jnp.dot(
                    part, gathered_ref[z, :, values], preferred_element_type=F32
                )
            out_ref[:, cols] = result.astype(BF16)

    return vmem_call(
        kernel,
        jax.ShapeDtypeStruct((rows, heads * head_dim), BF16),
        (True,) + (False,) * 4,
        scratch_shapes=[pltpu.VMEM((rows, devices * rows), F32)],
    )(scalar(me), gathered, own, all_ids, ids)


def unpack(dense, returned, slot_col, chosen, capacity):
    owners, height, head_dim = returned.shape
    rows, width = dense.shape
    slots = owners * capacity

    def kernel(dense_ref, block_ref, slot_ref, out_ref):
        out_ref[:, :width] = dense_ref[...]
        for i, h in enumerate(chosen):
            block = block_ref[:, i * capacity : (i + 1) * capacity, :].reshape(slots, head_dim)
            place = slot_ref[:, h : h + 1] == iota((rows, slots), 1)
            out_ref[:, h * head_dim : (h + 1) * head_dim] = jnp.dot(
                place.astype(BF16), block, preferred_element_type=F32
            ).astype(BF16)

    return vmem_call(
        kernel,
        jax.ShapeDtypeStruct((rows, width + len(chosen) * head_dim), BF16),
        (False,) * 3,
    )(dense, returned, slot_col)


def shifted(block, step, axis):
    size = lax.axis_size(axis)
    return lax.ppermute(block, axis, [(i, (i + step) % size) for i in range(size)])


def gather_z(own):
    from_minus4 = shifted(own, 4, "clu")
    from_plus4 = shifted(own, -4, "clu")
    from_8 = shifted(own, 8, "clu")
    four = jnp.stack([own, from_plus4, from_8, from_minus4])
    minus2 = shifted(jnp.stack([own, from_minus4]), 2, "clu")
    plus2 = shifted(jnp.stack([own, from_plus4]), -2, "clu")
    from_minus1 = shifted(four, 1, "clu")
    from_plus1 = shifted(four, -1, "clu")
    order = jnp.stack(
        [
            four,
            from_plus1,
            jnp.stack([plus2[0], plus2[1], minus2[1], minus2[0]]),
            jnp.concatenate([from_minus1[1:], from_minus1[:1]]),
        ],
        axis=1,
    )
    return order.reshape((lax.axis_size("clu"),) + own.shape)


def body(tokens, proj_weight, clusters):
    rows, depth = tokens.shape[1:]
    owners = lax.axis_size("clu")
    me = lax.axis_index("clu")
    x = lax.axis_index("x")
    heads = clusters.shape[2]
    shard = proj_weight.shape[0]
    width = 2 * proj_weight.shape[2]
    head_dim = proj_weight.shape[2] // heads
    capacity = 2 * rows // owners
    chips = lax.axis_size("x")
    dense = tuple(range(heads // 2))
    routed = tuple(range(heads // 2, heads))

    pieces = cut_tokens(tokens[0], lax.axis_index("core"), chips)
    pieces = lax.all_to_all(pieces, "x", split_axis=0, concat_axis=0, tiled=True)

    own = proj_weight.reshape(shard, 2, 2, width // 4).transpose(0, 2, 1, 3)
    ids = clusters[0].T.astype(BF16).reshape(-1, 128)
    ids = jnp.pad(ids, ((0, shard - ids.shape[0]), (0, 0)))
    own = jnp.concatenate([own.reshape(shard, width), ids], axis=1)
    blocks = gather_z(own)
    ring = jnp.roll(blocks[:, :, :width], me, axis=0).reshape(owners * shard, width)
    all_ids = jnp.roll(blocks[:, :16, width:], me, axis=0)
    other = lax.ppermute(ring, "core", [(0, 1), (1, 0)])

    slot_row, slot_col = routing(clusters[0], owners, capacity)
    steps = (2, 1, -1, 0)
    partials = []
    for g in range(2):
        sent = project(pieces, ring, other, x, steps, g * width // 2, width // 2)
        partials.append(
            [part if s == 0 else shifted(part, s, "x") for part, s in zip(sent, steps)]
        )

    here = add(partials[0])
    gathered = lax.all_gather(here, "clu", axis=0)
    outgoing = pack(partials[1], slot_row, routed, owners, capacity, head_dim)
    incoming = lax.all_to_all(outgoing, "clu", split_axis=0, concat_axis=0, tiled=True)
    mask = owned_mask(all_ids, me, routed, capacity)
    replies = attend(incoming, mask, capacity)
    returned = lax.all_to_all(replies, "clu", split_axis=0, concat_axis=0, tiled=True)
    attended = attend_all(gathered, here, all_ids, clusters[0], me, dense)
    return unpack(attended, returned, slot_col, routed, capacity)[None]


def solution(mesh):
    ctx, clu, tp = (mesh.shape[name] for name in mesh.axis_names)
    fine = jax.sharding.Mesh(
        mesh.devices.reshape(ctx // 2, 2, clu, tp), ("x", "core", "clu", "tp")
    )
    ctx_axes = ("x", "core")
    return jax.shard_map(
        body,
        mesh=fine,
        in_specs=(
            P(ctx_axes, "clu", None),
            P(ctx_axes + ("clu",), None, "tp"),
            P(ctx_axes, "clu", "tp"),
        ),
        out_specs=P(ctx_axes, "clu", "tp"),
        check_vma=False,
    )
```

```python
import jax
import jax.numpy as jnp
from jax import lax
from jax.experimental import pallas as pl
from jax.experimental.pallas import tpu as pltpu
from jax.sharding import PartitionSpec as P

CLUSTERS = 64
BF16 = jnp.bfloat16
F32 = jnp.float32
VMEM_LIMIT = 48 * 1024 * 1024


def vmem_call(kernel, out_shape, in_smem, **kwargs):
    vmem = pl.BlockSpec(memory_space=pltpu.VMEM)
    smem = pl.BlockSpec(memory_space=pltpu.SMEM)
    return pl.pallas_call(
        kernel,
        out_shape=out_shape,
        in_specs=[smem if flag else vmem for flag in in_smem],
        out_specs=jax.tree.map(lambda _: vmem, out_shape),
        compiler_params=pltpu.CompilerParams(vmem_limit_bytes=VMEM_LIMIT),
        **kwargs,
    )


def scalar(value):
    return jnp.reshape(value, (1,)).astype(jnp.int32)


def iota(shape, dim):
    return lax.broadcasted_iota(jnp.int32, shape, dim)


def routing(ids, owners, capacity):
    rows, heads = ids.shape
    per_owner = CLUSTERS // owners

    def kernel(ids_ref, ids_t_ref, slot_row_ref, slot_col_ref):
        before_col = (iota((rows, rows), 1) < iota((rows, rows), 0)).astype(BF16)
        before_row = (iota((rows, rows), 0) < iota((rows, rows), 1)).astype(BF16)
        for h in range(heads):
            owner_col = ids_ref[:, h : h + 1] // per_owner
            hot = owner_col == iota((rows, owners), 1)
            count = jnp.dot(before_col, hot.astype(BF16), preferred_element_type=F32)
            rank = jnp.sum(jnp.where(hot, count, 0.0), axis=1, keepdims=True)
            slot_col_ref[:, h : h + 1] = owner_col * capacity + rank.astype(jnp.int32)
            owner_row = ids_t_ref[h : h + 1, :] // per_owner
            hot = owner_row == iota((owners, rows), 0)
            count = jnp.dot(hot.astype(BF16), before_row, preferred_element_type=F32)
            rank = jnp.sum(jnp.where(hot, count, 0.0), axis=0, keepdims=True)
            slot_row_ref[h : h + 1, :] = owner_row * capacity + rank.astype(jnp.int32)

    return vmem_call(
        kernel,
        (
            jax.ShapeDtypeStruct((heads, rows), jnp.int32),
            jax.ShapeDtypeStruct((rows, heads), jnp.int32),
        ),
        (False, False),
    )(ids, ids.T)


def owned_members(all_ids, me, heads, capacity):
    sources, id_rows, lanes = all_ids.shape
    rows = sources * capacity // 2
    per_head = rows // lanes
    per_owner = CLUSTERS // sources
    slots = sources * capacity

    def kernel(me_ref, ids_ref, out_ref):
        before = (iota((rows, rows), 0) < iota((rows, rows), 1)).astype(BF16)
        place = iota((sources, capacity, rows), 1)
        kinds = iota((16, slots), 0) + 1
        column = iota((slots, lanes), 1)
        tags = jnp.zeros((slots, lanes), jnp.int32)
        for h in range(heads):
            ids = jnp.concatenate(
                [ids_ref[:, h * per_head + j, :] for j in range(per_head)], axis=1
            )
            ids = ids.astype(F32).astype(jnp.int32)
            owner = ids // per_owner
            mine = owner == me_ref[0]
            rank = jnp.dot(mine.astype(BF16), before, preferred_element_type=F32)
            rank = jnp.where(mine, rank.astype(jnp.int32), -1)
            tag = ids - owner * per_owner + 1
            placed = jnp.where(rank[:, None, :] == place, tag[:, None, :], 0)
            tag = jnp.sum(placed.reshape(slots, rows), axis=1, keepdims=True)
            tags = jnp.where(column == h, tag, tags)
        same_slot = (iota((slots, slots), 0) == iota((slots, slots), 1)).astype(BF16)
        tags = lax.dot_general(
            tags.astype(BF16), same_slot, (((0,), (0,)), ((), ())), preferred_element_type=F32
        ).astype(jnp.int32)
        for h in range(heads):
            out_ref[h] = (tags[h : h + 1, :] == kinds).astype(BF16)

    return vmem_call(kernel, jax.ShapeDtypeStruct((heads, 16, slots), BF16), (True, False))(
        scalar(me), all_ids
    )


def cut_tokens(local_rows, core, chips):
    rows, depth = local_rows.shape
    half = depth // chips // 2

    def kernel(core_ref, in_ref, own_ref, other_ref, sems):
        copies = []
        for p in range(chips):
            for j, out_ref in enumerate((own_ref, other_ref)):
                first = (2 * p + lax.rem(core_ref[0] + j, 2)) * half
                copies.append(
                    pltpu.make_async_copy(
                        in_ref.at[:, pl.ds(pl.multiple_of(first, half), half)],
                        out_ref.at[p],
                        sems.at[2 * p + j],
                    )
                )
        for copy in copies:
            copy.start()
        for copy in copies:
            copy.wait()

    vmem = pl.BlockSpec(memory_space=pltpu.VMEM)
    return pl.pallas_call(
        kernel,
        out_shape=(jax.ShapeDtypeStruct((chips, rows, half), BF16),) * 2,
        in_specs=[
            pl.BlockSpec(memory_space=pltpu.SMEM),
            pl.BlockSpec(memory_space=pl.ANY),
        ],
        out_specs=(vmem, vmem),
        scratch_shapes=[pltpu.SemaphoreType.DMA((2 * chips,))],
        compiler_params=pltpu.CompilerParams(vmem_limit_bytes=VMEM_LIMIT),
    )(scalar(core), local_rows)


def products(total, tokens, halves, steps, x, me, places, out_types):
    chips, rows, half = tokens[0].shape
    width = halves[0].shape[1]
    given = () if total is None else total
    shard = halves[0].shape[0] // len(places[0])
    classes = 4

    def kernel(x_ref, me_ref, *refs):
        total_refs = refs[: len(given)]
        token_refs = refs[len(given) : len(given) + 2]
        half_refs = refs[len(given) + 2 : -3]
        out_refs, weight_ref = refs[-3:-1], refs[-1]
        results = [ref[...] for ref in total_refs] if given else [0.0, 0.0]
        for n, step in enumerate(steps):
            for ref, blocks in zip(half_refs[2 * n : 2 * n + 2], places):
                for i, (kind, number) in enumerate(blocks):
                    device = lax.rem(me_ref[0] + kind, classes) + classes * number
                    at = pl.multiple_of(device * shard, shard)
                    weight_ref[pl.ds(at, shard), :] = ref[i * shard : (i + 1) * shard, :]
            chip = lax.rem(x_ref[0] + step + chips, chips)
            for i, token_ref in enumerate(token_refs):
                results[i] += jnp.dot(
                    token_ref[chip], weight_ref[...], preferred_element_type=F32
                )
        for result, out_ref in zip(results, out_refs):
            out_ref[...] = result.astype(out_ref.dtype)

    operands = tuple(given) + tuple(tokens) + tuple(halves)
    return vmem_call(
        kernel,
        tuple(jax.ShapeDtypeStruct((rows, width), t) for t in out_types),
        (True, True) + (False,) * len(operands),
        scratch_shapes=[pltpu.VMEM((half, width), BF16)],
    )(scalar(x), scalar(me), *operands)


def pack(own, received, slot_row, owners, capacity, head_dim):
    rows, width = own.shape
    heads = slot_row.shape[0]
    slots = owners * capacity

    def kernel(own_ref, received_ref, slot_ref, out_ref):
        for h in range(heads):
            place = iota((slots, rows), 0) == slot_ref[h : h + 1, :]
            place = place.astype(BF16)
            for m in range(2):
                cols = slice((m * heads + h) * head_dim, (m * heads + h + 1) * head_dim)
                total = own_ref[:, cols] + received_ref[:, cols].astype(F32)
                packed = jnp.dot(
                    place, total.astype(BF16), preferred_element_type=F32
                ).astype(BF16)
                out_ref[
                    :, h * capacity : (h + 1) * capacity, m * head_dim : (m + 1) * head_dim
                ] = packed.reshape(owners, capacity, head_dim)

    return vmem_call(
        kernel,
        jax.ShapeDtypeStruct((owners, heads * capacity, 2 * head_dim), BF16),
        (False,) * 3,
    )(own, received, slot_row)


def attend(blocks, members, capacity):
    sources, rows, width = blocks.shape
    head_dim = width // 2
    heads = rows // capacity
    slots = sources * capacity
    scale = head_dim ** (-0.5)

    def kernel(block_ref, member_ref, out_ref):
        query = iota((slots, slots), 0)
        key = iota((slots, slots), 1)
        for h in range(heads):
            here = slice(h * capacity, (h + 1) * capacity)
            keys = block_ref[:, here, :head_dim].reshape(slots, head_dim)
            values = block_ref[:, here, head_dim:].reshape(slots, head_dim)
            member = member_ref[h]
            same = lax.dot_general(
                member, member, (((0,), (0,)), ((), ())), preferred_element_type=F32
            )
            scores = lax.dot_general(
                keys, keys, (((1,), (1,)), ((), ())), preferred_element_type=F32
            )
            scores = jnp.where(query == key, -100000.0, scores * scale)
            scores = jnp.where((same > 0.5) & (key <= query), scores, -1e30)
            row_max = jnp.max(scores, axis=1, keepdims=True)
            weights = jnp.exp(scores - row_max)
            total = jnp.sum(weights, axis=1, keepdims=True)
            probabilities = (weights / total).astype(BF16)
            result = jnp.dot(probabilities, values, preferred_element_type=F32).astype(BF16)
            out_ref[:, here, :] = result.reshape(sources, capacity, head_dim)

    return vmem_call(
        kernel, jax.ShapeDtypeStruct((sources, rows, head_dim), BF16), (False, False)
    )(blocks, members)


def unpack(returned, slot_col, capacity):
    owners, height, head_dim = returned.shape
    rows, heads = slot_col.shape
    slots = owners * capacity

    def kernel(block_ref, slot_ref, out_ref):
        for h in range(heads):
            block = block_ref[:, h * capacity : (h + 1) * capacity, :].reshape(slots, head_dim)
            place = slot_ref[:, h : h + 1] == iota((rows, slots), 1)
            out_ref[:, h * head_dim : (h + 1) * head_dim] = jnp.dot(
                place.astype(BF16), block, preferred_element_type=F32
            ).astype(BF16)

    return vmem_call(
        kernel, jax.ShapeDtypeStruct((rows, heads * head_dim), BF16), (False, False)
    )(returned, slot_col)


CLU = ("zq", "zr")


def shifted(block, step, axis):
    size = lax.axis_size(axis)
    return lax.ppermute(block, axis, [(i, (i + step) % size) for i in range(size)])


def body(tokens, proj_weight, clusters):
    rows, depth = tokens.shape[1:]
    owners = lax.axis_size(CLU)
    me = lax.axis_index(CLU)
    x = lax.axis_index("x")
    heads = clusters.shape[2]
    shard = proj_weight.shape[0]
    width = 2 * proj_weight.shape[2]
    head_dim = proj_weight.shape[2] // heads
    capacity = 2 * rows // owners
    chips = lax.axis_size("x")

    ids = clusters[0].T.astype(BF16).reshape(-1, 128)
    ids = jnp.pad(ids, ((0, shard - ids.shape[0]), (0, 0)))
    own = jnp.concatenate([proj_weight.reshape(shard, width), ids], axis=1)
    four = lax.all_gather(own, "zq", axis=0)
    below = shifted(four, 1, CLU)
    above = shifted(four, -1, CLU)
    beyond = [shifted(four[:2], 2, CLU), shifted(four[2:], -2, CLU)]

    def weights_of(parts):
        parts = [part[:, :, :width].reshape(-1, width) for part in parts]
        return jnp.concatenate(parts, axis=0)

    first = weights_of([four, below])
    second = weights_of([above] + beyond)
    places = (
        [(0, j) for j in range(4)] + [(3, j) for j in range(4)],
        [(1, j) for j in range(4)] + [(2, j) for j in range(4)],
    )

    mine, send = cut_tokens(tokens[0], lax.axis_index("core"), chips)
    both = (mine, lax.ppermute(send, "core", [(0, 1), (1, 0)]))

    first_below, first_above = shifted(first, 1, "x"), shifted(first, -1, "x")
    second_below, second_above = shifted(second, 1, "x"), shifted(second, -1, "x")
    first_far, second_far = shifted(first_below, 1, "x"), shifted(second_above, -1, "x")
    total = products(
        None,
        both,
        [first, second, first_below, second_below, first_above, second_above],
        (0, -1, 1),
        x,
        me,
        places,
        (F32, F32),
    )
    kept, given = products(
        total, both, [first_far, second_far], (2,), x, me, places, (F32, BF16)
    )
    received = lax.ppermute(given, "core", [(0, 1), (1, 0)])

    slot_row, slot_col = routing(clusters[0], owners, capacity)
    outgoing = pack(kept, received, slot_row, owners, capacity, head_dim)
    incoming = lax.all_to_all(outgoing, CLU, split_axis=0, concat_axis=0, tiled=True)

    by_class = jnp.stack(
        [part[:, :16, width:] for part in (four, above, jnp.concatenate(beyond), below)]
    )
    by_class = jnp.roll(by_class, lax.axis_index("zr"), axis=0)
    all_ids = by_class.transpose(1, 0, 2, 3).reshape((owners,) + by_class.shape[2:])
    members = owned_members(all_ids, me, heads, capacity)
    replies = attend(incoming, members, capacity)
    returned = lax.all_to_all(replies, CLU, split_axis=0, concat_axis=0, tiled=True)
    return unpack(returned, slot_col, capacity)[None]


def solution(mesh):
    ctx, clu, tp = (mesh.shape[name] for name in mesh.axis_names)
    fine = jax.sharding.Mesh(
        mesh.devices.reshape(ctx // 2, 2, clu // 4, 4, tp), ("x", "core") + CLU + ("tp",)
    )
    ctx_axes = ("x", "core")
    return jax.shard_map(
        body,
        mesh=fine,
        in_specs=(
            P(ctx_axes, CLU, None),
            P(ctx_axes + CLU, None, "tp"),
            P(ctx_axes, CLU, "tp"),
        ),
        out_specs=P(ctx_axes, CLU, "tp"),
        check_vma=False,
    )
```

```python
import jax
import jax.numpy as jnp
from jax import lax
from jax.experimental import pallas as pl
from jax.experimental.pallas import tpu as pltpu
from jax.sharding import PartitionSpec as P

CLUSTERS = 64
GROUPS = 2
BF16 = jnp.bfloat16
F32 = jnp.float32
VMEM_LIMIT = 48 * 1024 * 1024


def vmem_call(kernel, out_shape, in_smem, **kwargs):
    vmem = pl.BlockSpec(memory_space=pltpu.VMEM)
    smem = pl.BlockSpec(memory_space=pltpu.SMEM)
    return pl.pallas_call(
        kernel,
        out_shape=out_shape,
        in_specs=[smem if flag else vmem for flag in in_smem],
        out_specs=jax.tree.map(lambda _: vmem, out_shape),
        compiler_params=pltpu.CompilerParams(vmem_limit_bytes=VMEM_LIMIT),
        **kwargs,
    )


def scalar(value):
    return jnp.reshape(value, (1,)).astype(jnp.int32)


def iota(shape, dim):
    return lax.broadcasted_iota(jnp.int32, shape, dim)


def routing(ids, owners, capacity):
    rows, heads = ids.shape
    per_owner = CLUSTERS // owners

    def kernel(ids_ref, ids_t_ref, slot_row_ref, slot_col_ref):
        before_col = (iota((rows, rows), 1) < iota((rows, rows), 0)).astype(BF16)
        before_row = (iota((rows, rows), 0) < iota((rows, rows), 1)).astype(BF16)
        for h in range(heads):
            owner_col = ids_ref[:, h : h + 1] // per_owner
            hot = owner_col == iota((rows, owners), 1)
            count = jnp.dot(before_col, hot.astype(BF16), preferred_element_type=F32)
            rank = jnp.sum(jnp.where(hot, count, 0.0), axis=1, keepdims=True)
            slot_col_ref[:, h : h + 1] = owner_col * capacity + rank.astype(jnp.int32)
            owner_row = ids_t_ref[h : h + 1, :] // per_owner
            hot = owner_row == iota((owners, rows), 0)
            count = jnp.dot(hot.astype(BF16), before_row, preferred_element_type=F32)
            rank = jnp.sum(jnp.where(hot, count, 0.0), axis=0, keepdims=True)
            slot_row_ref[h : h + 1, :] = owner_row * capacity + rank.astype(jnp.int32)

    return vmem_call(
        kernel,
        (
            jax.ShapeDtypeStruct((heads, rows), jnp.int32),
            jax.ShapeDtypeStruct((rows, heads), jnp.int32),
        ),
        (False, False),
    )(ids, ids.T)


def owned_members(all_ids, me, heads, capacity):
    sources, id_rows, lanes = all_ids.shape
    rows = sources * capacity // 2
    per_head = rows // lanes
    per_owner = CLUSTERS // sources
    slots = sources * capacity

    def kernel(me_ref, ids_ref, out_ref):
        before = (iota((rows, rows), 0) < iota((rows, rows), 1)).astype(BF16)
        place = iota((sources, capacity, rows), 1)
        kinds = iota((16, slots), 0) + 1
        column = iota((slots, lanes), 1)
        tags = jnp.zeros((slots, lanes), jnp.int32)
        for h in range(heads):
            ids = jnp.concatenate(
                [ids_ref[:, h * per_head + j, :] for j in range(per_head)], axis=1
            )
            ids = ids.astype(F32).astype(jnp.int32)
            owner = ids // per_owner
            mine = owner == me_ref[0]
            rank = jnp.dot(mine.astype(BF16), before, preferred_element_type=F32)
            rank = jnp.where(mine, rank.astype(jnp.int32), -1)
            tag = ids - owner * per_owner + 1
            placed = jnp.where(rank[:, None, :] == place, tag[:, None, :], 0)
            tag = jnp.sum(placed.reshape(slots, rows), axis=1, keepdims=True)
            tags = jnp.where(column == h, tag, tags)
        same_slot = (iota((slots, slots), 0) == iota((slots, slots), 1)).astype(BF16)
        tags = lax.dot_general(
            tags.astype(BF16), same_slot, (((0,), (0,)), ((), ())), preferred_element_type=F32
        ).astype(jnp.int32)
        for h in range(heads):
            out_ref[h] = (tags[h : h + 1, :] == kinds).astype(BF16)

    return vmem_call(kernel, jax.ShapeDtypeStruct((heads, 16, slots), BF16), (True, False))(
        scalar(me), all_ids
    )


def cut_tokens(local_rows, core, chips):
    rows, depth = local_rows.shape
    half = depth // chips // 2

    def kernel(core_ref, in_ref, own_ref, other_ref, sems):
        copies = []
        for p in range(chips):
            for j, out_ref in enumerate((own_ref, other_ref)):
                first = (2 * p + lax.rem(core_ref[0] + j, 2)) * half
                copies.append(
                    pltpu.make_async_copy(
                        in_ref.at[:, pl.ds(pl.multiple_of(first, half), half)],
                        out_ref.at[p],
                        sems.at[2 * p + j],
                    )
                )
        for copy in copies:
            copy.start()
        for copy in copies:
            copy.wait()

    vmem = pl.BlockSpec(memory_space=pltpu.VMEM)
    return pl.pallas_call(
        kernel,
        out_shape=(jax.ShapeDtypeStruct((chips, rows, half), BF16),) * 2,
        in_specs=[
            pl.BlockSpec(memory_space=pltpu.SMEM),
            pl.BlockSpec(memory_space=pl.ANY),
        ],
        out_specs=(vmem, vmem),
        scratch_shapes=[pltpu.SemaphoreType.DMA((2 * chips,))],
        compiler_params=pltpu.CompilerParams(vmem_limit_bytes=VMEM_LIMIT),
    )(scalar(core), local_rows)


def products(total, tokens, halves, steps, x, me, places, out_types):
    chips, rows, half = tokens[0].shape
    width = halves[0].shape[1]
    given = () if total is None else total
    shard = halves[0].shape[0] // len(places[0])
    classes = 4

    def kernel(x_ref, me_ref, *refs):
        total_refs = refs[: len(given)]
        token_refs = refs[len(given) : len(given) + 2]
        half_refs = refs[len(given) + 2 : -3]
        out_refs, weight_ref = refs[-3:-1], refs[-1]
        results = [ref[...] for ref in total_refs] if given else [0.0, 0.0]
        for n, step in enumerate(steps):
            for ref, blocks in zip(half_refs[2 * n : 2 * n + 2], places):
                for i, (kind, number) in enumerate(blocks):
                    device = lax.rem(me_ref[0] + kind, classes) + classes * number
                    at = pl.multiple_of(device * shard, shard)
                    weight_ref[n, pl.ds(at, shard), :] = ref[i * shard : (i + 1) * shard, :]
            chip = lax.rem(x_ref[0] + step + chips, chips)
            for i, token_ref in enumerate(token_refs):
                results[i] += jnp.dot(
                    token_ref[chip], weight_ref[n], preferred_element_type=F32
                )
        for result, out_ref in zip(results, out_refs):
            out_ref[...] = result.astype(out_ref.dtype)

    operands = tuple(given) + tuple(tokens) + tuple(halves)
    return vmem_call(
        kernel,
        tuple(jax.ShapeDtypeStruct((rows, width), t) for t in out_types),
        (True, True) + (False,) * len(operands),
        scratch_shapes=[pltpu.VMEM((len(steps), half, width), BF16)],
    )(scalar(x), scalar(me), *operands)


def pack(own, received, slot_row, chosen, owners, capacity, head_dim):
    rows, width = own.shape
    heads = len(chosen)
    slots = owners * capacity

    def kernel(own_ref, received_ref, slot_ref, out_ref):
        for i, h in enumerate(chosen):
            place = iota((slots, rows), 0) == slot_ref[h : h + 1, :]
            place = place.astype(BF16)
            for m in range(2):
                cols = slice((m * heads + i) * head_dim, (m * heads + i + 1) * head_dim)
                total = own_ref[:, cols] + received_ref[:, cols].astype(F32)
                packed = jnp.dot(
                    place, total.astype(BF16), preferred_element_type=F32
                ).astype(BF16)
                out_ref[
                    :, i * capacity : (i + 1) * capacity, m * head_dim : (m + 1) * head_dim
                ] = packed.reshape(owners, capacity, head_dim)

    return vmem_call(
        kernel,
        jax.ShapeDtypeStruct((owners, heads * capacity, 2 * head_dim), BF16),
        (False,) * 3,
    )(own, received, slot_row)


def attend(blocks, members, chosen, before, capacity):
    sources, rows, width = blocks.shape
    head_dim = width // 2
    slots = sources * capacity
    scale = head_dim ** (-0.5)
    done = 0 if before is None else before.shape[1]
    given = () if before is None else (before,)

    def kernel(*refs):
        block_ref, member_ref = refs[:2]
        out_ref = refs[-1]
        if given:
            out_ref[:, :done, :] = refs[2][...]
        query = iota((slots, slots), 0)
        key = iota((slots, slots), 1)
        for i, h in enumerate(chosen):
            here = slice(i * capacity, (i + 1) * capacity)
            keys = block_ref[:, here, :head_dim].reshape(slots, head_dim)
            values = block_ref[:, here, head_dim:].reshape(slots, head_dim)
            member = member_ref[h]
            same = lax.dot_general(
                member, member, (((0,), (0,)), ((), ())), preferred_element_type=F32
            )
            scores = lax.dot_general(
                keys, keys, (((1,), (1,)), ((), ())), preferred_element_type=F32
            )
            scores = jnp.where(query == key, -100000.0, scores * scale)
            scores = jnp.where((same > 0.5) & (key <= query), scores, -1e30)
            row_max = jnp.max(scores, axis=1, keepdims=True)
            weights = jnp.exp(scores - row_max)
            total = jnp.sum(weights, axis=1, keepdims=True)
            probabilities = (weights / total).astype(BF16)
            result = jnp.dot(probabilities, values, preferred_element_type=F32).astype(BF16)
            there = slice(done + i * capacity, done + (i + 1) * capacity)
            out_ref[:, there, :] = result.reshape(sources, capacity, head_dim)

    return vmem_call(
        kernel,
        jax.ShapeDtypeStruct((sources, done + rows, head_dim), BF16),
        (False,) * (2 + len(given)),
    )(blocks, members, *given)


def unpack(returned, slot_col, capacity):
    owners, height, head_dim = returned.shape
    rows, heads = slot_col.shape
    slots = owners * capacity

    def kernel(block_ref, slot_ref, out_ref):
        for h in range(heads):
            block = block_ref[:, h * capacity : (h + 1) * capacity, :].reshape(slots, head_dim)
            place = slot_ref[:, h : h + 1] == iota((rows, slots), 1)
            out_ref[:, h * head_dim : (h + 1) * head_dim] = jnp.dot(
                place.astype(BF16), block, preferred_element_type=F32
            ).astype(BF16)

    return vmem_call(
        kernel, jax.ShapeDtypeStruct((rows, heads * head_dim), BF16), (False, False)
    )(returned, slot_col)


CLU = ("zq", "zr")


def shifted(block, step, axis):
    size = lax.axis_size(axis)
    return lax.ppermute(block, axis, [(i, (i + step) % size) for i in range(size)])


def body(tokens, proj_weight, clusters):
    rows, depth = tokens.shape[1:]
    owners = lax.axis_size(CLU)
    me = lax.axis_index(CLU)
    x = lax.axis_index("x")
    heads = clusters.shape[2]
    shard = proj_weight.shape[0]
    width = 2 * proj_weight.shape[2]
    head_dim = proj_weight.shape[2] // heads
    capacity = 2 * rows // owners
    chips = lax.axis_size("x")

    own = proj_weight.reshape(shard, 2, GROUPS, -1).transpose(0, 2, 1, 3)
    ids = clusters[0].T.astype(BF16).reshape(-1, 128)
    ids = jnp.pad(ids, ((0, shard - ids.shape[0]), (0, 0)))
    own = jnp.concatenate([own.reshape(shard, width), ids], axis=1)
    four = lax.all_gather(own, "zq", axis=0)
    below = shifted(four, 1, CLU)
    above = shifted(four, -1, CLU)
    beyond = [shifted(four[:2], 2, CLU), shifted(four[2:], -2, CLU)]
    places = (
        [(0, j) for j in range(4)] + [(3, j) for j in range(4)],
        [(1, j) for j in range(4)] + [(2, j) for j in range(4)],
    )

    mine, send = cut_tokens(tokens[0], lax.axis_index("core"), chips)
    both = (mine, lax.ppermute(send, "core", [(0, 1), (1, 0)]))
    slot_row, slot_col = routing(clusters[0], owners, capacity)

    def partial_sums(first, second):
        first_below, first_above = shifted(first, 1, "x"), shifted(first, -1, "x")
        second_below, second_above = shifted(second, 1, "x"), shifted(second, -1, "x")
        first_far, second_far = shifted(first_below, 1, "x"), shifted(second_above, -1, "x")
        total = products(
            None,
            both,
            [first, second, first_below, second_below, first_above, second_above],
            (0, -1, 1),
            x,
            me,
            places,
            (F32, F32),
        )
        kept, given = products(
            total, both, [first_far, second_far], (2,), x, me, places, (F32, BF16)
        )
        return kept, lax.ppermute(given, "core", [(0, 1), (1, 0)])

    incoming = []
    outgoing = None
    for g in range(GROUPS):
        group_width = width // GROUPS
        cols = slice(g * group_width, (g + 1) * group_width)
        chosen = range(g * heads // GROUPS, (g + 1) * heads // GROUPS)
        parts = (four, below, above, *beyond)
        if outgoing is not None:
            parts, outgoing = lax.optimization_barrier((parts, outgoing))
            incoming.append(
                lax.all_to_all(outgoing, CLU, split_axis=0, concat_axis=0, tiled=True)
            )
        parts = [part[:, :, cols].reshape(-1, group_width) for part in parts]
        kept, received = partial_sums(
            jnp.concatenate(parts[:2], axis=0), jnp.concatenate(parts[2:], axis=0)
        )
        outgoing = pack(kept, received, slot_row, chosen, owners, capacity, head_dim)
    incoming.append(lax.all_to_all(outgoing, CLU, split_axis=0, concat_axis=0, tiled=True))

    by_class = jnp.stack(
        [part[:, :16, width:] for part in (four, above, jnp.concatenate(beyond), below)]
    )
    by_class = jnp.roll(by_class, lax.axis_index("zr"), axis=0)
    all_ids = by_class.transpose(1, 0, 2, 3).reshape((owners,) + by_class.shape[2:])
    members = owned_members(all_ids, me, heads, capacity)
    replies = None
    for g in range(GROUPS):
        chosen = range(g * heads // GROUPS, (g + 1) * heads // GROUPS)
        replies = attend(incoming[g], members, chosen, replies, capacity)
    returned = lax.all_to_all(replies, CLU, split_axis=0, concat_axis=0, tiled=True)
    return unpack(returned, slot_col, capacity)[None]


def solution(mesh):
    ctx, clu, tp = (mesh.shape[name] for name in mesh.axis_names)
    fine = jax.sharding.Mesh(
        mesh.devices.reshape(ctx // 2, 2, clu // 4, 4, tp), ("x", "core") + CLU + ("tp",)
    )
    ctx_axes = ("x", "core")
    return jax.shard_map(
        body,
        mesh=fine,
        in_specs=(
            P(ctx_axes, CLU, None),
            P(ctx_axes + CLU, None, "tp"),
            P(ctx_axes, CLU, "tp"),
        ),
        out_specs=P(ctx_axes, CLU, "tp"),
        check_vma=False,
    )
```

```python
import jax
import jax.numpy as jnp
from jax import lax
from jax.experimental import pallas as pl
from jax.experimental.pallas import tpu as pltpu
from jax.sharding import PartitionSpec as P

CLUSTERS = 64
BF16 = jnp.bfloat16
F32 = jnp.float32
VMEM_LIMIT = 48 * 1024 * 1024


def vmem_call(kernel, out_shape, in_smem, **kwargs):
    vmem = pl.BlockSpec(memory_space=pltpu.VMEM)
    smem = pl.BlockSpec(memory_space=pltpu.SMEM)
    return pl.pallas_call(
        kernel,
        out_shape=out_shape,
        in_specs=[smem if flag else vmem for flag in in_smem],
        out_specs=jax.tree.map(lambda _: vmem, out_shape),
        compiler_params=pltpu.CompilerParams(vmem_limit_bytes=VMEM_LIMIT),
        **kwargs,
    )


def scalar(value):
    return jnp.reshape(value, (1,)).astype(jnp.int32)


def iota(shape, dim):
    return lax.broadcasted_iota(jnp.int32, shape, dim)


def routing(ids, owners, capacity):
    rows, heads = ids.shape
    per_owner = CLUSTERS // owners

    def kernel(ids_ref, ids_t_ref, slot_row_ref, slot_col_ref):
        before_col = (iota((rows, rows), 1) < iota((rows, rows), 0)).astype(BF16)
        before_row = (iota((rows, rows), 0) < iota((rows, rows), 1)).astype(BF16)
        for h in range(heads):
            owner_col = ids_ref[:, h : h + 1] // per_owner
            hot = owner_col == iota((rows, owners), 1)
            count = jnp.dot(before_col, hot.astype(BF16), preferred_element_type=F32)
            rank = jnp.sum(jnp.where(hot, count, 0.0), axis=1, keepdims=True)
            slot_col_ref[:, h : h + 1] = owner_col * capacity + rank.astype(jnp.int32)
            owner_row = ids_t_ref[h : h + 1, :] // per_owner
            hot = owner_row == iota((owners, rows), 0)
            count = jnp.dot(hot.astype(BF16), before_row, preferred_element_type=F32)
            rank = jnp.sum(jnp.where(hot, count, 0.0), axis=0, keepdims=True)
            slot_row_ref[h : h + 1, :] = owner_row * capacity + rank.astype(jnp.int32)

    return vmem_call(
        kernel,
        (
            jax.ShapeDtypeStruct((heads, rows), jnp.int32),
            jax.ShapeDtypeStruct((rows, heads), jnp.int32),
        ),
        (False, False),
    )(ids, ids.T)


def owned_members(all_ids, me, heads, capacity):
    sources, id_rows, lanes = all_ids.shape
    rows = sources * capacity // 2
    per_head = rows // lanes
    per_owner = CLUSTERS // sources
    slots = sources * capacity

    def kernel(me_ref, ids_ref, out_ref):
        before = (iota((rows, rows), 0) < iota((rows, rows), 1)).astype(BF16)
        place = iota((sources, capacity, rows), 1)
        kinds = iota((16, slots), 0) + 1
        column = iota((slots, lanes), 1)
        tags = jnp.zeros((slots, lanes), jnp.int32)
        for h in range(heads):
            ids = jnp.concatenate(
                [ids_ref[:, h * per_head + j, :] for j in range(per_head)], axis=1
            )
            ids = ids.astype(F32).astype(jnp.int32)
            owner = ids // per_owner
            mine = owner == me_ref[0]
            rank = jnp.dot(mine.astype(BF16), before, preferred_element_type=F32)
            rank = jnp.where(mine, rank.astype(jnp.int32), -1)
            tag = ids - owner * per_owner + 1
            placed = jnp.where(rank[:, None, :] == place, tag[:, None, :], 0)
            tag = jnp.sum(placed.reshape(slots, rows), axis=1, keepdims=True)
            tags = jnp.where(column == h, tag, tags)
        same_slot = (iota((slots, slots), 0) == iota((slots, slots), 1)).astype(BF16)
        tags = lax.dot_general(
            tags.astype(BF16), same_slot, (((0,), (0,)), ((), ())), preferred_element_type=F32
        ).astype(jnp.int32)
        for h in range(heads):
            out_ref[h] = (tags[h : h + 1, :] == kinds).astype(BF16)

    return vmem_call(kernel, jax.ShapeDtypeStruct((heads, 16, slots), BF16), (True, False))(
        scalar(me), all_ids
    )


def cut_tokens(local_rows, core, chips):
    rows, depth = local_rows.shape
    half = depth // chips // 2

    def kernel(core_ref, in_ref, out_ref, sems):
        copies = []
        for p in range(chips):
            for j in range(2):
                first = (2 * p + lax.rem(core_ref[0] + j, 2)) * half
                copies.append(
                    pltpu.make_async_copy(
                        in_ref.at[:, pl.ds(pl.multiple_of(first, half), half)],
                        out_ref.at[p, :, j * half : (j + 1) * half],
                        sems.at[2 * p + j],
                    )
                )
        for copy in copies:
            copy.start()
        for copy in copies:
            copy.wait()

    return pl.pallas_call(
        kernel,
        out_shape=jax.ShapeDtypeStruct((chips, rows, 2 * half), BF16),
        in_specs=[
            pl.BlockSpec(memory_space=pltpu.SMEM),
            pl.BlockSpec(memory_space=pl.ANY),
        ],
        out_specs=pl.BlockSpec(memory_space=pltpu.VMEM),
        scratch_shapes=[pltpu.SemaphoreType.DMA((2 * chips,))],
        compiler_params=pltpu.CompilerParams(vmem_limit_bytes=VMEM_LIMIT),
    )(scalar(core), local_rows)


def project(pieces, ring, other, me, places):
    chips, rows, depth = pieces.shape
    half, width = ring.shape
    shard = half // len(places)
    classes = 4

    def kernel(me_ref, pieces_ref, ring_ref, other_ref, out_ref, weight_ref):
        for j, ref in enumerate((ring_ref, other_ref)):
            for i, (kind, number) in enumerate(places):
                device = lax.rem(me_ref[0] + kind, classes) + classes * number
                at = pl.multiple_of(j * half + device * shard, shard)
                weight_ref[pl.ds(at, shard), :] = ref[i * shard : (i + 1) * shard, :]
        for p in range(chips):
            out_ref[p] = jnp.dot(
                pieces_ref[p], weight_ref[...], preferred_element_type=F32
            ).astype(BF16)

    return vmem_call(
        kernel,
        jax.ShapeDtypeStruct((chips, rows, width), BF16),
        (True, False, False, False),
        scratch_shapes=[pltpu.VMEM((depth, width), BF16)],
    )(scalar(me), pieces, ring, other)


def pack(partial, slot_row, owners, capacity, head_dim):
    parts, rows, width = partial.shape
    heads = slot_row.shape[0]
    slots = owners * capacity

    def kernel(partial_ref, slot_ref, out_ref):
        for h in range(heads):
            place = iota((slots, rows), 0) == slot_ref[h : h + 1, :]
            place = place.astype(BF16)
            for m in range(2):
                cols = slice((m * heads + h) * head_dim, (m * heads + h + 1) * head_dim)
                total = partial_ref[0, :, cols].astype(F32)
                for p in range(1, parts):
                    total += partial_ref[p, :, cols].astype(F32)
                packed = jnp.dot(
                    place, total.astype(BF16), preferred_element_type=F32
                ).astype(BF16)
                out_ref[
                    :, h * capacity : (h + 1) * capacity, m * head_dim : (m + 1) * head_dim
                ] = packed.reshape(owners, capacity, head_dim)

    return vmem_call(
        kernel,
        jax.ShapeDtypeStruct((owners, heads * capacity, 2 * head_dim), BF16),
        (False,) * 2,
    )(partial, slot_row)


def attend(blocks, members, capacity):
    sources, rows, width = blocks.shape
    head_dim = width // 2
    heads = rows // capacity
    slots = sources * capacity
    scale = head_dim ** (-0.5)

    def kernel(block_ref, member_ref, out_ref):
        query = iota((slots, slots), 0)
        key = iota((slots, slots), 1)
        for h in range(heads):
            here = slice(h * capacity, (h + 1) * capacity)
            keys = block_ref[:, here, :head_dim].reshape(slots, head_dim)
            values = block_ref[:, here, head_dim:].reshape(slots, head_dim)
            member = member_ref[h]
            same = lax.dot_general(
                member, member, (((0,), (0,)), ((), ())), preferred_element_type=F32
            )
            scores = lax.dot_general(
                keys, keys, (((1,), (1,)), ((), ())), preferred_element_type=F32
            )
            scores = jnp.where(query == key, -100000.0, scores * scale)
            scores = jnp.where((same > 0.5) & (key <= query), scores, -1e30)
            row_max = jnp.max(scores, axis=1, keepdims=True)
            weights = jnp.exp(scores - row_max)
            total = jnp.sum(weights, axis=1, keepdims=True)
            probabilities = (weights / total).astype(BF16)
            result = jnp.dot(probabilities, values, preferred_element_type=F32).astype(BF16)
            out_ref[:, here, :] = result.reshape(sources, capacity, head_dim)

    return vmem_call(
        kernel, jax.ShapeDtypeStruct((sources, rows, head_dim), BF16), (False, False)
    )(blocks, members)


def unpack(returned, slot_col, capacity):
    owners, height, head_dim = returned.shape
    rows, heads = slot_col.shape
    slots = owners * capacity

    def kernel(block_ref, slot_ref, out_ref):
        for h in range(heads):
            block = block_ref[:, h * capacity : (h + 1) * capacity, :].reshape(slots, head_dim)
            place = slot_ref[:, h : h + 1] == iota((rows, slots), 1)
            out_ref[:, h * head_dim : (h + 1) * head_dim] = jnp.dot(
                place.astype(BF16), block, preferred_element_type=F32
            ).astype(BF16)

    return vmem_call(
        kernel, jax.ShapeDtypeStruct((rows, heads * head_dim), BF16), (False, False)
    )(returned, slot_col)


CLU = ("zq", "zr")


def shifted(block, step, axis):
    size = lax.axis_size(axis)
    return lax.ppermute(block, axis, [(i, (i + step) % size) for i in range(size)])


def body(tokens, proj_weight, clusters):
    rows, depth = tokens.shape[1:]
    owners = lax.axis_size(CLU)
    me = lax.axis_index(CLU)
    heads = clusters.shape[2]
    shard = proj_weight.shape[0]
    width = 2 * proj_weight.shape[2]
    head_dim = proj_weight.shape[2] // heads
    capacity = 2 * rows // owners
    chips = lax.axis_size("x")

    pieces = cut_tokens(tokens[0], lax.axis_index("core"), chips)
    ids = clusters[0].T.astype(BF16).reshape(-1, 128)
    ids = jnp.pad(ids, ((0, shard - ids.shape[0]), (0, 0)))
    own = jnp.concatenate([proj_weight.reshape(shard, width), ids], axis=1)
    own, pieces = lax.optimization_barrier((own, pieces))
    pieces = lax.all_to_all(pieces, "x", split_axis=0, concat_axis=0, tiled=True)

    four = lax.all_gather(own, "zq", axis=0)
    below = shifted(four, 1, CLU)
    above = shifted(four, -1, CLU)
    beyond = [shifted(four[:2], 2, CLU), shifted(four[2:], -2, CLU)]
    ring = jnp.concatenate(
        [part[:, :, :width].reshape(-1, width) for part in (four, below, above, *beyond)], axis=0
    )
    other = lax.ppermute(ring, "core", [(0, 1), (1, 0)])
    places = [(kind, j) for kind in (0, 3, 1, 2) for j in range(4)]
    partial = project(pieces, ring, other, me, places)
    partial = lax.all_to_all(partial, "x", split_axis=0, concat_axis=0, tiled=True)

    slot_row, slot_col = routing(clusters[0], owners, capacity)
    outgoing = pack(partial, slot_row, owners, capacity, head_dim)
    incoming = lax.all_to_all(outgoing, CLU, split_axis=0, concat_axis=0, tiled=True)

    by_class = jnp.stack(
        [part[:, :16, width:] for part in (four, above, jnp.concatenate(beyond), below)]
    )
    by_class = jnp.roll(by_class, lax.axis_index("zr"), axis=0)
    all_ids = by_class.transpose(1, 0, 2, 3).reshape((owners,) + by_class.shape[2:])
    members = owned_members(all_ids, me, heads, capacity)
    replies = attend(incoming, members, capacity)
    returned = lax.all_to_all(replies, CLU, split_axis=0, concat_axis=0, tiled=True)
    return unpack(returned, slot_col, capacity)[None]


def solution(mesh):
    ctx, clu, tp = (mesh.shape[name] for name in mesh.axis_names)
    fine = jax.sharding.Mesh(
        mesh.devices.reshape(ctx // 2, 2, clu // 4, 4, tp), ("x", "core") + CLU + ("tp",)
    )
    ctx_axes = ("x", "core")
    return jax.shard_map(
        body,
        mesh=fine,
        in_specs=(
            P(ctx_axes, CLU, None),
            P(ctx_axes + CLU, None, "tp"),
            P(ctx_axes, CLU, "tp"),
        ),
        out_specs=P(ctx_axes, CLU, "tp"),
        check_vma=False,
    )
```

```python
import jax
import jax.numpy as jnp
from jax import lax
from jax.experimental import pallas as pl
from jax.experimental.pallas import tpu as pltpu
from jax.sharding import PartitionSpec as P

CLUSTERS = 64
BF16 = jnp.bfloat16
F32 = jnp.float32
VMEM_LIMIT = 48 * 1024 * 1024


def vmem_call(kernel, out_shape, in_smem, **kwargs):
    vmem = pl.BlockSpec(memory_space=pltpu.VMEM)
    smem = pl.BlockSpec(memory_space=pltpu.SMEM)
    return pl.pallas_call(
        kernel,
        out_shape=out_shape,
        in_specs=[smem if flag else vmem for flag in in_smem],
        out_specs=jax.tree.map(lambda _: vmem, out_shape),
        compiler_params=pltpu.CompilerParams(vmem_limit_bytes=VMEM_LIMIT),
        **kwargs,
    )


def scalar(value):
    return jnp.reshape(value, (1,)).astype(jnp.int32)


def iota(shape, dim):
    return lax.broadcasted_iota(jnp.int32, shape, dim)


def routing(ids, owners, capacity):
    rows, heads = ids.shape
    per_owner = CLUSTERS // owners

    def kernel(ids_ref, ids_t_ref, slot_row_ref, slot_col_ref):
        before_col = (iota((rows, rows), 1) < iota((rows, rows), 0)).astype(BF16)
        before_row = (iota((rows, rows), 0) < iota((rows, rows), 1)).astype(BF16)
        for h in range(heads):
            owner_col = ids_ref[:, h : h + 1] // per_owner
            hot = owner_col == iota((rows, owners), 1)
            count = jnp.dot(before_col, hot.astype(BF16), preferred_element_type=F32)
            rank = jnp.sum(jnp.where(hot, count, 0.0), axis=1, keepdims=True)
            slot_col_ref[:, h : h + 1] = owner_col * capacity + rank.astype(jnp.int32)
            owner_row = ids_t_ref[h : h + 1, :] // per_owner
            hot = owner_row == iota((owners, rows), 0)
            count = jnp.dot(hot.astype(BF16), before_row, preferred_element_type=F32)
            rank = jnp.sum(jnp.where(hot, count, 0.0), axis=0, keepdims=True)
            slot_row_ref[h : h + 1, :] = owner_row * capacity + rank.astype(jnp.int32)

    return vmem_call(
        kernel,
        (
            jax.ShapeDtypeStruct((heads, rows), jnp.int32),
            jax.ShapeDtypeStruct((rows, heads), jnp.int32),
        ),
        (False, False),
    )(ids, ids.T)


def owned_members(all_ids, me, heads, capacity):
    sources, id_rows, lanes = all_ids.shape
    rows = sources * capacity // 2
    per_head = rows // lanes
    per_owner = CLUSTERS // sources
    slots = sources * capacity

    def kernel(me_ref, ids_ref, out_ref):
        before = (iota((rows, rows), 0) < iota((rows, rows), 1)).astype(BF16)
        place = iota((sources, capacity, rows), 1)
        kinds = iota((16, slots), 0) + 1
        column = iota((slots, lanes), 1)
        tags = jnp.zeros((slots, lanes), jnp.int32)
        for h in range(heads):
            ids = jnp.concatenate(
                [ids_ref[:, h * per_head + j, :] for j in range(per_head)], axis=1
            )
            ids = ids.astype(F32).astype(jnp.int32)
            owner = ids // per_owner
            mine = owner == me_ref[0]
            rank = jnp.dot(mine.astype(BF16), before, preferred_element_type=F32)
            rank = jnp.where(mine, rank.astype(jnp.int32), -1)
            tag = ids - owner * per_owner + 1
            placed = jnp.where(rank[:, None, :] == place, tag[:, None, :], 0)
            tag = jnp.sum(placed.reshape(slots, rows), axis=1, keepdims=True)
            tags = jnp.where(column == h, tag, tags)
        same_slot = (iota((slots, slots), 0) == iota((slots, slots), 1)).astype(BF16)
        tags = lax.dot_general(
            tags.astype(BF16), same_slot, (((0,), (0,)), ((), ())), preferred_element_type=F32
        ).astype(jnp.int32)
        for h in range(heads):
            out_ref[h] = (tags[h : h + 1, :] == kinds).astype(BF16)

    return vmem_call(kernel, jax.ShapeDtypeStruct((heads, 16, slots), BF16), (True, False))(
        scalar(me), all_ids
    )


def cut_tokens(local_rows, core, chips):
    rows, depth = local_rows.shape
    half = depth // chips // 2

    def kernel(core_ref, in_ref, out_ref, sems):
        copies = []
        for p in range(chips):
            for j in range(2):
                first = (2 * p + lax.rem(core_ref[0] + j, 2)) * half
                copies.append(
                    pltpu.make_async_copy(
                        in_ref.at[:, pl.ds(pl.multiple_of(first, half), half)],
                        out_ref.at[p, :, j * half : (j + 1) * half],
                        sems.at[2 * p + j],
                    )
                )
        for copy in copies:
            copy.start()
        for copy in copies:
            copy.wait()

    return pl.pallas_call(
        kernel,
        out_shape=jax.ShapeDtypeStruct((chips, rows, 2 * half), BF16),
        in_specs=[
            pl.BlockSpec(memory_space=pltpu.SMEM),
            pl.BlockSpec(memory_space=pl.ANY),
        ],
        out_specs=pl.BlockSpec(memory_space=pltpu.VMEM),
        scratch_shapes=[pltpu.SemaphoreType.DMA((2 * chips,))],
        compiler_params=pltpu.CompilerParams(vmem_limit_bytes=VMEM_LIMIT),
    )(scalar(core), local_rows)


def project(pieces, ring, other, me, places):
    chips, rows, depth = pieces.shape
    half, width = ring.shape
    shard = half // len(places)
    classes = 4

    def kernel(me_ref, pieces_ref, ring_ref, other_ref, out_ref, weight_ref):
        for j, ref in enumerate((ring_ref, other_ref)):
            for i, (kind, number) in enumerate(places):
                device = lax.rem(me_ref[0] + kind, classes) + classes * number
                at = pl.multiple_of(j * half + device * shard, shard)
                weight_ref[pl.ds(at, shard), :] = ref[i * shard : (i + 1) * shard, :]
        for p in range(chips):
            out_ref[p] = jnp.dot(
                pieces_ref[p], weight_ref[...], preferred_element_type=F32
            ).astype(BF16)

    return vmem_call(
        kernel,
        jax.ShapeDtypeStruct((chips, rows, width), BF16),
        (True, False, False, False),
        scratch_shapes=[pltpu.VMEM((depth, width), BF16)],
    )(scalar(me), pieces, ring, other)


def pack(partial, slot_row, owners, capacity, head_dim):
    parts, rows, width = partial.shape
    heads = slot_row.shape[0]
    slots = owners * capacity

    def kernel(partial_ref, slot_ref, out_ref):
        for h in range(heads):
            place = iota((slots, rows), 0) == slot_ref[h : h + 1, :]
            place = place.astype(BF16)
            for m in range(2):
                cols = slice((m * heads + h) * head_dim, (m * heads + h + 1) * head_dim)
                total = partial_ref[0, :, cols].astype(F32)
                for p in range(1, parts):
                    total += partial_ref[p, :, cols].astype(F32)
                packed = jnp.dot(
                    place, total.astype(BF16), preferred_element_type=F32
                ).astype(BF16)
                out_ref[
                    :, h * capacity : (h + 1) * capacity, m * head_dim : (m + 1) * head_dim
                ] = packed.reshape(owners, capacity, head_dim)

    return vmem_call(
        kernel,
        jax.ShapeDtypeStruct((owners, heads * capacity, 2 * head_dim), BF16),
        (False,) * 2,
    )(partial, slot_row)


def attend(blocks, members, capacity):
    sources, rows, width = blocks.shape
    head_dim = width // 2
    heads = rows // capacity
    slots = sources * capacity
    scale = head_dim ** (-0.5)

    def kernel(block_ref, member_ref, out_ref):
        query = iota((slots, slots), 0)
        key = iota((slots, slots), 1)
        for h in range(heads):
            here = slice(h * capacity, (h + 1) * capacity)
            keys = block_ref[:, here, :head_dim].reshape(slots, head_dim)
            values = block_ref[:, here, head_dim:].reshape(slots, head_dim)
            member = member_ref[h]
            same = lax.dot_general(
                member, member, (((0,), (0,)), ((), ())), preferred_element_type=F32
            )
            scores = lax.dot_general(
                keys, keys, (((1,), (1,)), ((), ())), preferred_element_type=F32
            )
            scores = jnp.where(query == key, -100000.0, scores * scale)
            scores = jnp.where((same > 0.5) & (key <= query), scores, -1e30)
            row_max = jnp.max(scores, axis=1, keepdims=True)
            weights = jnp.exp(scores - row_max)
            total = jnp.sum(weights, axis=1, keepdims=True)
            probabilities = (weights / total).astype(BF16)
            result = jnp.dot(probabilities, values, preferred_element_type=F32).astype(BF16)
            out_ref[:, here, :] = result.reshape(sources, capacity, head_dim)

    return vmem_call(
        kernel, jax.ShapeDtypeStruct((sources, rows, head_dim), BF16), (False, False)
    )(blocks, members)


def unpack(returned, slot_col, capacity):
    owners, height, head_dim = returned.shape
    rows, heads = slot_col.shape
    slots = owners * capacity

    def kernel(block_ref, slot_ref, out_ref):
        for h in range(heads):
            block = block_ref[:, h * capacity : (h + 1) * capacity, :].reshape(slots, head_dim)
            place = slot_ref[:, h : h + 1] == iota((rows, slots), 1)
            out_ref[:, h * head_dim : (h + 1) * head_dim] = jnp.dot(
                place.astype(BF16), block, preferred_element_type=F32
            ).astype(BF16)

    return vmem_call(
        kernel, jax.ShapeDtypeStruct((rows, heads * head_dim), BF16), (False, False)
    )(returned, slot_col)


CLU = ("zq", "zr")


def shifted(block, step, axis):
    size = lax.axis_size(axis)
    return lax.ppermute(block, axis, [(i, (i + step) % size) for i in range(size)])


def body(tokens, proj_weight, clusters):
    rows, depth = tokens.shape[1:]
    owners = lax.axis_size(CLU)
    me = lax.axis_index(CLU)
    heads = clusters.shape[2]
    shard = proj_weight.shape[0]
    width = 2 * proj_weight.shape[2]
    head_dim = proj_weight.shape[2] // heads
    capacity = 2 * rows // owners
    chips = lax.axis_size("x")

    pieces = cut_tokens(tokens[0], lax.axis_index("core"), chips)
    ids = clusters[0].T.astype(BF16).reshape(-1, 128)
    ids = jnp.pad(ids, ((0, shard - ids.shape[0]), (0, 0)))
    own = jnp.concatenate([proj_weight.reshape(shard, width), ids], axis=1)
    own, pieces = lax.optimization_barrier((own, pieces))
    pieces = lax.all_to_all(pieces, "x", split_axis=0, concat_axis=0, tiled=True)

    four = lax.all_gather(own, "zq", axis=0)
    below = shifted(four, 1, CLU)
    above = shifted(four, -1, CLU)
    later, pieces = lax.optimization_barrier((four, pieces))
    beyond = [shifted(later[:2], 2, CLU), shifted(later[2:], -2, CLU)]
    ring = jnp.concatenate(
        [part[:, :, :width].reshape(-1, width) for part in (four, below, above, *beyond)], axis=0
    )
    other = lax.ppermute(ring, "core", [(0, 1), (1, 0)])
    places = [(kind, j) for kind in (0, 3, 1, 2) for j in range(4)]
    partial = project(pieces, ring, other, me, places)
    partial = lax.all_to_all(partial, "x", split_axis=0, concat_axis=0, tiled=True)

    slot_row, slot_col = routing(clusters[0], owners, capacity)
    outgoing = pack(partial, slot_row, owners, capacity, head_dim)
    incoming = lax.all_to_all(outgoing, CLU, split_axis=0, concat_axis=0, tiled=True)

    by_class = jnp.stack(
        [part[:, :16, width:] for part in (four, above, jnp.concatenate(beyond), below)]
    )
    by_class = jnp.roll(by_class, lax.axis_index("zr"), axis=0)
    all_ids = by_class.transpose(1, 0, 2, 3).reshape((owners,) + by_class.shape[2:])
    members = owned_members(all_ids, me, heads, capacity)
    replies = attend(incoming, members, capacity)
    returned = lax.all_to_all(replies, CLU, split_axis=0, concat_axis=0, tiled=True)
    return unpack(returned, slot_col, capacity)[None]


def solution(mesh):
    ctx, clu, tp = (mesh.shape[name] for name in mesh.axis_names)
    fine = jax.sharding.Mesh(
        mesh.devices.reshape(ctx // 2, 2, clu // 4, 4, tp), ("x", "core") + CLU + ("tp",)
    )
    ctx_axes = ("x", "core")
    return jax.shard_map(
        body,
        mesh=fine,
        in_specs=(
            P(ctx_axes, CLU, None),
            P(ctx_axes + CLU, None, "tp"),
            P(ctx_axes, CLU, "tp"),
        ),
        out_specs=P(ctx_axes, CLU, "tp"),
        check_vma=False,
    )
```

```python
import jax
import jax.numpy as jnp
from jax import lax
from jax.experimental import pallas as pl
from jax.experimental.pallas import tpu as pltpu
from jax.sharding import PartitionSpec as P

CLUSTERS = 64
BF16 = jnp.bfloat16
F32 = jnp.float32
VMEM_LIMIT = 48 * 1024 * 1024


def vmem_call(kernel, out_shape, in_smem, **kwargs):
    vmem = pl.BlockSpec(memory_space=pltpu.VMEM)
    smem = pl.BlockSpec(memory_space=pltpu.SMEM)
    return pl.pallas_call(
        kernel,
        out_shape=out_shape,
        in_specs=[smem if flag else vmem for flag in in_smem],
        out_specs=jax.tree.map(lambda _: vmem, out_shape),
        compiler_params=pltpu.CompilerParams(vmem_limit_bytes=VMEM_LIMIT),
        **kwargs,
    )


def scalar(value):
    return jnp.reshape(value, (1,)).astype(jnp.int32)


def iota(shape, dim):
    return lax.broadcasted_iota(jnp.int32, shape, dim)


def routing(ids, owners, capacity):
    rows, heads = ids.shape
    per_owner = CLUSTERS // owners

    def kernel(ids_ref, ids_t_ref, slot_row_ref, slot_col_ref):
        before_col = (iota((rows, rows), 1) < iota((rows, rows), 0)).astype(BF16)
        before_row = (iota((rows, rows), 0) < iota((rows, rows), 1)).astype(BF16)
        for h in range(heads):
            owner_col = ids_ref[:, h : h + 1] // per_owner
            hot = owner_col == iota((rows, owners), 1)
            count = jnp.dot(before_col, hot.astype(BF16), preferred_element_type=F32)
            rank = jnp.sum(jnp.where(hot, count, 0.0), axis=1, keepdims=True)
            slot_col_ref[:, h : h + 1] = owner_col * capacity + rank.astype(jnp.int32)
            owner_row = ids_t_ref[h : h + 1, :] // per_owner
            hot = owner_row == iota((owners, rows), 0)
            count = jnp.dot(hot.astype(BF16), before_row, preferred_element_type=F32)
            rank = jnp.sum(jnp.where(hot, count, 0.0), axis=0, keepdims=True)
            slot_row_ref[h : h + 1, :] = owner_row * capacity + rank.astype(jnp.int32)

    return vmem_call(
        kernel,
        (
            jax.ShapeDtypeStruct((heads, rows), jnp.int32),
            jax.ShapeDtypeStruct((rows, heads), jnp.int32),
        ),
        (False, False),
    )(ids, ids.T)


def owned_members(all_ids, me, heads, capacity):
    sources, id_rows, lanes = all_ids.shape
    rows = sources * capacity // 2
    per_head = rows // lanes
    per_owner = CLUSTERS // sources
    slots = sources * capacity

    def kernel(me_ref, ids_ref, out_ref):
        before = (iota((rows, rows), 0) < iota((rows, rows), 1)).astype(BF16)
        place = iota((sources, capacity, rows), 1)
        kinds = iota((16, slots), 0) + 1
        column = iota((slots, lanes), 1)
        tags = jnp.zeros((slots, lanes), jnp.int32)
        for h in range(heads):
            ids = jnp.concatenate(
                [ids_ref[:, h * per_head + j, :] for j in range(per_head)], axis=1
            )
            ids = ids.astype(F32).astype(jnp.int32)
            owner = ids // per_owner
            mine = owner == me_ref[0]
            rank = jnp.dot(mine.astype(BF16), before, preferred_element_type=F32)
            rank = jnp.where(mine, rank.astype(jnp.int32), -1)
            tag = ids - owner * per_owner + 1
            placed = jnp.where(rank[:, None, :] == place, tag[:, None, :], 0)
            tag = jnp.sum(placed.reshape(slots, rows), axis=1, keepdims=True)
            tags = jnp.where(column == h, tag, tags)
        same_slot = (iota((slots, slots), 0) == iota((slots, slots), 1)).astype(BF16)
        tags = lax.dot_general(
            tags.astype(BF16), same_slot, (((0,), (0,)), ((), ())), preferred_element_type=F32
        ).astype(jnp.int32)
        for h in range(heads):
            out_ref[h] = (tags[h : h + 1, :] == kinds).astype(BF16)

    return vmem_call(kernel, jax.ShapeDtypeStruct((heads, 16, slots), BF16), (True, False))(
        scalar(me), all_ids
    )


def cut_tokens(local_rows, core, chips):
    rows, depth = local_rows.shape
    half = depth // chips // 2

    def kernel(core_ref, in_ref, out_ref, sems):
        copies = []
        for p in range(chips):
            for j in range(2):
                first = (2 * p + lax.rem(core_ref[0] + j, 2)) * half
                copies.append(
                    pltpu.make_async_copy(
                        in_ref.at[:, pl.ds(pl.multiple_of(first, half), half)],
                        out_ref.at[p, :, j * half : (j + 1) * half],
                        sems.at[2 * p + j],
                    )
                )
        for copy in copies:
            copy.start()
        for copy in copies:
            copy.wait()

    return pl.pallas_call(
        kernel,
        out_shape=jax.ShapeDtypeStruct((chips, rows, 2 * half), BF16),
        in_specs=[
            pl.BlockSpec(memory_space=pltpu.SMEM),
            pl.BlockSpec(memory_space=pl.ANY),
        ],
        out_specs=pl.BlockSpec(memory_space=pltpu.VMEM),
        scratch_shapes=[pltpu.SemaphoreType.DMA((2 * chips,))],
        compiler_params=pltpu.CompilerParams(vmem_limit_bytes=VMEM_LIMIT),
    )(scalar(core), local_rows)


def project(pieces, ring, other, me, places):
    chips, rows, depth = pieces.shape
    half, width = ring.shape
    shard = half // len(places)
    classes = 4

    def kernel(me_ref, pieces_ref, ring_ref, other_ref, out_ref, weight_ref):
        for j, ref in enumerate((ring_ref, other_ref)):
            for i, (kind, number) in enumerate(places):
                device = lax.rem(me_ref[0] + kind, classes) + classes * number
                at = pl.multiple_of(j * half + device * shard, shard)
                weight_ref[pl.ds(at, shard), :] = ref[i * shard : (i + 1) * shard, :]
        for p in range(chips):
            out_ref[p] = jnp.dot(
                pieces_ref[p], weight_ref[...], preferred_element_type=F32
            ).astype(BF16)

    return vmem_call(
        kernel,
        jax.ShapeDtypeStruct((chips, rows, width), BF16),
        (True, False, False, False),
        scratch_shapes=[pltpu.VMEM((depth, width), BF16)],
    )(scalar(me), pieces, ring, other)


def pack(partial, slot_row, owners, capacity, head_dim):
    parts, rows, width = partial.shape
    heads = slot_row.shape[0]
    slots = owners * capacity

    def kernel(partial_ref, slot_ref, out_ref):
        for h in range(heads):
            place = iota((slots, rows), 0) == slot_ref[h : h + 1, :]
            place = place.astype(BF16)
            for m in range(2):
                cols = slice((m * heads + h) * head_dim, (m * heads + h + 1) * head_dim)
                total = partial_ref[0, :, cols].astype(F32)
                for p in range(1, parts):
                    total += partial_ref[p, :, cols].astype(F32)
                packed = jnp.dot(
                    place, total.astype(BF16), preferred_element_type=F32
                ).astype(BF16)
                out_ref[
                    :, h * capacity : (h + 1) * capacity, m * head_dim : (m + 1) * head_dim
                ] = packed.reshape(owners, capacity, head_dim)

    return vmem_call(
        kernel,
        jax.ShapeDtypeStruct((owners, heads * capacity, 2 * head_dim), BF16),
        (False,) * 2,
    )(partial, slot_row)


def attend(blocks, members, capacity):
    sources, rows, width = blocks.shape
    head_dim = width // 2
    heads = rows // capacity
    slots = sources * capacity
    scale = head_dim ** (-0.5)

    def kernel(block_ref, member_ref, out_ref):
        query = iota((slots, slots), 0)
        key = iota((slots, slots), 1)
        for h in range(heads):
            here = slice(h * capacity, (h + 1) * capacity)
            keys = block_ref[:, here, :head_dim].reshape(slots, head_dim)
            values = block_ref[:, here, head_dim:].reshape(slots, head_dim)
            member = member_ref[h]
            same = lax.dot_general(
                member, member, (((0,), (0,)), ((), ())), preferred_element_type=F32
            )
            scores = lax.dot_general(
                keys, keys, (((1,), (1,)), ((), ())), preferred_element_type=F32
            )
            scores = jnp.where(query == key, -100000.0, scores * scale)
            scores = jnp.where((same > 0.5) & (key <= query), scores, -1e30)
            row_max = jnp.max(scores, axis=1, keepdims=True)
            weights = jnp.exp(scores - row_max)
            total = jnp.sum(weights, axis=1, keepdims=True)
            probabilities = (weights / total).astype(BF16)
            result = jnp.dot(probabilities, values, preferred_element_type=F32).astype(BF16)
            out_ref[:, here, :] = result.reshape(sources, capacity, head_dim)

    return vmem_call(
        kernel, jax.ShapeDtypeStruct((sources, rows, head_dim), BF16), (False, False)
    )(blocks, members)


def unpack(returned, slot_col, capacity):
    owners, height, head_dim = returned.shape
    rows, heads = slot_col.shape
    slots = owners * capacity

    def kernel(block_ref, slot_ref, out_ref):
        for h in range(heads):
            block = block_ref[:, h * capacity : (h + 1) * capacity, :].reshape(slots, head_dim)
            place = slot_ref[:, h : h + 1] == iota((rows, slots), 1)
            out_ref[:, h * head_dim : (h + 1) * head_dim] = jnp.dot(
                place.astype(BF16), block, preferred_element_type=F32
            ).astype(BF16)

    return vmem_call(
        kernel, jax.ShapeDtypeStruct((rows, heads * head_dim), BF16), (False, False)
    )(returned, slot_col)


CLU = ("zq", "zr")


def shifted(block, step, axis):
    size = lax.axis_size(axis)
    return lax.ppermute(block, axis, [(i, (i + step) % size) for i in range(size)])


def body(tokens, proj_weight, clusters):
    rows, depth = tokens.shape[1:]
    owners = lax.axis_size(CLU)
    me = lax.axis_index(CLU)
    heads = clusters.shape[2]
    shard = proj_weight.shape[0]
    width = 2 * proj_weight.shape[2]
    head_dim = proj_weight.shape[2] // heads
    capacity = 2 * rows // owners
    chips = lax.axis_size("x")

    pieces = cut_tokens(tokens[0], lax.axis_index("core"), chips)
    ids = clusters[0].T.astype(BF16).reshape(-1, 128)
    ids = jnp.pad(ids, ((0, shard - ids.shape[0]), (0, 0)))
    own = jnp.concatenate([proj_weight.reshape(shard, width), ids], axis=1)
    own, pieces = lax.optimization_barrier((own, pieces))
    pieces = lax.all_to_all(pieces, "x", split_axis=0, concat_axis=0, tiled=True)

    four = lax.all_gather(own, "zq", axis=0)
    below = shifted(four, 1, CLU)
    later, pieces = lax.optimization_barrier((four, pieces))
    above = shifted(later, -1, CLU)
    beyond = [shifted(four[:2], 2, CLU), shifted(four[2:], -2, CLU)]
    ring = jnp.concatenate(
        [part[:, :, :width].reshape(-1, width) for part in (four, below, above, *beyond)], axis=0
    )
    other = lax.ppermute(ring, "core", [(0, 1), (1, 0)])
    places = [(kind, j) for kind in (0, 3, 1, 2) for j in range(4)]
    partial = project(pieces, ring, other, me, places)
    partial = lax.all_to_all(partial, "x", split_axis=0, concat_axis=0, tiled=True)

    slot_row, slot_col = routing(clusters[0], owners, capacity)
    outgoing = pack(partial, slot_row, owners, capacity, head_dim)
    incoming = lax.all_to_all(outgoing, CLU, split_axis=0, concat_axis=0, tiled=True)

    by_class = jnp.stack(
        [part[:, :16, width:] for part in (four, above, jnp.concatenate(beyond), below)]
    )
    by_class = jnp.roll(by_class, lax.axis_index("zr"), axis=0)
    all_ids = by_class.transpose(1, 0, 2, 3).reshape((owners,) + by_class.shape[2:])
    members = owned_members(all_ids, me, heads, capacity)
    replies = attend(incoming, members, capacity)
    returned = lax.all_to_all(replies, CLU, split_axis=0, concat_axis=0, tiled=True)
    return unpack(returned, slot_col, capacity)[None]


def solution(mesh):
    ctx, clu, tp = (mesh.shape[name] for name in mesh.axis_names)
    fine = jax.sharding.Mesh(
        mesh.devices.reshape(ctx // 2, 2, clu // 4, 4, tp), ("x", "core") + CLU + ("tp",)
    )
    ctx_axes = ("x", "core")
    return jax.shard_map(
        body,
        mesh=fine,
        in_specs=(
            P(ctx_axes, CLU, None),
            P(ctx_axes + CLU, None, "tp"),
            P(ctx_axes, CLU, "tp"),
        ),
        out_specs=P(ctx_axes, CLU, "tp"),
        check_vma=False,
    )
```

```python
import jax
import jax.numpy as jnp
from jax import lax
from jax.experimental import pallas as pl
from jax.experimental.pallas import tpu as pltpu
from jax.sharding import PartitionSpec as P

CLUSTERS = 64
BF16 = jnp.bfloat16
F32 = jnp.float32
VMEM_LIMIT = 48 * 1024 * 1024


def vmem_call(kernel, out_shape, in_smem, **kwargs):
    vmem = pl.BlockSpec(memory_space=pltpu.VMEM)
    smem = pl.BlockSpec(memory_space=pltpu.SMEM)
    return pl.pallas_call(
        kernel,
        out_shape=out_shape,
        in_specs=[smem if flag else vmem for flag in in_smem],
        out_specs=jax.tree.map(lambda _: vmem, out_shape),
        compiler_params=pltpu.CompilerParams(vmem_limit_bytes=VMEM_LIMIT),
        **kwargs,
    )


def scalar(value):
    return jnp.reshape(value, (1,)).astype(jnp.int32)


def iota(shape, dim):
    return lax.broadcasted_iota(jnp.int32, shape, dim)


def routing(ids, owners, capacity):
    rows, heads = ids.shape
    per_owner = CLUSTERS // owners

    def kernel(ids_ref, ids_t_ref, slot_row_ref, slot_col_ref):
        before_col = (iota((rows, rows), 1) < iota((rows, rows), 0)).astype(BF16)
        before_row = (iota((rows, rows), 0) < iota((rows, rows), 1)).astype(BF16)
        for h in range(heads):
            owner_col = ids_ref[:, h : h + 1] // per_owner
            hot = owner_col == iota((rows, owners), 1)
            count = jnp.dot(before_col, hot.astype(BF16), preferred_element_type=F32)
            rank = jnp.sum(jnp.where(hot, count, 0.0), axis=1, keepdims=True)
            slot_col_ref[:, h : h + 1] = owner_col * capacity + rank.astype(jnp.int32)
            owner_row = ids_t_ref[h : h + 1, :] // per_owner
            hot = owner_row == iota((owners, rows), 0)
            count = jnp.dot(hot.astype(BF16), before_row, preferred_element_type=F32)
            rank = jnp.sum(jnp.where(hot, count, 0.0), axis=0, keepdims=True)
            slot_row_ref[h : h + 1, :] = owner_row * capacity + rank.astype(jnp.int32)

    return vmem_call(
        kernel,
        (
            jax.ShapeDtypeStruct((heads, rows), jnp.int32),
            jax.ShapeDtypeStruct((rows, heads), jnp.int32),
        ),
        (False, False),
    )(ids, ids.T)


def owned_members(all_ids, me, heads, capacity):
    sources, id_rows, lanes = all_ids.shape
    rows = sources * capacity // 2
    per_head = rows // lanes
    per_owner = CLUSTERS // sources
    slots = sources * capacity

    def kernel(me_ref, ids_ref, out_ref):
        before = (iota((rows, rows), 0) < iota((rows, rows), 1)).astype(BF16)
        place = iota((sources, capacity, rows), 1)
        kinds = iota((16, slots), 0) + 1
        column = iota((slots, lanes), 1)
        tags = jnp.zeros((slots, lanes), jnp.int32)
        for h in range(heads):
            ids = jnp.concatenate(
                [ids_ref[:, h * per_head + j, :] for j in range(per_head)], axis=1
            )
            ids = ids.astype(F32).astype(jnp.int32)
            owner = ids // per_owner
            mine = owner == me_ref[0]
            rank = jnp.dot(mine.astype(BF16), before, preferred_element_type=F32)
            rank = jnp.where(mine, rank.astype(jnp.int32), -1)
            tag = ids - owner * per_owner + 1
            placed = jnp.where(rank[:, None, :] == place, tag[:, None, :], 0)
            tag = jnp.sum(placed.reshape(slots, rows), axis=1, keepdims=True)
            tags = jnp.where(column == h, tag, tags)
        same_slot = (iota((slots, slots), 0) == iota((slots, slots), 1)).astype(BF16)
        tags = lax.dot_general(
            tags.astype(BF16), same_slot, (((0,), (0,)), ((), ())), preferred_element_type=F32
        ).astype(jnp.int32)
        for h in range(heads):
            out_ref[h] = (tags[h : h + 1, :] == kinds).astype(BF16)

    return vmem_call(kernel, jax.ShapeDtypeStruct((heads, 16, slots), BF16), (True, False))(
        scalar(me), all_ids
    )


def cut_tokens(local_rows, core, chips):
    rows, depth = local_rows.shape
    half = depth // chips // 2

    def kernel(core_ref, in_ref, out_ref, sems):
        copies = []
        for p in range(chips):
            for j in range(2):
                first = (2 * p + lax.rem(core_ref[0] + j, 2)) * half
                copies.append(
                    pltpu.make_async_copy(
                        in_ref.at[:, pl.ds(pl.multiple_of(first, half), half)],
                        out_ref.at[p, :, j * half : (j + 1) * half],
                        sems.at[2 * p + j],
                    )
                )
        for copy in copies:
            copy.start()
        for copy in copies:
            copy.wait()

    return pl.pallas_call(
        kernel,
        out_shape=jax.ShapeDtypeStruct((chips, rows, 2 * half), BF16),
        in_specs=[
            pl.BlockSpec(memory_space=pltpu.SMEM),
            pl.BlockSpec(memory_space=pltpu.HBM),
        ],
        out_specs=pl.BlockSpec(memory_space=pltpu.VMEM),
        scratch_shapes=[pltpu.SemaphoreType.DMA((2 * chips,))],
        compiler_params=pltpu.CompilerParams(vmem_limit_bytes=VMEM_LIMIT),
    )(scalar(core), local_rows)


def project(pieces, ring, other, x, me, steps, places):
    chips, rows, depth = pieces.shape
    half, width = ring.shape
    shard = half // len(places)
    classes = 4

    def kernel(x_ref, me_ref, pieces_ref, ring_ref, other_ref, *refs):
        out_refs, weight_ref = refs[:-1], refs[-1]
        for j, ref in enumerate((ring_ref, other_ref)):
            for i, (kind, number) in enumerate(places):
                device = lax.rem(me_ref[0] + kind, classes) + classes * number
                at = pl.multiple_of(j * half + device * shard, shard)
                weight_ref[pl.ds(at, shard), :] = ref[i * shard : (i + 1) * shard, :]
        for step, out_ref in zip(steps, out_refs):
            p = lax.rem(x_ref[0] + step + chips, chips)
            out_ref[...] = jnp.dot(
                pieces_ref[p], weight_ref[...], preferred_element_type=F32
            ).astype(BF16)

    return vmem_call(
        kernel,
        (jax.ShapeDtypeStruct((rows, width), BF16),) * len(steps),
        (True, True, False, False, False),
        scratch_shapes=[pltpu.VMEM((depth, width), BF16)],
    )(scalar(x), scalar(me), pieces, ring, other)


def exchange_x(parts, steps):
    chips = lax.axis_size("x")
    received = []
    for core in (1, 0):
        for i, step in enumerate(steps):
            pairs = [(2 * x + core, (x + step) % chips * 2 + core) for x in range(chips)]
            received.append(lax.ppermute(parts[i], ("x", "core"), pairs))
        if core == 1:
            ready = sum(part[:16, :128] for part in received)
            ready = lax.ppermute(ready, "core", [(1, 0)])
            parts, ready = lax.optimization_barrier((parts, ready))
    return received, ready


def pack(partials, ready, slot_row, owners, capacity, head_dim):
    rows, width = partials[0].shape
    heads = slot_row.shape[0]
    slots = owners * capacity

    def kernel(*refs):
        slot_ref, _, out_ref = refs[-3:]
        for h in range(heads):
            place = iota((slots, rows), 0) == slot_ref[h : h + 1, :]
            place = place.astype(BF16)
            for m in range(2):
                cols = slice((m * heads + h) * head_dim, (m * heads + h + 1) * head_dim)
                total = refs[0][:, cols].astype(F32)
                for ref in refs[1:-3]:
                    total += ref[:, cols].astype(F32)
                packed = jnp.dot(
                    place, total.astype(BF16), preferred_element_type=F32
                ).astype(BF16)
                out_ref[
                    :, h * capacity : (h + 1) * capacity, m * head_dim : (m + 1) * head_dim
                ] = packed.reshape(owners, capacity, head_dim)

    return vmem_call(
        kernel,
        jax.ShapeDtypeStruct((owners, heads * capacity, 2 * head_dim), BF16),
        (False,) * (len(partials) + 2),
    )(*partials, slot_row, ready)


def attend(blocks, members, capacity):
    sources, rows, width = blocks.shape
    head_dim = width // 2
    heads = rows // capacity
    slots = sources * capacity
    scale = head_dim ** (-0.5)

    def kernel(block_ref, member_ref, out_ref):
        query = iota((slots, slots), 0)
        key = iota((slots, slots), 1)
        for h in range(heads):
            here = slice(h * capacity, (h + 1) * capacity)
            keys = block_ref[:, here, :head_dim].reshape(slots, head_dim)
            values = block_ref[:, here, head_dim:].reshape(slots, head_dim)
            member = member_ref[h]
            same = lax.dot_general(
                member, member, (((0,), (0,)), ((), ())), preferred_element_type=F32
            )
            scores = lax.dot_general(
                keys, keys, (((1,), (1,)), ((), ())), preferred_element_type=F32
            )
            scores = jnp.where(query == key, -100000.0, scores * scale)
            scores = jnp.where((same > 0.5) & (key <= query), scores, -1e30)
            row_max = jnp.max(scores, axis=1, keepdims=True)
            weights = jnp.exp(scores - row_max)
            total = jnp.sum(weights, axis=1, keepdims=True)
            probabilities = (weights / total).astype(BF16)
            result = jnp.dot(probabilities, values, preferred_element_type=F32).astype(BF16)
            out_ref[:, here, :] = result.reshape(sources, capacity, head_dim)

    return vmem_call(
        kernel, jax.ShapeDtypeStruct((sources, rows, head_dim), BF16), (False, False)
    )(blocks, members)


def unpack(returned, slot_col, capacity):
    owners, height, head_dim = returned.shape
    rows, heads = slot_col.shape
    slots = owners * capacity

    def kernel(block_ref, slot_ref, out_ref):
        for h in range(heads):
            block = block_ref[:, h * capacity : (h + 1) * capacity, :].reshape(slots, head_dim)
            place = slot_ref[:, h : h + 1] == iota((rows, slots), 1)
            out_ref[:, h * head_dim : (h + 1) * head_dim] = jnp.dot(
                place.astype(BF16), block, preferred_element_type=F32
            ).astype(BF16)

    return vmem_call(
        kernel, jax.ShapeDtypeStruct((rows, heads * head_dim), BF16), (False, False)
    )(returned, slot_col)


CLU = ("zq", "zr")


def shifted(block, step, axis):
    size = lax.axis_size(axis)
    return lax.ppermute(block, axis, [(i, (i + step) % size) for i in range(size)])


def body(tokens, proj_weight, clusters):
    rows, depth = tokens.shape[1:]
    owners = lax.axis_size(CLU)
    me = lax.axis_index(CLU)
    heads = clusters.shape[2]
    shard = proj_weight.shape[0]
    width = 2 * proj_weight.shape[2]
    head_dim = proj_weight.shape[2] // heads
    capacity = 2 * rows // owners
    chips = lax.axis_size("x")

    pieces = cut_tokens(tokens[0], lax.axis_index("core"), chips)
    ids = clusters[0].T.astype(BF16).reshape(-1, 128)
    ids = jnp.pad(ids, ((0, shard - ids.shape[0]), (0, 0)))
    own = jnp.concatenate([proj_weight.reshape(shard, width), ids], axis=1)
    own, pieces = lax.optimization_barrier((own, pieces))
    pieces = lax.all_to_all(pieces, "x", split_axis=0, concat_axis=0, tiled=True)

    four = lax.all_gather(own, "zq", axis=0)
    below = shifted(four, 1, CLU)
    later, pieces = lax.optimization_barrier((four, pieces))
    above = shifted(later, -1, CLU)
    beyond = [shifted(four[:2], 2, CLU), shifted(four[2:], -2, CLU)]
    ring = jnp.concatenate(
        [part[:, :, :width].reshape(-1, width) for part in (four, below, above, *beyond)], axis=0
    )
    other = lax.ppermute(ring, "core", [(0, 1), (1, 0)])
    places = [(kind, j) for kind in (0, 3, 1, 2) for j in range(4)]
    steps = (2, 1, -1, 0)
    sent = project(pieces, ring, other, lax.axis_index("x"), me, steps, places)
    received, ready = exchange_x(sent[:-1], steps[:-1])
    partials = [sent[-1]] + received

    slot_row, slot_col = routing(clusters[0], owners, capacity)
    outgoing = pack(partials, ready, slot_row, owners, capacity, head_dim)
    incoming = lax.all_to_all(outgoing, CLU, split_axis=0, concat_axis=0, tiled=True)

    by_class = jnp.stack(
        [part[:, :16, width:] for part in (four, above, jnp.concatenate(beyond), below)]
    )
    by_class = jnp.roll(by_class, lax.axis_index("zr"), axis=0)
    all_ids = by_class.transpose(1, 0, 2, 3).reshape((owners,) + by_class.shape[2:])
    members = owned_members(all_ids, me, heads, capacity)
    replies = attend(incoming, members, capacity)
    returned = lax.all_to_all(replies, CLU, split_axis=0, concat_axis=0, tiled=True)
    return unpack(returned, slot_col, capacity)[None]


def solution(mesh):
    ctx, clu, tp = (mesh.shape[name] for name in mesh.axis_names)
    fine = jax.sharding.Mesh(
        mesh.devices.reshape(ctx // 2, 2, clu // 4, 4, tp), ("x", "core") + CLU + ("tp",)
    )
    ctx_axes = ("x", "core")
    return jax.shard_map(
        body,
        mesh=fine,
        in_specs=(
            P(ctx_axes, CLU, None),
            P(ctx_axes + CLU, None, "tp"),
            P(ctx_axes, CLU, "tp"),
        ),
        out_specs=P(ctx_axes, CLU, "tp"),
        check_vma=False,
    )
```

```python
import jax
import jax.numpy as jnp
from jax import lax
from jax.experimental import pallas as pl
from jax.experimental.pallas import tpu as pltpu
from jax.sharding import PartitionSpec as P

CLUSTERS = 64
BF16 = jnp.bfloat16
F32 = jnp.float32
VMEM_LIMIT = 48 * 1024 * 1024


def vmem_call(kernel, out_shape, in_smem, **kwargs):
    vmem = pl.BlockSpec(memory_space=pltpu.VMEM)
    smem = pl.BlockSpec(memory_space=pltpu.SMEM)
    return pl.pallas_call(
        kernel,
        out_shape=out_shape,
        in_specs=[smem if flag else vmem for flag in in_smem],
        out_specs=jax.tree.map(lambda _: vmem, out_shape),
        compiler_params=pltpu.CompilerParams(vmem_limit_bytes=VMEM_LIMIT),
        **kwargs,
    )


def scalar(value):
    return jnp.reshape(value, (1,)).astype(jnp.int32)


def iota(shape, dim):
    return lax.broadcasted_iota(jnp.int32, shape, dim)


def routing(ids, owners, capacity):
    rows, heads = ids.shape
    per_owner = CLUSTERS // owners

    def kernel(ids_ref, ids_t_ref, slot_row_ref, slot_col_ref):
        before_col = (iota((rows, rows), 1) < iota((rows, rows), 0)).astype(BF16)
        before_row = (iota((rows, rows), 0) < iota((rows, rows), 1)).astype(BF16)
        for h in range(heads):
            owner_col = ids_ref[:, h : h + 1] // per_owner
            hot = owner_col == iota((rows, owners), 1)
            count = jnp.dot(before_col, hot.astype(BF16), preferred_element_type=F32)
            rank = jnp.sum(jnp.where(hot, count, 0.0), axis=1, keepdims=True)
            slot_col_ref[:, h : h + 1] = owner_col * capacity + rank.astype(jnp.int32)
            owner_row = ids_t_ref[h : h + 1, :] // per_owner
            hot = owner_row == iota((owners, rows), 0)
            count = jnp.dot(hot.astype(BF16), before_row, preferred_element_type=F32)
            rank = jnp.sum(jnp.where(hot, count, 0.0), axis=0, keepdims=True)
            slot_row_ref[h : h + 1, :] = owner_row * capacity + rank.astype(jnp.int32)

    return vmem_call(
        kernel,
        (
            jax.ShapeDtypeStruct((heads, rows), jnp.int32),
            jax.ShapeDtypeStruct((rows, heads), jnp.int32),
        ),
        (False, False),
    )(ids, ids.T)


def owned_members(all_ids, me, heads, capacity):
    sources, id_rows, lanes = all_ids.shape
    rows = sources * capacity // 2
    per_head = rows // lanes
    per_owner = CLUSTERS // sources
    slots = sources * capacity

    def kernel(me_ref, ids_ref, out_ref):
        before = (iota((rows, rows), 0) < iota((rows, rows), 1)).astype(BF16)
        place = iota((sources, capacity, rows), 1)
        kinds = iota((16, slots), 0) + 1
        column = iota((slots, lanes), 1)
        tags = jnp.zeros((slots, lanes), jnp.int32)
        for h in range(heads):
            ids = jnp.concatenate(
                [ids_ref[:, h * per_head + j, :] for j in range(per_head)], axis=1
            )
            ids = ids.astype(F32).astype(jnp.int32)
            owner = ids // per_owner
            mine = owner == me_ref[0]
            rank = jnp.dot(mine.astype(BF16), before, preferred_element_type=F32)
            rank = jnp.where(mine, rank.astype(jnp.int32), -1)
            tag = ids - owner * per_owner + 1
            placed = jnp.where(rank[:, None, :] == place, tag[:, None, :], 0)
            tag = jnp.sum(placed.reshape(slots, rows), axis=1, keepdims=True)
            tags = jnp.where(column == h, tag, tags)
        same_slot = (iota((slots, slots), 0) == iota((slots, slots), 1)).astype(BF16)
        tags = lax.dot_general(
            tags.astype(BF16), same_slot, (((0,), (0,)), ((), ())), preferred_element_type=F32
        ).astype(jnp.int32)
        for h in range(heads):
            out_ref[h] = (tags[h : h + 1, :] == kinds).astype(BF16)

    return vmem_call(kernel, jax.ShapeDtypeStruct((heads, 16, slots), BF16), (True, False))(
        scalar(me), all_ids
    )


def cut_tokens(local_rows, core, chips):
    rows, depth = local_rows.shape
    half = depth // chips // 2

    def kernel(core_ref, in_ref, out_ref, sems):
        copies = []
        for p in range(chips):
            for j in range(2):
                first = (2 * p + lax.rem(core_ref[0] + j, 2)) * half
                copies.append(
                    pltpu.make_async_copy(
                        in_ref.at[:, pl.ds(pl.multiple_of(first, half), half)],
                        out_ref.at[p, :, j * half : (j + 1) * half],
                        sems.at[2 * p + j],
                    )
                )
        for copy in copies:
            copy.start()
        for copy in copies:
            copy.wait()

    return pl.pallas_call(
        kernel,
        out_shape=jax.ShapeDtypeStruct((chips, rows, 2 * half), BF16),
        in_specs=[
            pl.BlockSpec(memory_space=pltpu.SMEM),
            pl.BlockSpec(memory_space=pltpu.VMEM),
        ],
        out_specs=pl.BlockSpec(memory_space=pl.ANY),
        scratch_shapes=[pltpu.SemaphoreType.DMA((2 * chips,))],
        compiler_params=pltpu.CompilerParams(vmem_limit_bytes=VMEM_LIMIT),
    )(scalar(core), local_rows)


def assemble(parts, places, me, width):
    shard = parts[0].shape[1]
    count = sum(part.shape[0] for part in parts)
    classes = 4

    def kernel(me_ref, *refs):
        out_ref = refs[-1]
        for ref, (kind, first) in zip(refs, places):
            device = lax.rem(me_ref[0] + kind, classes) + classes * first
            for j in range(ref.shape[0]):
                at = pl.multiple_of((device + classes * j) * shard, shard)
                out_ref[pl.ds(at, shard), :] = ref[j, :, :width]

    return vmem_call(
        kernel,
        jax.ShapeDtypeStruct((count * shard, width), BF16),
        (True,) + (False,) * len(parts),
    )(scalar(me), *parts)


def project(pieces, ring, other, x, steps):
    chips, rows, depth = pieces.shape
    half, width = ring.shape

    def kernel(x_ref, pieces_ref, ring_ref, other_ref, *out_refs):
        for step, out_ref in zip(steps, out_refs):
            p = lax.rem(x_ref[0] + step + chips, chips)
            total = jnp.dot(pieces_ref[p, :, :half], ring_ref[...], preferred_element_type=F32)
            total += jnp.dot(pieces_ref[p, :, half:], other_ref[...], preferred_element_type=F32)
            out_ref[...] = total.astype(BF16)

    return vmem_call(
        kernel,
        (jax.ShapeDtypeStruct((rows, width), BF16),) * len(steps),
        (True, False, False, False),
    )(scalar(x), pieces, ring, other)


def exchange_x(parts, steps):
    chips = lax.axis_size("x")
    received = []
    for core in (1, 0):
        for i, step in enumerate(steps):
            pairs = [(2 * x + core, (x + step) % chips * 2 + core) for x in range(chips)]
            received.append(lax.ppermute(parts[i], ("x", "core"), pairs))
        if core == 1:
            ready = sum(part[:16, :128] for part in received)
            ready = lax.ppermute(ready, "core", [(1, 0)])
            parts, ready = lax.optimization_barrier((parts, ready))
    return received, ready


def pack(own, received, ready, slot_row, core, owners, capacity, head_dim):
    rows, width = own.shape
    heads = slot_row.shape[0]
    slots = owners * capacity
    count = len(received) // 2

    def kernel(core_ref, own_ref, *refs):
        slot_ref, _, out_ref = refs[-3:]

        def place_sums(part_refs):
            for h in range(heads):
                place = iota((slots, rows), 0) == slot_ref[h : h + 1, :]
                place = place.astype(BF16)
                for m in range(2):
                    cols = slice((m * heads + h) * head_dim, (m * heads + h + 1) * head_dim)
                    total = own_ref[:, cols].astype(F32)
                    for ref in part_refs:
                        total += ref[:, cols].astype(F32)
                    packed = jnp.dot(
                        place, total.astype(BF16), preferred_element_type=F32
                    ).astype(BF16)
                    out_ref[
                        :, h * capacity : (h + 1) * capacity, m * head_dim : (m + 1) * head_dim
                    ] = packed.reshape(owners, capacity, head_dim)

        @pl.when(core_ref[0] == 1)
        def _():
            place_sums(refs[:count])

        @pl.when(core_ref[0] == 0)
        def _():
            place_sums(refs[count : 2 * count])

    return vmem_call(
        kernel,
        jax.ShapeDtypeStruct((owners, heads * capacity, 2 * head_dim), BF16),
        (True,) + (False,) * (len(received) + 3),
    )(scalar(core), own, *received, slot_row, ready)


def attend(blocks, members, capacity):
    sources, rows, width = blocks.shape
    head_dim = width // 2
    heads = rows // capacity
    slots = sources * capacity
    scale = head_dim ** (-0.5)

    def kernel(block_ref, member_ref, out_ref):
        query = iota((slots, slots), 0)
        key = iota((slots, slots), 1)
        for h in range(heads):
            here = slice(h * capacity, (h + 1) * capacity)
            keys = block_ref[:, here, :head_dim].reshape(slots, head_dim)
            values = block_ref[:, here, head_dim:].reshape(slots, head_dim)
            member = member_ref[h]
            same = lax.dot_general(
                member, member, (((0,), (0,)), ((), ())), preferred_element_type=F32
            )
            scores = lax.dot_general(
                keys, keys, (((1,), (1,)), ((), ())), preferred_element_type=F32
            )
            scores = jnp.where(query == key, -100000.0, scores * scale)
            scores = jnp.where((same > 0.5) & (key <= query), scores, -1e30)
            row_max = jnp.max(scores, axis=1, keepdims=True)
            weights = jnp.exp(scores - row_max)
            total = jnp.sum(weights, axis=1, keepdims=True)
            probabilities = (weights / total).astype(BF16)
            result = jnp.dot(probabilities, values, preferred_element_type=F32).astype(BF16)
            out_ref[:, here, :] = result.reshape(sources, capacity, head_dim)

    return vmem_call(
        kernel, jax.ShapeDtypeStruct((sources, rows, head_dim), BF16), (False, False)
    )(blocks, members)


def unpack(returned, slot_col, capacity):
    owners, height, head_dim = returned.shape
    rows, heads = slot_col.shape
    slots = owners * capacity

    def kernel(block_ref, slot_ref, out_ref):
        for h in range(heads):
            block = block_ref[:, h * capacity : (h + 1) * capacity, :].reshape(slots, head_dim)
            place = slot_ref[:, h : h + 1] == iota((rows, slots), 1)
            out_ref[:, h * head_dim : (h + 1) * head_dim] = jnp.dot(
                place.astype(BF16), block, preferred_element_type=F32
            ).astype(BF16)

    return vmem_call(
        kernel, jax.ShapeDtypeStruct((rows, heads * head_dim), BF16), (False, False)
    )(returned, slot_col)


CLU = ("zq", "zr")


def shifted(block, step, axis):
    size = lax.axis_size(axis)
    return lax.ppermute(block, axis, [(i, (i + step) % size) for i in range(size)])


def body(tokens, proj_weight, clusters):
    rows, depth = tokens.shape[1:]
    owners = lax.axis_size(CLU)
    me = lax.axis_index(CLU)
    heads = clusters.shape[2]
    shard = proj_weight.shape[0]
    width = 2 * proj_weight.shape[2]
    head_dim = proj_weight.shape[2] // heads
    capacity = 2 * rows // owners
    chips = lax.axis_size("x")

    pieces = cut_tokens(tokens[0], lax.axis_index("core"), chips)
    ids = clusters[0].T.astype(BF16).reshape(-1, 128)
    ids = jnp.pad(ids, ((0, shard - ids.shape[0]), (0, 0)))
    own = jnp.concatenate([proj_weight.reshape(shard, width), ids], axis=1)
    own, pieces = lax.optimization_barrier((own, pieces))
    pieces = lax.all_to_all(pieces, "x", split_axis=0, concat_axis=0, tiled=True)

    four = lax.all_gather(own, "zq", axis=0)
    below = shifted(four, 1, CLU)
    above = shifted(four, -1, CLU)
    low = shifted(four[:2], 2, CLU)
    later, pieces = lax.optimization_barrier((four[2:], pieces))
    high = shifted(later, -2, CLU)
    parts = [four, below, above, low, high]
    ring = assemble(parts, [(0, 0), (3, 0), (1, 0), (2, 0), (2, 2)], me, width)
    slot_row, slot_col = routing(clusters[0], owners, capacity)
    ring, slot_row = lax.optimization_barrier((ring, slot_row))
    other = lax.ppermute(ring, "core", [(0, 1), (1, 0)])
    steps = (2, 1, -1, 0)
    *sent, kept = project(pieces, ring, other, lax.axis_index("x"), steps)
    received, ready = exchange_x(sent, steps[:-1])
    outgoing = pack(
        kept, received, ready, slot_row, lax.axis_index("core"), owners, capacity, head_dim
    )
    incoming = lax.all_to_all(outgoing, CLU, split_axis=0, concat_axis=0, tiled=True)

    by_class = jnp.stack(
        [part[:, :16, width:] for part in (four, above, jnp.concatenate([low, high]), below)]
    )
    by_class = jnp.roll(by_class, lax.axis_index("zr"), axis=0)
    all_ids = by_class.transpose(1, 0, 2, 3).reshape((owners,) + by_class.shape[2:])
    members = owned_members(all_ids, me, heads, capacity)
    replies = attend(incoming, members, capacity)
    returned = lax.all_to_all(replies, CLU, split_axis=0, concat_axis=0, tiled=True)
    return unpack(returned, slot_col, capacity)[None]


def solution(mesh):
    ctx, clu, tp = (mesh.shape[name] for name in mesh.axis_names)
    fine = jax.sharding.Mesh(
        mesh.devices.reshape(ctx // 2, 2, clu // 4, 4, tp), ("x", "core") + CLU + ("tp",)
    )
    ctx_axes = ("x", "core")
    return jax.shard_map(
        body,
        mesh=fine,
        in_specs=(
            P(ctx_axes, CLU, None),
            P(ctx_axes + CLU, None, "tp"),
            P(ctx_axes, CLU, "tp"),
        ),
        out_specs=P(ctx_axes, CLU, "tp"),
        check_vma=False,
    )
```

```python
import jax
import jax.numpy as jnp
from jax import lax
from jax.experimental import pallas as pl
from jax.experimental.pallas import tpu as pltpu
from jax.sharding import PartitionSpec as P

CLUSTERS = 64
BF16 = jnp.bfloat16
F32 = jnp.float32
VMEM_LIMIT = 48 * 1024 * 1024
CUT_LIMIT = 62 * 1024 * 1024


def vmem_call(kernel, out_shape, in_smem, **kwargs):
    vmem = pl.BlockSpec(memory_space=pltpu.VMEM)
    smem = pl.BlockSpec(memory_space=pltpu.SMEM)
    return pl.pallas_call(
        kernel,
        out_shape=out_shape,
        in_specs=[smem if flag else vmem for flag in in_smem],
        out_specs=jax.tree.map(lambda _: vmem, out_shape),
        compiler_params=pltpu.CompilerParams(vmem_limit_bytes=VMEM_LIMIT),
        **kwargs,
    )


def scalar(value):
    return jnp.reshape(value, (1,)).astype(jnp.int32)


def iota(shape, dim):
    return lax.broadcasted_iota(jnp.int32, shape, dim)


def routing(ids, owners, capacity):
    rows, heads = ids.shape
    per_owner = CLUSTERS // owners

    def kernel(ids_ref, ids_t_ref, slot_row_ref, slot_col_ref):
        before_col = (iota((rows, rows), 1) < iota((rows, rows), 0)).astype(BF16)
        before_row = (iota((rows, rows), 0) < iota((rows, rows), 1)).astype(BF16)
        for h in range(heads):
            owner_col = ids_ref[:, h : h + 1] // per_owner
            hot = owner_col == iota((rows, owners), 1)
            count = jnp.dot(before_col, hot.astype(BF16), preferred_element_type=F32)
            rank = jnp.sum(jnp.where(hot, count, 0.0), axis=1, keepdims=True)
            slot_col_ref[:, h : h + 1] = owner_col * capacity + rank.astype(jnp.int32)
            owner_row = ids_t_ref[h : h + 1, :] // per_owner
            hot = owner_row == iota((owners, rows), 0)
            count = jnp.dot(hot.astype(BF16), before_row, preferred_element_type=F32)
            rank = jnp.sum(jnp.where(hot, count, 0.0), axis=0, keepdims=True)
            slot_row_ref[h : h + 1, :] = owner_row * capacity + rank.astype(jnp.int32)

    return vmem_call(
        kernel,
        (
            jax.ShapeDtypeStruct((heads, rows), jnp.int32),
            jax.ShapeDtypeStruct((rows, heads), jnp.int32),
        ),
        (False, False),
    )(ids, ids.T)


def owned_members(all_ids, me, heads, capacity):
    sources, id_rows, lanes = all_ids.shape
    rows = sources * capacity // 2
    per_head = rows // lanes
    per_owner = CLUSTERS // sources
    slots = sources * capacity

    def kernel(me_ref, ids_ref, out_ref):
        before = (iota((rows, rows), 0) < iota((rows, rows), 1)).astype(BF16)
        place = iota((sources, capacity, rows), 1)
        kinds = iota((16, slots), 0) + 1
        column = iota((slots, lanes), 1)
        tags = jnp.zeros((slots, lanes), jnp.int32)
        for h in range(heads):
            ids = jnp.concatenate(
                [ids_ref[:, h * per_head + j, :] for j in range(per_head)], axis=1
            )
            ids = ids.astype(F32).astype(jnp.int32)
            owner = ids // per_owner
            mine = owner == me_ref[0]
            rank = jnp.dot(mine.astype(BF16), before, preferred_element_type=F32)
            rank = jnp.where(mine, rank.astype(jnp.int32), -1)
            tag = ids - owner * per_owner + 1
            placed = jnp.where(rank[:, None, :] == place, tag[:, None, :], 0)
            tag = jnp.sum(placed.reshape(slots, rows), axis=1, keepdims=True)
            tags = jnp.where(column == h, tag, tags)
        same_slot = (iota((slots, slots), 0) == iota((slots, slots), 1)).astype(BF16)
        tags = lax.dot_general(
            tags.astype(BF16), same_slot, (((0,), (0,)), ((), ())), preferred_element_type=F32
        ).astype(jnp.int32)
        for h in range(heads):
            out_ref[h] = (tags[h : h + 1, :] == kinds).astype(BF16)

    return vmem_call(kernel, jax.ShapeDtypeStruct((heads, 16, slots), BF16), (True, False))(
        scalar(me), all_ids
    )


def cut_tokens(local_rows, core, chips):
    rows, depth = local_rows.shape
    half = depth // chips // 2

    def kernel(core_ref, in_ref, out_ref, block_ref, in_sems, out_sems):
        blocks = [(p, j) for p in range(chips) for j in range(2)]
        reads, writes = [], []
        for i, (p, j) in enumerate(blocks):
            first = (2 * p + lax.rem(core_ref[0] + j, 2)) * half
            reads.append(
                pltpu.make_async_copy(
                    in_ref.at[:, pl.ds(pl.multiple_of(first, half), half)],
                    block_ref.at[i],
                    in_sems.at[i],
                )
            )
            writes.append(
                pltpu.make_async_copy(
                    block_ref.at[i], out_ref.at[p, :, j * half : (j + 1) * half], out_sems.at[i]
                )
            )
        for read in reads:
            read.start()
        for read, write in zip(reads, writes):
            read.wait()
            write.start()
        for write in writes:
            write.wait()

    return pl.pallas_call(
        kernel,
        out_shape=jax.ShapeDtypeStruct((chips, rows, 2 * half), BF16),
        in_specs=[
            pl.BlockSpec(memory_space=pltpu.SMEM),
            pl.BlockSpec(memory_space=pl.ANY),
        ],
        out_specs=pl.BlockSpec(memory_space=pl.ANY),
        scratch_shapes=[
            pltpu.VMEM((2 * chips, rows, half), BF16),
            pltpu.SemaphoreType.DMA((2 * chips,)),
            pltpu.SemaphoreType.DMA((2 * chips,)),
        ],
        compiler_params=pltpu.CompilerParams(vmem_limit_bytes=CUT_LIMIT),
    )(scalar(core), local_rows)


def assemble(parts, places, me, width):
    shard = parts[0].shape[1]
    count = sum(part.shape[0] for part in parts)
    classes = 4

    def kernel(me_ref, *refs):
        out_ref = refs[-1]
        for ref, (kind, first) in zip(refs, places):
            device = lax.rem(me_ref[0] + kind, classes) + classes * first
            for j in range(ref.shape[0]):
                at = pl.multiple_of((device + classes * j) * shard, shard)
                out_ref[pl.ds(at, shard), :] = ref[j, :, :width]

    return vmem_call(
        kernel,
        jax.ShapeDtypeStruct((count * shard, width), BF16),
        (True,) + (False,) * len(parts),
    )(scalar(me), *parts)


def project(pieces, ring, other, x, steps):
    chips, rows, depth = pieces.shape
    half, width = ring.shape

    def kernel(x_ref, pieces_ref, ring_ref, other_ref, *out_refs):
        for step, out_ref in zip(steps, out_refs):
            p = lax.rem(x_ref[0] + step + chips, chips)
            total = jnp.dot(pieces_ref[p, :, :half], ring_ref[...], preferred_element_type=F32)
            total += jnp.dot(pieces_ref[p, :, half:], other_ref[...], preferred_element_type=F32)
            out_ref[...] = total.astype(BF16)

    return vmem_call(
        kernel,
        (jax.ShapeDtypeStruct((rows, width), BF16),) * len(steps),
        (True, False, False, False),
    )(scalar(x), pieces, ring, other)


def exchange_x(parts, steps):
    chips = lax.axis_size("x")
    received = []
    for core in (1, 0):
        for i, step in enumerate(steps):
            pairs = [(2 * x + core, (x + step) % chips * 2 + core) for x in range(chips)]
            received.append(lax.ppermute(parts[i], ("x", "core"), pairs))
        if core == 1:
            ready = lax.ppermute(received[0][:16, :128], "core", [(1, 0)])
            parts, ready = lax.optimization_barrier((parts, ready))
    return received, ready


def pack(own, received, ready, slot_row, core, owners, capacity, head_dim):
    rows, width = own.shape
    heads = slot_row.shape[0]
    slots = owners * capacity
    count = len(received) // 2

    def kernel(core_ref, own_ref, *refs):
        slot_ref, _, out_ref = refs[-3:]

        def place_sums(part_refs):
            for h in range(heads):
                place = iota((slots, rows), 0) == slot_ref[h : h + 1, :]
                place = place.astype(BF16)
                for m in range(2):
                    cols = slice((m * heads + h) * head_dim, (m * heads + h + 1) * head_dim)
                    total = own_ref[:, cols].astype(F32)
                    for ref in part_refs:
                        total += ref[:, cols].astype(F32)
                    packed = jnp.dot(
                        place, total.astype(BF16), preferred_element_type=F32
                    ).astype(BF16)
                    out_ref[
                        :, h * capacity : (h + 1) * capacity, m * head_dim : (m + 1) * head_dim
                    ] = packed.reshape(owners, capacity, head_dim)

        @pl.when(core_ref[0] == 1)
        def _():
            place_sums(refs[:count])

        @pl.when(core_ref[0] == 0)
        def _():
            place_sums(refs[count : 2 * count])

    return vmem_call(
        kernel,
        jax.ShapeDtypeStruct((owners, heads * capacity, 2 * head_dim), BF16),
        (True,) + (False,) * (len(received) + 3),
    )(scalar(core), own, *received, slot_row, ready)


def attend(blocks, members, capacity):
    sources, rows, width = blocks.shape
    head_dim = width // 2
    heads = rows // capacity
    slots = sources * capacity
    scale = head_dim ** (-0.5)

    def kernel(block_ref, member_ref, out_ref):
        query = iota((slots, slots), 0)
        key = iota((slots, slots), 1)
        for h in range(heads):
            here = slice(h * capacity, (h + 1) * capacity)
            keys = block_ref[:, here, :head_dim].reshape(slots, head_dim)
            values = block_ref[:, here, head_dim:].reshape(slots, head_dim)
            member = member_ref[h]
            same = lax.dot_general(
                member, member, (((0,), (0,)), ((), ())), preferred_element_type=F32
            )
            scores = lax.dot_general(
                keys, keys, (((1,), (1,)), ((), ())), preferred_element_type=F32
            )
            scores = jnp.where(query == key, -100000.0, scores * scale)
            scores = jnp.where((same > 0.5) & (key <= query), scores, -1e30)
            row_max = jnp.max(scores, axis=1, keepdims=True)
            weights = jnp.exp(scores - row_max)
            total = jnp.sum(weights, axis=1, keepdims=True)
            probabilities = (weights / total).astype(BF16)
            result = jnp.dot(probabilities, values, preferred_element_type=F32).astype(BF16)
            out_ref[:, here, :] = result.reshape(sources, capacity, head_dim)

    return vmem_call(
        kernel, jax.ShapeDtypeStruct((sources, rows, head_dim), BF16), (False, False)
    )(blocks, members)


def unpack(returned, slot_col, capacity):
    owners, height, head_dim = returned.shape
    rows, heads = slot_col.shape
    slots = owners * capacity

    def kernel(block_ref, slot_ref, out_ref):
        for h in range(heads):
            block = block_ref[:, h * capacity : (h + 1) * capacity, :].reshape(slots, head_dim)
            place = slot_ref[:, h : h + 1] == iota((rows, slots), 1)
            out_ref[:, h * head_dim : (h + 1) * head_dim] = jnp.dot(
                place.astype(BF16), block, preferred_element_type=F32
            ).astype(BF16)

    return vmem_call(
        kernel, jax.ShapeDtypeStruct((rows, heads * head_dim), BF16), (False, False)
    )(returned, slot_col)


CLU = ("zq", "zr")


def shifted(block, step, axis):
    size = lax.axis_size(axis)
    return lax.ppermute(block, axis, [(i, (i + step) % size) for i in range(size)])


def body(tokens, proj_weight, clusters):
    rows, depth = tokens.shape[1:]
    owners = lax.axis_size(CLU)
    me = lax.axis_index(CLU)
    heads = clusters.shape[2]
    shard = proj_weight.shape[0]
    width = 2 * proj_weight.shape[2]
    head_dim = proj_weight.shape[2] // heads
    capacity = 2 * rows // owners
    chips = lax.axis_size("x")

    pieces = cut_tokens(tokens[0], lax.axis_index("core"), chips)
    ids = clusters[0].T.astype(BF16).reshape(-1, 128)
    ids = jnp.pad(ids, ((0, shard - ids.shape[0]), (0, 0)))
    own = jnp.concatenate([proj_weight.reshape(shard, width), ids], axis=1)
    own, pieces = lax.optimization_barrier((own, pieces))
    pieces = lax.all_to_all(pieces, "x", split_axis=0, concat_axis=0, tiled=True)

    four = lax.all_gather(own, "zq", axis=0)
    below = shifted(four, 1, CLU)
    above = shifted(four, -1, CLU)
    low = shifted(four[:2], 2, CLU)
    later, pieces = lax.optimization_barrier((four[2:], pieces))
    high = shifted(later, -2, CLU)
    parts = [four, below, above, low, high]
    ring = assemble(parts, [(0, 0), (3, 0), (1, 0), (2, 0), (2, 2)], me, width)
    slot_row, slot_col = routing(clusters[0], owners, capacity)
    ring, slot_row = lax.optimization_barrier((ring, slot_row))
    other = lax.ppermute(ring, "core", [(0, 1), (1, 0)])
    steps = (2, 1, -1, 0)
    *sent, kept = project(pieces, ring, other, lax.axis_index("x"), steps)
    received, ready = exchange_x(sent, steps[:-1])
    outgoing = pack(
        kept, received, ready, slot_row, lax.axis_index("core"), owners, capacity, head_dim
    )
    incoming = lax.all_to_all(outgoing, CLU, split_axis=0, concat_axis=0, tiled=True)

    by_class = jnp.stack(
        [part[:, :16, width:] for part in (four, above, jnp.concatenate([low, high]), below)]
    )
    by_class = jnp.roll(by_class, lax.axis_index("zr"), axis=0)
    all_ids = by_class.transpose(1, 0, 2, 3).reshape((owners,) + by_class.shape[2:])
    members = owned_members(all_ids, me, heads, capacity)
    replies = attend(incoming, members, capacity)
    returned = lax.all_to_all(replies, CLU, split_axis=0, concat_axis=0, tiled=True)
    return unpack(returned, slot_col, capacity)[None]


def solution(mesh):
    ctx, clu, tp = (mesh.shape[name] for name in mesh.axis_names)
    fine = jax.sharding.Mesh(
        mesh.devices.reshape(ctx // 2, 2, clu // 4, 4, tp), ("x", "core") + CLU + ("tp",)
    )
    ctx_axes = ("x", "core")
    return jax.shard_map(
        body,
        mesh=fine,
        in_specs=(
            P(ctx_axes, CLU, None),
            P(ctx_axes + CLU, None, "tp"),
            P(ctx_axes, CLU, "tp"),
        ),
        out_specs=P(ctx_axes, CLU, "tp"),
        check_vma=False,
    )
```

```python
import jax
import jax.numpy as jnp
from jax import lax
from jax.experimental import pallas as pl
from jax.experimental.pallas import tpu as pltpu
from jax.sharding import PartitionSpec as P

CLUSTERS = 64
BF16 = jnp.bfloat16
F32 = jnp.float32
VMEM_LIMIT = 48 * 1024 * 1024
CUT_LIMIT = 62 * 1024 * 1024


def vmem_call(kernel, out_shape, in_smem, **kwargs):
    vmem = pl.BlockSpec(memory_space=pltpu.VMEM)
    smem = pl.BlockSpec(memory_space=pltpu.SMEM)
    return pl.pallas_call(
        kernel,
        out_shape=out_shape,
        in_specs=[smem if flag else vmem for flag in in_smem],
        out_specs=jax.tree.map(lambda _: vmem, out_shape),
        compiler_params=pltpu.CompilerParams(vmem_limit_bytes=VMEM_LIMIT),
        **kwargs,
    )


def scalar(value):
    return jnp.reshape(value, (1,)).astype(jnp.int32)


def iota(shape, dim):
    return lax.broadcasted_iota(jnp.int32, shape, dim)


def routing(ids, owners, capacity):
    rows, heads = ids.shape
    per_owner = CLUSTERS // owners

    def kernel(ids_ref, ids_t_ref, slot_row_ref, slot_col_ref):
        before_col = (iota((rows, rows), 1) < iota((rows, rows), 0)).astype(BF16)
        before_row = (iota((rows, rows), 0) < iota((rows, rows), 1)).astype(BF16)
        for h in range(heads):
            owner_col = ids_ref[:, h : h + 1] // per_owner
            hot = owner_col == iota((rows, owners), 1)
            count = jnp.dot(before_col, hot.astype(BF16), preferred_element_type=F32)
            rank = jnp.sum(jnp.where(hot, count, 0.0), axis=1, keepdims=True)
            slot_col_ref[:, h : h + 1] = owner_col * capacity + rank.astype(jnp.int32)
            owner_row = ids_t_ref[h : h + 1, :] // per_owner
            hot = owner_row == iota((owners, rows), 0)
            count = jnp.dot(hot.astype(BF16), before_row, preferred_element_type=F32)
            rank = jnp.sum(jnp.where(hot, count, 0.0), axis=0, keepdims=True)
            slot_row_ref[h : h + 1, :] = owner_row * capacity + rank.astype(jnp.int32)

    return vmem_call(
        kernel,
        (
            jax.ShapeDtypeStruct((heads, rows), jnp.int32),
            jax.ShapeDtypeStruct((rows, heads), jnp.int32),
        ),
        (False, False),
    )(ids, ids.T)


def owned_members(all_ids, me, heads, capacity):
    sources, id_rows, lanes = all_ids.shape
    rows = sources * capacity // 2
    per_head = rows // lanes
    per_owner = CLUSTERS // sources
    slots = sources * capacity

    def kernel(me_ref, ids_ref, out_ref):
        before = (iota((rows, rows), 0) < iota((rows, rows), 1)).astype(BF16)
        place = iota((sources, capacity, rows), 1)
        kinds = iota((16, slots), 0) + 1
        column = iota((slots, lanes), 1)
        tags = jnp.zeros((slots, lanes), jnp.int32)
        for h in range(heads):
            ids = jnp.concatenate(
                [ids_ref[:, h * per_head + j, :] for j in range(per_head)], axis=1
            )
            ids = ids.astype(F32).astype(jnp.int32)
            owner = ids // per_owner
            mine = owner == me_ref[0]
            rank = jnp.dot(mine.astype(BF16), before, preferred_element_type=F32)
            rank = jnp.where(mine, rank.astype(jnp.int32), -1)
            tag = ids - owner * per_owner + 1
            placed = jnp.where(rank[:, None, :] == place, tag[:, None, :], 0)
            tag = jnp.sum(placed.reshape(slots, rows), axis=1, keepdims=True)
            tags = jnp.where(column == h, tag, tags)
        same_slot = (iota((slots, slots), 0) == iota((slots, slots), 1)).astype(BF16)
        tags = lax.dot_general(
            tags.astype(BF16), same_slot, (((0,), (0,)), ((), ())), preferred_element_type=F32
        ).astype(jnp.int32)
        for h in range(heads):
            out_ref[h] = (tags[h : h + 1, :] == kinds).astype(BF16)

    return vmem_call(kernel, jax.ShapeDtypeStruct((heads, 16, slots), BF16), (True, False))(
        scalar(me), all_ids
    )


def cut_tokens(local_rows, core, chips):
    rows, depth = local_rows.shape
    half = depth // chips // 2

    def kernel(core_ref, in_ref, out_ref, block_ref, in_sems, out_sems):
        blocks = [(p, j) for p in range(chips) for j in range(2)]
        reads, writes = [], []
        for i, (p, j) in enumerate(blocks):
            first = (2 * p + lax.rem(core_ref[0] + j, 2)) * half
            reads.append(
                pltpu.make_async_copy(
                    in_ref.at[:, pl.ds(pl.multiple_of(first, half), half)],
                    block_ref.at[i],
                    in_sems.at[i],
                )
            )
            writes.append(
                pltpu.make_async_copy(
                    block_ref.at[i], out_ref.at[p, :, j * half : (j + 1) * half], out_sems.at[i]
                )
            )
        for read in reads:
            read.start()
        for read, write in zip(reads, writes):
            read.wait()
            write.start()
        for write in writes:
            write.wait()

    return pl.pallas_call(
        kernel,
        out_shape=jax.ShapeDtypeStruct((chips, rows, 2 * half), BF16),
        in_specs=[
            pl.BlockSpec(memory_space=pltpu.SMEM),
            pl.BlockSpec(memory_space=pl.ANY),
        ],
        out_specs=pl.BlockSpec(memory_space=pl.ANY),
        scratch_shapes=[
            pltpu.VMEM((2 * chips, rows, half), BF16),
            pltpu.SemaphoreType.DMA((2 * chips,)),
            pltpu.SemaphoreType.DMA((2 * chips,)),
        ],
        compiler_params=pltpu.CompilerParams(vmem_limit_bytes=CUT_LIMIT),
    )(scalar(core), local_rows)


def assemble(parts, places, me, width):
    shard = parts[0].shape[1]
    count = sum(part.shape[0] for part in parts)
    classes = 4

    def kernel(me_ref, *refs):
        out_ref = refs[-1]
        for ref, (kind, first) in zip(refs, places):
            device = lax.rem(me_ref[0] + kind, classes) + classes * first
            for j in range(ref.shape[0]):
                at = pl.multiple_of((device + classes * j) * shard, shard)
                out_ref[pl.ds(at, shard), :] = ref[j, :, :width]

    return vmem_call(
        kernel,
        jax.ShapeDtypeStruct((count * shard, width), BF16),
        (True,) + (False,) * len(parts),
    )(scalar(me), *parts)


def project(pieces, ring, other, x, steps):
    chips, rows, depth = pieces.shape
    half, width = ring.shape

    def kernel(x_ref, pieces_ref, ring_ref, other_ref, *out_refs):
        for step, out_ref in zip(steps, out_refs):
            p = lax.rem(x_ref[0] + step + chips, chips)
            total = jnp.dot(pieces_ref[p, :, :half], ring_ref[...], preferred_element_type=F32)
            total += jnp.dot(pieces_ref[p, :, half:], other_ref[...], preferred_element_type=F32)
            out_ref[...] = total.astype(BF16)

    return vmem_call(
        kernel,
        (jax.ShapeDtypeStruct((rows, width), BF16),) * len(steps),
        (True, False, False, False),
    )(scalar(x), pieces, ring, other)


def exchange_x(parts, steps):
    chips = lax.axis_size("x")
    received = []
    for core in (1, 0):
        for i, step in enumerate(steps):
            pairs = [(2 * x + core, (x + step) % chips * 2 + core) for x in range(chips)]
            received.append(lax.ppermute(parts[i], ("x", "core"), pairs))
        if core == 1:
            ready = sum(part[:16, :128] for part in received)
            ready = lax.ppermute(ready, "core", [(1, 0)])
            parts, ready = lax.optimization_barrier((parts, ready))
    return received, ready


def pack(own, received, ready, slot_row, core, owners, capacity, head_dim):
    rows, width = own.shape
    heads = slot_row.shape[0]
    slots = owners * capacity
    count = len(received) // 2

    def kernel(core_ref, slot_ref, own_ref, *refs):
        out_ref, part_ref, sems = refs[-3:]

        def copies(part_refs):
            return [
                pltpu.make_async_copy(ref, part_ref.at[i], sems.at[i])
                for i, ref in enumerate((own_ref,) + part_refs)
            ]

        for number, first in ((1, 0), (0, count)):

            @pl.when(core_ref[0] == number)
            def _():
                for copy in copies(refs[first : first + count]):
                    copy.start()
                for copy in copies(refs[first : first + count]):
                    copy.wait()

        for h in range(heads):
            place = iota((slots, rows), 0) == slot_ref[h : h + 1, :]
            place = place.astype(BF16)
            for m in range(2):
                cols = slice((m * heads + h) * head_dim, (m * heads + h + 1) * head_dim)
                total = part_ref[0, :, cols].astype(F32)
                for i in range(1, count + 1):
                    total += part_ref[i, :, cols].astype(F32)
                packed = jnp.dot(
                    place, total.astype(BF16), preferred_element_type=F32
                ).astype(BF16)
                out_ref[
                    :, h * capacity : (h + 1) * capacity, m * head_dim : (m + 1) * head_dim
                ] = packed.reshape(owners, capacity, head_dim)

    vmem = pl.BlockSpec(memory_space=pltpu.VMEM)
    whole = pl.BlockSpec(memory_space=pl.ANY)
    return pl.pallas_call(
        kernel,
        out_shape=jax.ShapeDtypeStruct((owners, heads * capacity, 2 * head_dim), BF16),
        in_specs=[pl.BlockSpec(memory_space=pltpu.SMEM), vmem] + [whole] * (len(received) + 2),
        out_specs=vmem,
        scratch_shapes=[
            pltpu.VMEM((count + 1, rows, width), BF16),
            pltpu.SemaphoreType.DMA((count + 1,)),
        ],
        compiler_params=pltpu.CompilerParams(vmem_limit_bytes=VMEM_LIMIT),
    )(scalar(core), slot_row, own, *received, ready)


def attend(blocks, members, capacity):
    sources, rows, width = blocks.shape
    head_dim = width // 2
    heads = rows // capacity
    slots = sources * capacity
    scale = head_dim ** (-0.5)

    def kernel(block_ref, member_ref, out_ref):
        query = iota((slots, slots), 0)
        key = iota((slots, slots), 1)
        for h in range(heads):
            here = slice(h * capacity, (h + 1) * capacity)
            keys = block_ref[:, here, :head_dim].reshape(slots, head_dim)
            values = block_ref[:, here, head_dim:].reshape(slots, head_dim)
            member = member_ref[h]
            same = lax.dot_general(
                member, member, (((0,), (0,)), ((), ())), preferred_element_type=F32
            )
            scores = lax.dot_general(
                keys, keys, (((1,), (1,)), ((), ())), preferred_element_type=F32
            )
            scores = jnp.where(query == key, -100000.0, scores * scale)
            scores = jnp.where((same > 0.5) & (key <= query), scores, -1e30)
            row_max = jnp.max(scores, axis=1, keepdims=True)
            weights = jnp.exp(scores - row_max)
            total = jnp.sum(weights, axis=1, keepdims=True)
            probabilities = (weights / total).astype(BF16)
            result = jnp.dot(probabilities, values, preferred_element_type=F32).astype(BF16)
            out_ref[:, here, :] = result.reshape(sources, capacity, head_dim)

    return vmem_call(
        kernel, jax.ShapeDtypeStruct((sources, rows, head_dim), BF16), (False, False)
    )(blocks, members)


def unpack(returned, slot_col, capacity):
    owners, height, head_dim = returned.shape
    rows, heads = slot_col.shape
    slots = owners * capacity

    def kernel(block_ref, slot_ref, out_ref):
        for h in range(heads):
            block = block_ref[:, h * capacity : (h + 1) * capacity, :].reshape(slots, head_dim)
            place = slot_ref[:, h : h + 1] == iota((rows, slots), 1)
            out_ref[:, h * head_dim : (h + 1) * head_dim] = jnp.dot(
                place.astype(BF16), block, preferred_element_type=F32
            ).astype(BF16)

    return vmem_call(
        kernel, jax.ShapeDtypeStruct((rows, heads * head_dim), BF16), (False, False)
    )(returned, slot_col)


CLU = ("zq", "zr")


def shifted(block, step, axis):
    size = lax.axis_size(axis)
    return lax.ppermute(block, axis, [(i, (i + step) % size) for i in range(size)])


def body(tokens, proj_weight, clusters):
    rows, depth = tokens.shape[1:]
    owners = lax.axis_size(CLU)
    me = lax.axis_index(CLU)
    heads = clusters.shape[2]
    shard = proj_weight.shape[0]
    width = 2 * proj_weight.shape[2]
    head_dim = proj_weight.shape[2] // heads
    capacity = 2 * rows // owners
    chips = lax.axis_size("x")

    pieces = cut_tokens(tokens[0], lax.axis_index("core"), chips)
    ids = clusters[0].T.astype(BF16).reshape(-1, 128)
    ids = jnp.pad(ids, ((0, shard - ids.shape[0]), (0, 0)))
    own = jnp.concatenate([proj_weight.reshape(shard, width), ids], axis=1)
    own, pieces = lax.optimization_barrier((own, pieces))
    pieces = lax.all_to_all(pieces, "x", split_axis=0, concat_axis=0, tiled=True)

    four = lax.all_gather(own, "zq", axis=0)
    below = shifted(four, 1, CLU)
    above = shifted(four, -1, CLU)
    low = shifted(four[:2], 2, CLU)
    later, pieces = lax.optimization_barrier((four[2:], pieces))
    high = shifted(later, -2, CLU)
    parts = [four, below, above, low, high]
    ring = assemble(parts, [(0, 0), (3, 0), (1, 0), (2, 0), (2, 2)], me, width)
    slot_row, slot_col = routing(clusters[0], owners, capacity)
    ring, slot_row = lax.optimization_barrier((ring, slot_row))
    other = lax.ppermute(ring, "core", [(0, 1), (1, 0)])
    steps = (2, 1, -1, 0)
    *sent, kept = project(pieces, ring, other, lax.axis_index("x"), steps)
    received, ready = exchange_x(sent, steps[:-1])
    outgoing = pack(
        kept, received, ready, slot_row, lax.axis_index("core"), owners, capacity, head_dim
    )
    incoming = lax.all_to_all(outgoing, CLU, split_axis=0, concat_axis=0, tiled=True)

    by_class = jnp.stack(
        [part[:, :16, width:] for part in (four, above, jnp.concatenate([low, high]), below)]
    )
    by_class = jnp.roll(by_class, lax.axis_index("zr"), axis=0)
    all_ids = by_class.transpose(1, 0, 2, 3).reshape((owners,) + by_class.shape[2:])
    members = owned_members(all_ids, me, heads, capacity)
    replies = attend(incoming, members, capacity)
    returned = lax.all_to_all(replies, CLU, split_axis=0, concat_axis=0, tiled=True)
    return unpack(returned, slot_col, capacity)[None]


def solution(mesh):
    ctx, clu, tp = (mesh.shape[name] for name in mesh.axis_names)
    fine = jax.sharding.Mesh(
        mesh.devices.reshape(ctx // 2, 2, clu // 4, 4, tp), ("x", "core") + CLU + ("tp",)
    )
    ctx_axes = ("x", "core")
    return jax.shard_map(
        body,
        mesh=fine,
        in_specs=(
            P(ctx_axes, CLU, None),
            P(ctx_axes + CLU, None, "tp"),
            P(ctx_axes, CLU, "tp"),
        ),
        out_specs=P(ctx_axes, CLU, "tp"),
        check_vma=False,
    )
```

```python
import jax
import jax.numpy as jnp
from jax import lax
from jax.experimental import pallas as pl
from jax.experimental.pallas import tpu as pltpu
from jax.sharding import PartitionSpec as P

CLUSTERS = 64
BF16 = jnp.bfloat16
F32 = jnp.float32
VMEM_LIMIT = 48 * 1024 * 1024
CUT_LIMIT = 62 * 1024 * 1024


def vmem_call(kernel, out_shape, in_smem, **kwargs):
    vmem = pl.BlockSpec(memory_space=pltpu.VMEM)
    smem = pl.BlockSpec(memory_space=pltpu.SMEM)
    return pl.pallas_call(
        kernel,
        out_shape=out_shape,
        in_specs=[smem if flag else vmem for flag in in_smem],
        out_specs=jax.tree.map(lambda _: vmem, out_shape),
        compiler_params=pltpu.CompilerParams(vmem_limit_bytes=VMEM_LIMIT),
        **kwargs,
    )


def scalar(value):
    return jnp.reshape(value, (1,)).astype(jnp.int32)


def iota(shape, dim):
    return lax.broadcasted_iota(jnp.int32, shape, dim)


def routing(ids, owners, capacity):
    rows, heads = ids.shape
    per_owner = CLUSTERS // owners

    def kernel(ids_ref, ids_t_ref, slot_row_ref, slot_col_ref):
        before_col = (iota((rows, rows), 1) < iota((rows, rows), 0)).astype(BF16)
        before_row = (iota((rows, rows), 0) < iota((rows, rows), 1)).astype(BF16)
        for h in range(heads):
            owner_col = ids_ref[:, h : h + 1] // per_owner
            hot = owner_col == iota((rows, owners), 1)
            count = jnp.dot(before_col, hot.astype(BF16), preferred_element_type=F32)
            rank = jnp.sum(jnp.where(hot, count, 0.0), axis=1, keepdims=True)
            slot_col_ref[:, h : h + 1] = owner_col * capacity + rank.astype(jnp.int32)
            owner_row = ids_t_ref[h : h + 1, :] // per_owner
            hot = owner_row == iota((owners, rows), 0)
            count = jnp.dot(hot.astype(BF16), before_row, preferred_element_type=F32)
            rank = jnp.sum(jnp.where(hot, count, 0.0), axis=0, keepdims=True)
            slot_row_ref[h : h + 1, :] = owner_row * capacity + rank.astype(jnp.int32)

    return vmem_call(
        kernel,
        (
            jax.ShapeDtypeStruct((heads, rows), jnp.int32),
            jax.ShapeDtypeStruct((rows, heads), jnp.int32),
        ),
        (False, False),
    )(ids, ids.T)


def owned_members(all_ids, me, heads, capacity):
    sources, id_rows, lanes = all_ids.shape
    rows = sources * capacity // 2
    per_head = rows // lanes
    per_owner = CLUSTERS // sources
    slots = sources * capacity

    def kernel(me_ref, ids_ref, out_ref):
        before = (iota((rows, rows), 0) < iota((rows, rows), 1)).astype(BF16)
        place = iota((sources, capacity, rows), 1)
        kinds = iota((16, slots), 0) + 1
        column = iota((slots, lanes), 1)
        tags = jnp.zeros((slots, lanes), jnp.int32)
        for h in range(heads):
            ids = jnp.concatenate(
                [ids_ref[:, h * per_head + j, :] for j in range(per_head)], axis=1
            )
            ids = ids.astype(F32).astype(jnp.int32)
            owner = ids // per_owner
            mine = owner == me_ref[0]
            rank = jnp.dot(mine.astype(BF16), before, preferred_element_type=F32)
            rank = jnp.where(mine, rank.astype(jnp.int32), -1)
            tag = ids - owner * per_owner + 1
            placed = jnp.where(rank[:, None, :] == place, tag[:, None, :], 0)
            tag = jnp.sum(placed.reshape(slots, rows), axis=1, keepdims=True)
            tags = jnp.where(column == h, tag, tags)
        same_slot = (iota((slots, slots), 0) == iota((slots, slots), 1)).astype(BF16)
        tags = lax.dot_general(
            tags.astype(BF16), same_slot, (((0,), (0,)), ((), ())), preferred_element_type=F32
        ).astype(jnp.int32)
        for h in range(heads):
            out_ref[h] = (tags[h : h + 1, :] == kinds).astype(BF16)

    return vmem_call(kernel, jax.ShapeDtypeStruct((heads, 16, slots), BF16), (True, False))(
        scalar(me), all_ids
    )


def cut_tokens(local_rows, core, chips):
    rows, depth = local_rows.shape
    half = depth // chips // 2

    def kernel(core_ref, in_ref, out_ref, block_ref, in_sems, out_sems):
        blocks = [(p, j) for p in range(chips) for j in range(2)]
        reads, writes = [], []
        for i, (p, j) in enumerate(blocks):
            first = (2 * p + lax.rem(core_ref[0] + j, 2)) * half
            reads.append(
                pltpu.make_async_copy(
                    in_ref.at[:, pl.ds(pl.multiple_of(first, half), half)],
                    block_ref.at[i],
                    in_sems.at[i],
                )
            )
            writes.append(
                pltpu.make_async_copy(
                    block_ref.at[i], out_ref.at[p, :, j * half : (j + 1) * half], out_sems.at[i]
                )
            )
        for read in reads:
            read.start()
        for read, write in zip(reads, writes):
            read.wait()
            write.start()
        for write in writes:
            write.wait()

    return pl.pallas_call(
        kernel,
        out_shape=jax.ShapeDtypeStruct((chips, rows, 2 * half), BF16),
        in_specs=[
            pl.BlockSpec(memory_space=pltpu.SMEM),
            pl.BlockSpec(memory_space=pl.ANY),
        ],
        out_specs=pl.BlockSpec(memory_space=pl.ANY),
        scratch_shapes=[
            pltpu.VMEM((2 * chips, rows, half), BF16),
            pltpu.SemaphoreType.DMA((2 * chips,)),
            pltpu.SemaphoreType.DMA((2 * chips,)),
        ],
        compiler_params=pltpu.CompilerParams(vmem_limit_bytes=CUT_LIMIT),
    )(scalar(core), local_rows)


def assemble(parts, places, me, width):
    shard = parts[0].shape[1]
    count = sum(part.shape[0] for part in parts)
    classes = 4

    def kernel(me_ref, *refs):
        out_ref = refs[-1]
        for ref, (kind, first) in zip(refs, places):
            device = lax.rem(me_ref[0] + kind, classes) + classes * first
            for j in range(ref.shape[0]):
                at = pl.multiple_of((device + classes * j) * shard, shard)
                out_ref[pl.ds(at, shard), :] = ref[j, :, :width]

    return vmem_call(
        kernel,
        jax.ShapeDtypeStruct((count * shard, width), BF16),
        (True,) + (False,) * len(parts),
    )(scalar(me), *parts)


def project(pieces, ring, other, x, steps):
    chips, rows, depth = pieces.shape
    half, width = ring.shape

    def kernel(x_ref, pieces_ref, ring_ref, other_ref, *out_refs):
        for step, out_ref in zip(steps, out_refs):
            p = lax.rem(x_ref[0] + step + chips, chips)
            total = jnp.dot(pieces_ref[p, :, :half], ring_ref[...], preferred_element_type=F32)
            total += jnp.dot(pieces_ref[p, :, half:], other_ref[...], preferred_element_type=F32)
            out_ref[...] = total.astype(BF16)

    return vmem_call(
        kernel,
        (jax.ShapeDtypeStruct((rows, width), BF16),) * len(steps),
        (True, False, False, False),
    )(scalar(x), pieces, ring, other)


def exchange_x(parts, steps, both):
    chips = lax.axis_size("x")

    def send(part, step, cores):
        pairs = [
            (2 * x + core, (x + step) % chips * 2 + core) for x in range(chips) for core in cores
        ]
        return lax.ppermute(part, ("x", "core"), pairs)

    received = [[], []]
    for core in (1, 0):
        for i, step in enumerate(steps):
            if step != both:
                received[core].append(send(parts[i], step, (core,)))
        if core == 1:
            common = send(parts[steps.index(both)], both, (0, 1))
            ready = sum(part[:16, :128] for part in received[1] + [common])
            ready = lax.ppermute(ready, "core", [(1, 0)])
            parts, ready = lax.optimization_barrier((parts, ready))
    return common, received, ready


def pack(own, common, received, ready, slot_row, core, owners, capacity, head_dim):
    rows, width = own.shape
    heads = slot_row.shape[0]
    slots = owners * capacity
    count = len(received[0])
    total_count = count + 2

    def kernel(core_ref, slot_ref, own_ref, common_ref, *refs):
        out_ref, part_ref, sems = refs[-3:]

        def copies(part_refs):
            return [
                pltpu.make_async_copy(ref, part_ref.at[i], sems.at[i])
                for i, ref in enumerate((own_ref, common_ref) + part_refs)
            ]

        for number, first in ((0, 0), (1, count)):

            @pl.when(core_ref[0] == number)
            def _():
                for copy in copies(refs[first : first + count]):
                    copy.start()
                for copy in copies(refs[first : first + count]):
                    copy.wait()

        for h in range(heads):
            place = iota((slots, rows), 0) == slot_ref[h : h + 1, :]
            place = place.astype(BF16)
            for m in range(2):
                cols = slice((m * heads + h) * head_dim, (m * heads + h + 1) * head_dim)
                total = part_ref[0, :, cols].astype(F32)
                for i in range(1, total_count):
                    total += part_ref[i, :, cols].astype(F32)
                packed = jnp.dot(
                    place, total.astype(BF16), preferred_element_type=F32
                ).astype(BF16)
                out_ref[
                    :, h * capacity : (h + 1) * capacity, m * head_dim : (m + 1) * head_dim
                ] = packed.reshape(owners, capacity, head_dim)

    vmem = pl.BlockSpec(memory_space=pltpu.VMEM)
    whole = pl.BlockSpec(memory_space=pl.ANY)
    return pl.pallas_call(
        kernel,
        out_shape=jax.ShapeDtypeStruct((owners, heads * capacity, 2 * head_dim), BF16),
        in_specs=[pl.BlockSpec(memory_space=pltpu.SMEM), vmem] + [whole] * (2 * count + 3),
        out_specs=vmem,
        scratch_shapes=[
            pltpu.VMEM((total_count, rows, width), BF16),
            pltpu.SemaphoreType.DMA((total_count,)),
        ],
        compiler_params=pltpu.CompilerParams(vmem_limit_bytes=VMEM_LIMIT),
    )(scalar(core), slot_row, own, common, *received[0], *received[1], ready)


def attend(blocks, members, capacity):
    sources, rows, width = blocks.shape
    head_dim = width // 2
    heads = rows // capacity
    slots = sources * capacity
    scale = head_dim ** (-0.5)

    def kernel(block_ref, member_ref, out_ref):
        query = iota((slots, slots), 0)
        key = iota((slots, slots), 1)
        for h in range(heads):
            here = slice(h * capacity, (h + 1) * capacity)
            keys = block_ref[:, here, :head_dim].reshape(slots, head_dim)
            values = block_ref[:, here, head_dim:].reshape(slots, head_dim)
            member = member_ref[h]
            same = lax.dot_general(
                member, member, (((0,), (0,)), ((), ())), preferred_element_type=F32
            )
            scores = lax.dot_general(
                keys, keys, (((1,), (1,)), ((), ())), preferred_element_type=F32
            )
            scores = jnp.where(query == key, -100000.0, scores * scale)
            scores = jnp.where((same > 0.5) & (key <= query), scores, -1e30)
            row_max = jnp.max(scores, axis=1, keepdims=True)
            weights = jnp.exp(scores - row_max)
            total = jnp.sum(weights, axis=1, keepdims=True)
            probabilities = (weights / total).astype(BF16)
            result = jnp.dot(probabilities, values, preferred_element_type=F32).astype(BF16)
            out_ref[:, here, :] = result.reshape(sources, capacity, head_dim)

    return vmem_call(
        kernel, jax.ShapeDtypeStruct((sources, rows, head_dim), BF16), (False, False)
    )(blocks, members)


def unpack(returned, slot_col, capacity):
    owners, height, head_dim = returned.shape
    rows, heads = slot_col.shape
    slots = owners * capacity

    def kernel(block_ref, slot_ref, out_ref):
        for h in range(heads):
            block = block_ref[:, h * capacity : (h + 1) * capacity, :].reshape(slots, head_dim)
            place = slot_ref[:, h : h + 1] == iota((rows, slots), 1)
            out_ref[:, h * head_dim : (h + 1) * head_dim] = jnp.dot(
                place.astype(BF16), block, preferred_element_type=F32
            ).astype(BF16)

    return vmem_call(
        kernel, jax.ShapeDtypeStruct((rows, heads * head_dim), BF16), (False, False)
    )(returned, slot_col)


CLU = ("zq", "zr")


def shifted(block, step, axis):
    size = lax.axis_size(axis)
    return lax.ppermute(block, axis, [(i, (i + step) % size) for i in range(size)])


def body(tokens, proj_weight, clusters):
    rows, depth = tokens.shape[1:]
    owners = lax.axis_size(CLU)
    me = lax.axis_index(CLU)
    heads = clusters.shape[2]
    shard = proj_weight.shape[0]
    width = 2 * proj_weight.shape[2]
    head_dim = proj_weight.shape[2] // heads
    capacity = 2 * rows // owners
    chips = lax.axis_size("x")

    pieces = cut_tokens(tokens[0], lax.axis_index("core"), chips)
    ids = clusters[0].T.astype(BF16).reshape(-1, 128)
    ids = jnp.pad(ids, ((0, shard - ids.shape[0]), (0, 0)))
    own = jnp.concatenate([proj_weight.reshape(shard, width), ids], axis=1)
    own, pieces = lax.optimization_barrier((own, pieces))
    pieces = lax.all_to_all(pieces, "x", split_axis=0, concat_axis=0, tiled=True)

    four = lax.all_gather(own, "zq", axis=0)
    below = shifted(four, 1, CLU)
    above = shifted(four, -1, CLU)
    low = shifted(four[:2], 2, CLU)
    later, pieces = lax.optimization_barrier((four[2:], pieces))
    high = shifted(later, -2, CLU)
    parts = [four, below, above, low, high]
    ring = assemble(parts, [(0, 0), (3, 0), (1, 0), (2, 0), (2, 2)], me, width)
    slot_row, slot_col = routing(clusters[0], owners, capacity)
    ring, slot_row = lax.optimization_barrier((ring, slot_row))
    other = lax.ppermute(ring, "core", [(0, 1), (1, 0)])
    steps = (2, 1, -1, 0)
    *sent, kept = project(pieces, ring, other, lax.axis_index("x"), steps)
    common, received, ready = exchange_x(sent, steps[:-1], -1)
    outgoing = pack(
        kept, common, received, ready, slot_row, lax.axis_index("core"), owners, capacity, head_dim
    )
    incoming = lax.all_to_all(outgoing, CLU, split_axis=0, concat_axis=0, tiled=True)

    by_class = jnp.stack(
        [part[:, :16, width:] for part in (four, above, jnp.concatenate([low, high]), below)]
    )
    by_class = jnp.roll(by_class, lax.axis_index("zr"), axis=0)
    all_ids = by_class.transpose(1, 0, 2, 3).reshape((owners,) + by_class.shape[2:])
    members = owned_members(all_ids, me, heads, capacity)
    replies = attend(incoming, members, capacity)
    returned = lax.all_to_all(replies, CLU, split_axis=0, concat_axis=0, tiled=True)
    return unpack(returned, slot_col, capacity)[None]


def solution(mesh):
    ctx, clu, tp = (mesh.shape[name] for name in mesh.axis_names)
    fine = jax.sharding.Mesh(
        mesh.devices.reshape(ctx // 2, 2, clu // 4, 4, tp), ("x", "core") + CLU + ("tp",)
    )
    ctx_axes = ("x", "core")
    return jax.shard_map(
        body,
        mesh=fine,
        in_specs=(
            P(ctx_axes, CLU, None),
            P(ctx_axes + CLU, None, "tp"),
            P(ctx_axes, CLU, "tp"),
        ),
        out_specs=P(ctx_axes, CLU, "tp"),
        check_vma=False,
    )
```

```python
import jax
import jax.numpy as jnp
from jax import lax
from jax.experimental import pallas as pl
from jax.experimental.pallas import tpu as pltpu
from jax.sharding import PartitionSpec as P

CLUSTERS = 64
BF16 = jnp.bfloat16
F32 = jnp.float32
VMEM_LIMIT = 48 * 1024 * 1024
CUT_LIMIT = 62 * 1024 * 1024


def vmem_call(kernel, out_shape, in_smem, **kwargs):
    vmem = pl.BlockSpec(memory_space=pltpu.VMEM)
    smem = pl.BlockSpec(memory_space=pltpu.SMEM)
    return pl.pallas_call(
        kernel,
        out_shape=out_shape,
        in_specs=[smem if flag else vmem for flag in in_smem],
        out_specs=jax.tree.map(lambda _: vmem, out_shape),
        compiler_params=pltpu.CompilerParams(vmem_limit_bytes=VMEM_LIMIT),
        **kwargs,
    )


def scalar(value):
    return jnp.reshape(value, (1,)).astype(jnp.int32)


def iota(shape, dim):
    return lax.broadcasted_iota(jnp.int32, shape, dim)


def routing(ids, owners, capacity):
    rows, heads = ids.shape
    per_owner = CLUSTERS // owners

    def kernel(ids_ref, ids_t_ref, slot_row_ref, slot_col_ref):
        before_col = (iota((rows, rows), 1) < iota((rows, rows), 0)).astype(BF16)
        before_row = (iota((rows, rows), 0) < iota((rows, rows), 1)).astype(BF16)
        for h in range(heads):
            owner_col = ids_ref[:, h : h + 1] // per_owner
            hot = owner_col == iota((rows, owners), 1)
            count = jnp.dot(before_col, hot.astype(BF16), preferred_element_type=F32)
            rank = jnp.sum(jnp.where(hot, count, 0.0), axis=1, keepdims=True)
            slot_col_ref[:, h : h + 1] = owner_col * capacity + rank.astype(jnp.int32)
            owner_row = ids_t_ref[h : h + 1, :] // per_owner
            hot = owner_row == iota((owners, rows), 0)
            count = jnp.dot(hot.astype(BF16), before_row, preferred_element_type=F32)
            rank = jnp.sum(jnp.where(hot, count, 0.0), axis=0, keepdims=True)
            slot_row_ref[h : h + 1, :] = owner_row * capacity + rank.astype(jnp.int32)

    return vmem_call(
        kernel,
        (
            jax.ShapeDtypeStruct((heads, rows), jnp.int32),
            jax.ShapeDtypeStruct((rows, heads), jnp.int32),
        ),
        (False, False),
    )(ids, ids.T)


def owned_members(all_ids, me, heads, capacity):
    sources, id_rows, lanes = all_ids.shape
    rows = sources * capacity // 2
    per_head = rows // lanes
    per_owner = CLUSTERS // sources
    slots = sources * capacity

    def kernel(me_ref, ids_ref, out_ref):
        before = (iota((rows, rows), 0) < iota((rows, rows), 1)).astype(BF16)
        place = iota((sources, capacity, rows), 1)
        kinds = iota((16, slots), 0) + 1
        column = iota((slots, lanes), 1)
        tags = jnp.zeros((slots, lanes), jnp.int32)
        for h in range(heads):
            ids = jnp.concatenate(
                [ids_ref[:, h * per_head + j, :] for j in range(per_head)], axis=1
            )
            ids = ids.astype(F32).astype(jnp.int32)
            owner = ids // per_owner
            mine = owner == me_ref[0]
            rank = jnp.dot(mine.astype(BF16), before, preferred_element_type=F32)
            rank = jnp.where(mine, rank.astype(jnp.int32), -1)
            tag = ids - owner * per_owner + 1
            placed = jnp.where(rank[:, None, :] == place, tag[:, None, :], 0)
            tag = jnp.sum(placed.reshape(slots, rows), axis=1, keepdims=True)
            tags = jnp.where(column == h, tag, tags)
        same_slot = (iota((slots, slots), 0) == iota((slots, slots), 1)).astype(BF16)
        tags = lax.dot_general(
            tags.astype(BF16), same_slot, (((0,), (0,)), ((), ())), preferred_element_type=F32
        ).astype(jnp.int32)
        for h in range(heads):
            out_ref[h] = (tags[h : h + 1, :] == kinds).astype(BF16)

    return vmem_call(kernel, jax.ShapeDtypeStruct((heads, 16, slots), BF16), (True, False))(
        scalar(me), all_ids
    )


def cut_tokens(local_rows, core, chips):
    rows, depth = local_rows.shape
    half = depth // chips // 2

    def kernel(core_ref, in_ref, out_ref, block_ref, in_sems, out_sems):
        blocks = [(p, j) for p in range(chips) for j in range(2)]
        reads, writes = [], []
        for i, (p, j) in enumerate(blocks):
            first = (2 * p + lax.rem(core_ref[0] + j, 2)) * half
            reads.append(
                pltpu.make_async_copy(
                    in_ref.at[:, pl.ds(pl.multiple_of(first, half), half)],
                    block_ref.at[i],
                    in_sems.at[i],
                )
            )
            writes.append(
                pltpu.make_async_copy(
                    block_ref.at[i], out_ref.at[p, :, j * half : (j + 1) * half], out_sems.at[i]
                )
            )
        for read in reads:
            read.start()
        for read, write in zip(reads, writes):
            read.wait()
            write.start()
        for write in writes:
            write.wait()

    return pl.pallas_call(
        kernel,
        out_shape=jax.ShapeDtypeStruct((chips, rows, 2 * half), BF16),
        in_specs=[
            pl.BlockSpec(memory_space=pltpu.SMEM),
            pl.BlockSpec(memory_space=pl.ANY),
        ],
        out_specs=pl.BlockSpec(memory_space=pl.ANY),
        scratch_shapes=[
            pltpu.VMEM((2 * chips, rows, half), BF16),
            pltpu.SemaphoreType.DMA((2 * chips,)),
            pltpu.SemaphoreType.DMA((2 * chips,)),
        ],
        compiler_params=pltpu.CompilerParams(vmem_limit_bytes=CUT_LIMIT),
    )(scalar(core), local_rows)


def assemble(parts, places, me, width):
    shard = parts[0].shape[1]
    count = sum(part.shape[0] for part in parts)
    classes = 4

    def kernel(me_ref, *refs):
        out_ref = refs[-1]
        for ref, (kind, first) in zip(refs, places):
            device = lax.rem(me_ref[0] + kind, classes) + classes * first
            for j in range(ref.shape[0]):
                at = pl.multiple_of((device + classes * j) * shard, shard)
                out_ref[pl.ds(at, shard), :] = ref[j, :, :width]

    return vmem_call(
        kernel,
        jax.ShapeDtypeStruct((count * shard, width), BF16),
        (True,) + (False,) * len(parts),
    )(scalar(me), *parts)


def project(pieces, ring, other, x, steps):
    chips, rows, depth = pieces.shape
    half, width = ring.shape

    def kernel(x_ref, pieces_ref, ring_ref, other_ref, *refs):
        out_refs, (piece_ref, sems) = refs[:-2], refs[-2:]
        copies = [
            pltpu.make_async_copy(
                pieces_ref.at[lax.rem(x_ref[0] + step + chips, chips)], piece_ref.at[i], sems.at[i]
            )
            for i, step in enumerate(steps)
        ]
        for copy in copies:
            copy.start()
        for i, out_ref in enumerate(out_refs):
            copies[i].wait()
            total = jnp.dot(piece_ref[i, :, :half], ring_ref[...], preferred_element_type=F32)
            total += jnp.dot(piece_ref[i, :, half:], other_ref[...], preferred_element_type=F32)
            out_ref[...] = total.astype(BF16)

    smem = pl.BlockSpec(memory_space=pltpu.SMEM)
    vmem = pl.BlockSpec(memory_space=pltpu.VMEM)
    return pl.pallas_call(
        kernel,
        out_shape=(jax.ShapeDtypeStruct((rows, width), BF16),) * len(steps),
        in_specs=[smem, pl.BlockSpec(memory_space=pl.ANY), vmem, vmem],
        out_specs=(vmem,) * len(steps),
        scratch_shapes=[
            pltpu.VMEM((len(steps), rows, depth), BF16),
            pltpu.SemaphoreType.DMA((len(steps),)),
        ],
        compiler_params=pltpu.CompilerParams(vmem_limit_bytes=VMEM_LIMIT),
    )(scalar(x), pieces, ring, other)


def exchange_x(parts, steps):
    chips = lax.axis_size("x")
    received = []
    for core in (1, 0):
        for i, step in enumerate(steps):
            pairs = [(2 * x + core, (x + step) % chips * 2 + core) for x in range(chips)]
            received.append(lax.ppermute(parts[i], ("x", "core"), pairs))
        if core == 1:
            ready = sum(part[:16, :128] for part in received)
            ready = lax.ppermute(ready, "core", [(1, 0)])
            parts, ready = lax.optimization_barrier((parts, ready))
    return received, ready


def pack(own, received, ready, slot_row, core, owners, capacity, head_dim):
    rows, width = own.shape
    heads = slot_row.shape[0]
    slots = owners * capacity
    count = len(received) // 2

    def kernel(core_ref, slot_ref, own_ref, *refs):
        out_ref, part_ref, sems = refs[-3:]

        def columns(h, m):
            return slice((m * heads + h) * head_dim, (m * heads + h + 1) * head_dim)

        def copies(part_refs, h):
            return [
                pltpu.make_async_copy(
                    ref.at[:, columns(h, m)], part_ref.at[i, :, columns(h, m)], sems.at[h, m, i]
                )
                for m in range(2)
                for i, ref in enumerate((own_ref,) + part_refs)
            ]

        chosen = [(1, refs[:count]), (0, refs[count : 2 * count])]
        for number, part_refs in chosen:

            @pl.when(core_ref[0] == number)
            def _():
                for h in range(heads):
                    for copy in copies(part_refs, h):
                        copy.start()

        for h in range(heads):
            for number, part_refs in chosen:

                @pl.when(core_ref[0] == number)
                def _():
                    for copy in copies(part_refs, h):
                        copy.wait()

            place = iota((slots, rows), 0) == slot_ref[h : h + 1, :]
            place = place.astype(BF16)
            for m in range(2):
                total = part_ref[0, :, columns(h, m)].astype(F32)
                for i in range(1, count + 1):
                    total += part_ref[i, :, columns(h, m)].astype(F32)
                packed = jnp.dot(
                    place, total.astype(BF16), preferred_element_type=F32
                ).astype(BF16)
                out_ref[
                    :, h * capacity : (h + 1) * capacity, m * head_dim : (m + 1) * head_dim
                ] = packed.reshape(owners, capacity, head_dim)

    vmem = pl.BlockSpec(memory_space=pltpu.VMEM)
    whole = pl.BlockSpec(memory_space=pl.ANY)
    return pl.pallas_call(
        kernel,
        out_shape=jax.ShapeDtypeStruct((owners, heads * capacity, 2 * head_dim), BF16),
        in_specs=[pl.BlockSpec(memory_space=pltpu.SMEM), vmem] + [whole] * (len(received) + 2),
        out_specs=vmem,
        scratch_shapes=[
            pltpu.VMEM((count + 1, rows, width), BF16),
            pltpu.SemaphoreType.DMA((heads, 2, count + 1)),
        ],
        compiler_params=pltpu.CompilerParams(vmem_limit_bytes=VMEM_LIMIT),
    )(scalar(core), slot_row, own, *received, ready)


def attend(blocks, members, capacity):
    sources, rows, width = blocks.shape
    head_dim = width // 2
    heads = rows // capacity
    slots = sources * capacity
    scale = head_dim ** (-0.5)

    def kernel(block_ref, member_ref, out_ref):
        query = iota((slots, slots), 0)
        key = iota((slots, slots), 1)
        for h in range(heads):
            here = slice(h * capacity, (h + 1) * capacity)
            keys = block_ref[:, here, :head_dim].reshape(slots, head_dim)
            values = block_ref[:, here, head_dim:].reshape(slots, head_dim)
            member = member_ref[h]
            same = lax.dot_general(
                member, member, (((0,), (0,)), ((), ())), preferred_element_type=F32
            )
            scores = lax.dot_general(
                keys, keys, (((1,), (1,)), ((), ())), preferred_element_type=F32
            )
            scores = jnp.where(query == key, -100000.0, scores * scale)
            scores = jnp.where((same > 0.5) & (key <= query), scores, -1e30)
            row_max = jnp.max(scores, axis=1, keepdims=True)
            weights = jnp.exp(scores - row_max)
            total = jnp.sum(weights, axis=1, keepdims=True)
            probabilities = (weights / total).astype(BF16)
            result = jnp.dot(probabilities, values, preferred_element_type=F32).astype(BF16)
            out_ref[:, here, :] = result.reshape(sources, capacity, head_dim)

    return vmem_call(
        kernel, jax.ShapeDtypeStruct((sources, rows, head_dim), BF16), (False, False)
    )(blocks, members)


def unpack(returned, slot_col, capacity):
    owners, height, head_dim = returned.shape
    rows, heads = slot_col.shape
    slots = owners * capacity

    def kernel(block_ref, slot_ref, out_ref):
        for h in range(heads):
            block = block_ref[:, h * capacity : (h + 1) * capacity, :].reshape(slots, head_dim)
            place = slot_ref[:, h : h + 1] == iota((rows, slots), 1)
            out_ref[:, h * head_dim : (h + 1) * head_dim] = jnp.dot(
                place.astype(BF16), block, preferred_element_type=F32
            ).astype(BF16)

    return vmem_call(
        kernel, jax.ShapeDtypeStruct((rows, heads * head_dim), BF16), (False, False)
    )(returned, slot_col)


CLU = ("zq", "zr")


def shifted(block, step, axis):
    size = lax.axis_size(axis)
    return lax.ppermute(block, axis, [(i, (i + step) % size) for i in range(size)])


def body(tokens, proj_weight, clusters):
    rows, depth = tokens.shape[1:]
    owners = lax.axis_size(CLU)
    me = lax.axis_index(CLU)
    heads = clusters.shape[2]
    shard = proj_weight.shape[0]
    width = 2 * proj_weight.shape[2]
    head_dim = proj_weight.shape[2] // heads
    capacity = 2 * rows // owners
    chips = lax.axis_size("x")

    pieces = cut_tokens(tokens[0], lax.axis_index("core"), chips)
    ids = clusters[0].T.astype(BF16).reshape(-1, 128)
    ids = jnp.pad(ids, ((0, shard - ids.shape[0]), (0, 0)))
    own = jnp.concatenate([proj_weight.reshape(shard, width), ids], axis=1)
    own, pieces = lax.optimization_barrier((own, pieces))
    pieces = lax.all_to_all(pieces, "x", split_axis=0, concat_axis=0, tiled=True)

    four = lax.all_gather(own, "zq", axis=0)
    below = shifted(four, 1, CLU)
    above = shifted(four, -1, CLU)
    low = shifted(four[:2], 2, CLU)
    later, pieces = lax.optimization_barrier((four[2:], pieces))
    high = shifted(later, -2, CLU)
    parts = [four, below, above, low, high]
    ring = assemble(parts, [(0, 0), (3, 0), (1, 0), (2, 0), (2, 2)], me, width)
    slot_row, slot_col = routing(clusters[0], owners, capacity)
    ring, slot_row = lax.optimization_barrier((ring, slot_row))
    other = lax.ppermute(ring, "core", [(0, 1), (1, 0)])
    steps = (2, 1, -1, 0)
    *sent, kept = project(pieces, ring, other, lax.axis_index("x"), steps)
    received, ready = exchange_x(sent, steps[:-1])
    outgoing = pack(
        kept, received, ready, slot_row, lax.axis_index("core"), owners, capacity, head_dim
    )
    incoming = lax.all_to_all(outgoing, CLU, split_axis=0, concat_axis=0, tiled=True)

    by_class = jnp.stack(
        [part[:, :16, width:] for part in (four, above, jnp.concatenate([low, high]), below)]
    )
    by_class = jnp.roll(by_class, lax.axis_index("zr"), axis=0)
    all_ids = by_class.transpose(1, 0, 2, 3).reshape((owners,) + by_class.shape[2:])
    members = owned_members(all_ids, me, heads, capacity)
    replies = attend(incoming, members, capacity)
    returned = lax.all_to_all(replies, CLU, split_axis=0, concat_axis=0, tiled=True)
    return unpack(returned, slot_col, capacity)[None]


def solution(mesh):
    ctx, clu, tp = (mesh.shape[name] for name in mesh.axis_names)
    fine = jax.sharding.Mesh(
        mesh.devices.reshape(ctx // 2, 2, clu // 4, 4, tp), ("x", "core") + CLU + ("tp",)
    )
    ctx_axes = ("x", "core")
    return jax.shard_map(
        body,
        mesh=fine,
        in_specs=(
            P(ctx_axes, CLU, None),
            P(ctx_axes + CLU, None, "tp"),
            P(ctx_axes, CLU, "tp"),
        ),
        out_specs=P(ctx_axes, CLU, "tp"),
        check_vma=False,
    )
```

```python
import jax
import jax.numpy as jnp
from jax import lax
from jax.experimental import pallas as pl
from jax.experimental.pallas import tpu as pltpu
from jax.sharding import PartitionSpec as P

CLUSTERS = 64
BF16 = jnp.bfloat16
F32 = jnp.float32
VMEM_LIMIT = 48 * 1024 * 1024
CUT_LIMIT = 62 * 1024 * 1024


def vmem_call(kernel, out_shape, in_smem, **kwargs):
    vmem = pl.BlockSpec(memory_space=pltpu.VMEM)
    smem = pl.BlockSpec(memory_space=pltpu.SMEM)
    return pl.pallas_call(
        kernel,
        out_shape=out_shape,
        in_specs=[smem if flag else vmem for flag in in_smem],
        out_specs=jax.tree.map(lambda _: vmem, out_shape),
        compiler_params=pltpu.CompilerParams(vmem_limit_bytes=VMEM_LIMIT),
        **kwargs,
    )


def scalar(value):
    return jnp.reshape(value, (1,)).astype(jnp.int32)


def iota(shape, dim):
    return lax.broadcasted_iota(jnp.int32, shape, dim)


def routing(ids, owners, capacity):
    rows, heads = ids.shape
    per_owner = CLUSTERS // owners

    def kernel(ids_ref, ids_t_ref, slot_row_ref, slot_col_ref):
        before_col = (iota((rows, rows), 1) < iota((rows, rows), 0)).astype(BF16)
        before_row = (iota((rows, rows), 0) < iota((rows, rows), 1)).astype(BF16)
        for h in range(heads):
            owner_col = ids_ref[:, h : h + 1] // per_owner
            hot = owner_col == iota((rows, owners), 1)
            count = jnp.dot(before_col, hot.astype(BF16), preferred_element_type=F32)
            rank = jnp.sum(jnp.where(hot, count, 0.0), axis=1, keepdims=True)
            slot_col_ref[:, h : h + 1] = owner_col * capacity + rank.astype(jnp.int32)
            owner_row = ids_t_ref[h : h + 1, :] // per_owner
            hot = owner_row == iota((owners, rows), 0)
            count = jnp.dot(hot.astype(BF16), before_row, preferred_element_type=F32)
            rank = jnp.sum(jnp.where(hot, count, 0.0), axis=0, keepdims=True)
            slot_row_ref[h : h + 1, :] = owner_row * capacity + rank.astype(jnp.int32)

    return vmem_call(
        kernel,
        (
            jax.ShapeDtypeStruct((heads, rows), jnp.int32),
            jax.ShapeDtypeStruct((rows, heads), jnp.int32),
        ),
        (False, False),
    )(ids, ids.T)


def owned_members(all_ids, me, heads, capacity):
    sources, id_rows, lanes = all_ids.shape
    rows = sources * capacity // 2
    per_head = rows // lanes
    per_owner = CLUSTERS // sources
    slots = sources * capacity

    def kernel(me_ref, ids_ref, out_ref):
        before = (iota((rows, rows), 0) < iota((rows, rows), 1)).astype(BF16)
        place = iota((sources, capacity, rows), 1)
        kinds = iota((16, slots), 0) + 1
        column = iota((slots, lanes), 1)
        tags = jnp.zeros((slots, lanes), jnp.int32)
        for h in range(heads):
            ids = jnp.concatenate(
                [ids_ref[:, h * per_head + j, :] for j in range(per_head)], axis=1
            )
            ids = ids.astype(F32).astype(jnp.int32)
            owner = ids // per_owner
            mine = owner == me_ref[0]
            rank = jnp.dot(mine.astype(BF16), before, preferred_element_type=F32)
            rank = jnp.where(mine, rank.astype(jnp.int32), -1)
            tag = ids - owner * per_owner + 1
            placed = jnp.where(rank[:, None, :] == place, tag[:, None, :], 0)
            tag = jnp.sum(placed.reshape(slots, rows), axis=1, keepdims=True)
            tags = jnp.where(column == h, tag, tags)
        same_slot = (iota((slots, slots), 0) == iota((slots, slots), 1)).astype(BF16)
        tags = lax.dot_general(
            tags.astype(BF16), same_slot, (((0,), (0,)), ((), ())), preferred_element_type=F32
        ).astype(jnp.int32)
        for h in range(heads):
            out_ref[h] = (tags[h : h + 1, :] == kinds).astype(BF16)

    return vmem_call(kernel, jax.ShapeDtypeStruct((heads, 16, slots), BF16), (True, False))(
        scalar(me), all_ids
    )


def cut_tokens(local_rows, core, chips):
    rows, depth = local_rows.shape
    half = depth // chips // 2

    def kernel(core_ref, in_ref, out_ref, block_ref, in_sems, out_sems):
        blocks = [(p, j) for p in range(chips) for j in range(2)]
        reads, writes = [], []
        for i, (p, j) in enumerate(blocks):
            first = (2 * p + lax.rem(core_ref[0] + j, 2)) * half
            reads.append(
                pltpu.make_async_copy(
                    in_ref.at[:, pl.ds(pl.multiple_of(first, half), half)],
                    block_ref.at[i],
                    in_sems.at[i],
                )
            )
            writes.append(
                pltpu.make_async_copy(
                    block_ref.at[i], out_ref.at[p, :, j * half : (j + 1) * half], out_sems.at[i]
                )
            )
        for read in reads:
            read.start()
        for read, write in zip(reads, writes):
            read.wait()
            write.start()
        for write in writes:
            write.wait()

    return pl.pallas_call(
        kernel,
        out_shape=jax.ShapeDtypeStruct((chips, rows, 2 * half), BF16),
        in_specs=[
            pl.BlockSpec(memory_space=pltpu.SMEM),
            pl.BlockSpec(memory_space=pl.ANY),
        ],
        out_specs=pl.BlockSpec(memory_space=pl.ANY),
        scratch_shapes=[
            pltpu.VMEM((2 * chips, rows, half), BF16),
            pltpu.SemaphoreType.DMA((2 * chips,)),
            pltpu.SemaphoreType.DMA((2 * chips,)),
        ],
        compiler_params=pltpu.CompilerParams(vmem_limit_bytes=CUT_LIMIT),
    )(scalar(core), local_rows)


def assemble(parts, places, me, width):
    shard = parts[0].shape[1]
    count = sum(part.shape[0] for part in parts)
    classes = 4

    def kernel(me_ref, *refs):
        out_ref = refs[-1]
        for ref, (kind, first) in zip(refs, places):
            device = lax.rem(me_ref[0] + kind, classes) + classes * first
            for j in range(ref.shape[0]):
                at = pl.multiple_of((device + classes * j) * shard, shard)
                out_ref[pl.ds(at, shard), :] = ref[j, :, :width]

    return vmem_call(
        kernel,
        jax.ShapeDtypeStruct((count * shard, width), BF16),
        (True,) + (False,) * len(parts),
    )(scalar(me), *parts)


def project(pieces, ring, other, x, steps):
    chips, rows, depth = pieces.shape
    half, width = ring.shape

    def kernel(x_ref, pieces_ref, ring_ref, other_ref, *out_refs):
        for step, out_ref in zip(steps, out_refs):
            p = lax.rem(x_ref[0] + step + chips, chips)
            total = jnp.dot(pieces_ref[p, :, :half], ring_ref[...], preferred_element_type=F32)
            total += jnp.dot(pieces_ref[p, :, half:], other_ref[...], preferred_element_type=F32)
            out_ref[...] = total.astype(BF16)

    return vmem_call(
        kernel,
        (jax.ShapeDtypeStruct((rows, width), BF16),) * len(steps),
        (True, False, False, False),
    )(scalar(x), pieces, ring, other)


def exchange_x(parts, steps, free):
    chips = lax.axis_size("x")

    def send(part, step, core):
        pairs = [(2 * x + core, (x + step) % chips * 2 + core) for x in range(chips)]
        return lax.ppermute(part, ("x", "core"), pairs)

    first = [send(part, step, 1) for part, step in zip(parts, steps)]
    second = [send(parts[steps.index(free)], free, 0)]
    ready = sum(part[:16, :128] for part in first)
    ready = lax.ppermute(ready, "core", [(1, 0)])
    parts, ready = lax.optimization_barrier((parts, ready))
    second += [send(part, step, 0) for part, step in zip(parts, steps) if step != free]
    return first + second, ready


def pack(own, received, ready, slot_row, core, owners, capacity, head_dim):
    rows, width = own.shape
    heads = slot_row.shape[0]
    slots = owners * capacity
    count = len(received) // 2

    def kernel(core_ref, own_ref, *refs):
        slot_ref, _, out_ref = refs[-3:]

        def place_sums(part_refs):
            for h in range(heads):
                place = iota((slots, rows), 0) == slot_ref[h : h + 1, :]
                place = place.astype(BF16)
                for m in range(2):
                    cols = slice((m * heads + h) * head_dim, (m * heads + h + 1) * head_dim)
                    total = own_ref[:, cols].astype(F32)
                    for ref in part_refs:
                        total += ref[:, cols].astype(F32)
                    packed = jnp.dot(
                        place, total.astype(BF16), preferred_element_type=F32
                    ).astype(BF16)
                    out_ref[
                        :, h * capacity : (h + 1) * capacity, m * head_dim : (m + 1) * head_dim
                    ] = packed.reshape(owners, capacity, head_dim)

        @pl.when(core_ref[0] == 1)
        def _():
            place_sums(refs[:count])

        @pl.when(core_ref[0] == 0)
        def _():
            place_sums(refs[count : 2 * count])

    return vmem_call(
        kernel,
        jax.ShapeDtypeStruct((owners, heads * capacity, 2 * head_dim), BF16),
        (True,) + (False,) * (len(received) + 3),
    )(scalar(core), own, *received, slot_row, ready)


def attend(blocks, members, capacity):
    sources, rows, width = blocks.shape
    head_dim = width // 2
    heads = rows // capacity
    slots = sources * capacity
    scale = head_dim ** (-0.5)

    def kernel(block_ref, member_ref, out_ref):
        query = iota((slots, slots), 0)
        key = iota((slots, slots), 1)
        for h in range(heads):
            here = slice(h * capacity, (h + 1) * capacity)
            keys = block_ref[:, here, :head_dim].reshape(slots, head_dim)
            values = block_ref[:, here, head_dim:].reshape(slots, head_dim)
            member = member_ref[h]
            same = lax.dot_general(
                member, member, (((0,), (0,)), ((), ())), preferred_element_type=F32
            )
            scores = lax.dot_general(
                keys, keys, (((1,), (1,)), ((), ())), preferred_element_type=F32
            )
            scores = jnp.where(query == key, -100000.0, scores * scale)
            scores = jnp.where((same > 0.5) & (key <= query), scores, -1e30)
            row_max = jnp.max(scores, axis=1, keepdims=True)
            weights = jnp.exp(scores - row_max)
            total = jnp.sum(weights, axis=1, keepdims=True)
            probabilities = (weights / total).astype(BF16)
            result = jnp.dot(probabilities, values, preferred_element_type=F32).astype(BF16)
            out_ref[:, here, :] = result.reshape(sources, capacity, head_dim)

    return vmem_call(
        kernel, jax.ShapeDtypeStruct((sources, rows, head_dim), BF16), (False, False)
    )(blocks, members)


def unpack(returned, slot_col, capacity):
    owners, height, head_dim = returned.shape
    rows, heads = slot_col.shape
    slots = owners * capacity

    def kernel(block_ref, slot_ref, out_ref):
        for h in range(heads):
            block = block_ref[:, h * capacity : (h + 1) * capacity, :].reshape(slots, head_dim)
            place = slot_ref[:, h : h + 1] == iota((rows, slots), 1)
            out_ref[:, h * head_dim : (h + 1) * head_dim] = jnp.dot(
                place.astype(BF16), block, preferred_element_type=F32
            ).astype(BF16)

    return vmem_call(
        kernel, jax.ShapeDtypeStruct((rows, heads * head_dim), BF16), (False, False)
    )(returned, slot_col)


CLU = ("zq", "zr")


def shifted(block, step, axis):
    size = lax.axis_size(axis)
    return lax.ppermute(block, axis, [(i, (i + step) % size) for i in range(size)])


def body(tokens, proj_weight, clusters):
    rows, depth = tokens.shape[1:]
    owners = lax.axis_size(CLU)
    me = lax.axis_index(CLU)
    heads = clusters.shape[2]
    shard = proj_weight.shape[0]
    width = 2 * proj_weight.shape[2]
    head_dim = proj_weight.shape[2] // heads
    capacity = 2 * rows // owners
    chips = lax.axis_size("x")

    pieces = cut_tokens(tokens[0], lax.axis_index("core"), chips)
    ids = clusters[0].T.astype(BF16).reshape(-1, 128)
    ids = jnp.pad(ids, ((0, shard - ids.shape[0]), (0, 0)))
    own = jnp.concatenate([proj_weight.reshape(shard, width), ids], axis=1)
    own, pieces = lax.optimization_barrier((own, pieces))
    pieces = lax.all_to_all(pieces, "x", split_axis=0, concat_axis=0, tiled=True)

    four = lax.all_gather(own, "zq", axis=0)
    below = shifted(four, 1, CLU)
    above = shifted(four, -1, CLU)
    low = shifted(four[:2], 2, CLU)
    later, pieces = lax.optimization_barrier((four[2:], pieces))
    high = shifted(later, -2, CLU)
    parts = [four, below, above, low, high]
    ring = assemble(parts, [(0, 0), (3, 0), (1, 0), (2, 0), (2, 2)], me, width)
    slot_row, slot_col = routing(clusters[0], owners, capacity)
    ring, slot_row = lax.optimization_barrier((ring, slot_row))
    other = lax.ppermute(ring, "core", [(0, 1), (1, 0)])
    steps = (2, 1, -1, 0)
    *sent, kept = project(pieces, ring, other, lax.axis_index("x"), steps)
    received, ready = exchange_x(sent, steps[:-1], -1)
    outgoing = pack(
        kept, received, ready, slot_row, lax.axis_index("core"), owners, capacity, head_dim
    )
    incoming = lax.all_to_all(outgoing, CLU, split_axis=0, concat_axis=0, tiled=True)

    by_class = jnp.stack(
        [part[:, :16, width:] for part in (four, above, jnp.concatenate([low, high]), below)]
    )
    by_class = jnp.roll(by_class, lax.axis_index("zr"), axis=0)
    all_ids = by_class.transpose(1, 0, 2, 3).reshape((owners,) + by_class.shape[2:])
    members = owned_members(all_ids, me, heads, capacity)
    replies = attend(incoming, members, capacity)
    returned = lax.all_to_all(replies, CLU, split_axis=0, concat_axis=0, tiled=True)
    return unpack(returned, slot_col, capacity)[None]


def solution(mesh):
    ctx, clu, tp = (mesh.shape[name] for name in mesh.axis_names)
    fine = jax.sharding.Mesh(
        mesh.devices.reshape(ctx // 2, 2, clu // 4, 4, tp), ("x", "core") + CLU + ("tp",)
    )
    ctx_axes = ("x", "core")
    return jax.shard_map(
        body,
        mesh=fine,
        in_specs=(
            P(ctx_axes, CLU, None),
            P(ctx_axes + CLU, None, "tp"),
            P(ctx_axes, CLU, "tp"),
        ),
        out_specs=P(ctx_axes, CLU, "tp"),
        check_vma=False,
    )
```

```python
import jax
import jax.numpy as jnp
from jax import lax
from jax.experimental import pallas as pl
from jax.experimental.pallas import tpu as pltpu
from jax.sharding import PartitionSpec as P

CLUSTERS = 64
BF16 = jnp.bfloat16
F32 = jnp.float32
VMEM_LIMIT = 48 * 1024 * 1024
CUT_LIMIT = 62 * 1024 * 1024


def vmem_call(kernel, out_shape, in_smem, **kwargs):
    vmem = pl.BlockSpec(memory_space=pltpu.VMEM)
    smem = pl.BlockSpec(memory_space=pltpu.SMEM)
    return pl.pallas_call(
        kernel,
        out_shape=out_shape,
        in_specs=[smem if flag else vmem for flag in in_smem],
        out_specs=jax.tree.map(lambda _: vmem, out_shape),
        compiler_params=pltpu.CompilerParams(vmem_limit_bytes=VMEM_LIMIT),
        **kwargs,
    )


def scalar(value):
    return jnp.reshape(value, (1,)).astype(jnp.int32)


def iota(shape, dim):
    return lax.broadcasted_iota(jnp.int32, shape, dim)


def routing(ids, owners, capacity):
    rows, heads = ids.shape
    per_owner = CLUSTERS // owners

    def kernel(ids_ref, ids_t_ref, slot_row_ref, slot_col_ref):
        before_col = (iota((rows, rows), 1) < iota((rows, rows), 0)).astype(BF16)
        before_row = (iota((rows, rows), 0) < iota((rows, rows), 1)).astype(BF16)
        for h in range(heads):
            owner_col = ids_ref[:, h : h + 1] // per_owner
            hot = owner_col == iota((rows, owners), 1)
            count = jnp.dot(before_col, hot.astype(BF16), preferred_element_type=F32)
            rank = jnp.sum(jnp.where(hot, count, 0.0), axis=1, keepdims=True)
            slot_col_ref[:, h : h + 1] = owner_col * capacity + rank.astype(jnp.int32)
            owner_row = ids_t_ref[h : h + 1, :] // per_owner
            hot = owner_row == iota((owners, rows), 0)
            count = jnp.dot(hot.astype(BF16), before_row, preferred_element_type=F32)
            rank = jnp.sum(jnp.where(hot, count, 0.0), axis=0, keepdims=True)
            slot_row_ref[h : h + 1, :] = owner_row * capacity + rank.astype(jnp.int32)

    return vmem_call(
        kernel,
        (
            jax.ShapeDtypeStruct((heads, rows), jnp.int32),
            jax.ShapeDtypeStruct((rows, heads), jnp.int32),
        ),
        (False, False),
    )(ids, ids.T)


def owned_members(all_ids, me, heads, capacity):
    sources, id_rows, lanes = all_ids.shape
    rows = sources * capacity // 2
    per_head = rows // lanes
    per_owner = CLUSTERS // sources
    slots = sources * capacity

    def kernel(me_ref, ids_ref, out_ref):
        before = (iota((rows, rows), 0) < iota((rows, rows), 1)).astype(BF16)
        place = iota((sources, capacity, rows), 1)
        kinds = iota((16, slots), 0) + 1
        column = iota((slots, lanes), 1)
        tags = jnp.zeros((slots, lanes), jnp.int32)
        for h in range(heads):
            ids = jnp.concatenate(
                [ids_ref[:, h * per_head + j, :] for j in range(per_head)], axis=1
            )
            ids = ids.astype(F32).astype(jnp.int32)
            owner = ids // per_owner
            mine = owner == me_ref[0]
            rank = jnp.dot(mine.astype(BF16), before, preferred_element_type=F32)
            rank = jnp.where(mine, rank.astype(jnp.int32), -1)
            tag = ids - owner * per_owner + 1
            placed = jnp.where(rank[:, None, :] == place, tag[:, None, :], 0)
            tag = jnp.sum(placed.reshape(slots, rows), axis=1, keepdims=True)
            tags = jnp.where(column == h, tag, tags)
        same_slot = (iota((slots, slots), 0) == iota((slots, slots), 1)).astype(BF16)
        tags = lax.dot_general(
            tags.astype(BF16), same_slot, (((0,), (0,)), ((), ())), preferred_element_type=F32
        ).astype(jnp.int32)
        for h in range(heads):
            out_ref[h] = (tags[h : h + 1, :] == kinds).astype(BF16)

    return vmem_call(kernel, jax.ShapeDtypeStruct((heads, 16, slots), BF16), (True, False))(
        scalar(me), all_ids
    )


def cut_tokens(local_rows, core, chips):
    rows, depth = local_rows.shape
    half = depth // chips // 2

    def kernel(core_ref, in_ref, out_ref, block_ref, in_sems, out_sems):
        blocks = [(p, j) for p in range(chips) for j in range(2)]
        reads, writes = [], []
        for i, (p, j) in enumerate(blocks):
            first = (2 * p + lax.rem(core_ref[0] + j, 2)) * half
            reads.append(
                pltpu.make_async_copy(
                    in_ref.at[:, pl.ds(pl.multiple_of(first, half), half)],
                    block_ref.at[i],
                    in_sems.at[i],
                )
            )
            writes.append(
                pltpu.make_async_copy(
                    block_ref.at[i], out_ref.at[p, :, j * half : (j + 1) * half], out_sems.at[i]
                )
            )
        for read in reads:
            read.start()
        for read, write in zip(reads, writes):
            read.wait()
            write.start()
        for write in writes:
            write.wait()

    return pl.pallas_call(
        kernel,
        out_shape=jax.ShapeDtypeStruct((chips, rows, 2 * half), BF16),
        in_specs=[
            pl.BlockSpec(memory_space=pltpu.SMEM),
            pl.BlockSpec(memory_space=pl.ANY),
        ],
        out_specs=pl.BlockSpec(memory_space=pl.ANY),
        scratch_shapes=[
            pltpu.VMEM((2 * chips, rows, half), BF16),
            pltpu.SemaphoreType.DMA((2 * chips,)),
            pltpu.SemaphoreType.DMA((2 * chips,)),
        ],
        compiler_params=pltpu.CompilerParams(vmem_limit_bytes=CUT_LIMIT),
    )(scalar(core), local_rows)


def assemble(parts, places, me, width):
    shard = parts[0].shape[1]
    count = sum(part.shape[0] for part in parts)
    classes = 4

    def kernel(me_ref, *refs):
        out_ref = refs[-1]
        for ref, (kind, first) in zip(refs, places):
            device = lax.rem(me_ref[0] + kind, classes) + classes * first
            for j in range(ref.shape[0]):
                at = pl.multiple_of((device + classes * j) * shard, shard)
                out_ref[pl.ds(at, shard), :] = ref[j, :, :width]

    return vmem_call(
        kernel,
        jax.ShapeDtypeStruct((count * shard, width), BF16),
        (True,) + (False,) * len(parts),
    )(scalar(me), *parts)


def project(pieces, ring, other, x, steps):
    chips, rows, depth = pieces.shape
    half, width = ring.shape

    def kernel(x_ref, pieces_ref, ring_ref, other_ref, *out_refs):
        for step, out_ref in zip(steps, out_refs):
            p = lax.rem(x_ref[0] + step + chips, chips)
            total = jnp.dot(pieces_ref[p, :, :half], ring_ref[...], preferred_element_type=F32)
            total += jnp.dot(pieces_ref[p, :, half:], other_ref[...], preferred_element_type=F32)
            out_ref[...] = total.astype(BF16)

    return vmem_call(
        kernel,
        (jax.ShapeDtypeStruct((rows, width), BF16),) * len(steps),
        (True, False, False, False),
    )(scalar(x), pieces, ring, other)


def exchange_x(parts, steps):
    chips = lax.axis_size("x")
    received = []
    for core in (1, 0):
        for i, step in enumerate(steps):
            pairs = [(2 * x + core, (x + step) % chips * 2 + core) for x in range(chips)]
            received.append(lax.ppermute(parts[i], ("x", "core"), pairs))
        if core == 1:
            ready = sum(part[:16, :128] for part in received)
            ready = lax.ppermute(ready, "core", [(1, 0)])
            parts, ready = lax.optimization_barrier((parts, ready))
    return received, ready


def pack(own, received, ready, slot_row, core, owners, capacity, head_dim):
    rows, width = own.shape
    heads = slot_row.shape[0]
    slots = owners * capacity
    count = len(received) // 2

    def kernel(core_ref, own_ref, *refs):
        slot_ref, _, out_ref = refs[-3:]

        def place_sums(part_refs):
            for h in range(heads):
                place = iota((slots, rows), 0) == slot_ref[h : h + 1, :]
                place = place.astype(BF16)
                for m in range(2):
                    cols = slice((m * heads + h) * head_dim, (m * heads + h + 1) * head_dim)
                    total = own_ref[:, cols].astype(F32)
                    for ref in part_refs:
                        total += ref[:, cols].astype(F32)
                    packed = jnp.dot(
                        place, total.astype(BF16), preferred_element_type=F32
                    ).astype(BF16)
                    out_ref[
                        :, h * capacity : (h + 1) * capacity, m * head_dim : (m + 1) * head_dim
                    ] = packed.reshape(owners, capacity, head_dim)

        @pl.when(core_ref[0] == 1)
        def _():
            place_sums(refs[:count])

        @pl.when(core_ref[0] == 0)
        def _():
            place_sums(refs[count : 2 * count])

    return vmem_call(
        kernel,
        jax.ShapeDtypeStruct((owners, heads * capacity, 2 * head_dim), BF16),
        (True,) + (False,) * (len(received) + 3),
    )(scalar(core), own, *received, slot_row, ready)


def attend(blocks, members, capacity):
    sources, rows, width = blocks.shape
    head_dim = width // 2
    heads = rows // capacity
    slots = sources * capacity
    scale = head_dim ** (-0.5)

    def kernel(block_ref, member_ref, out_ref):
        query = iota((slots, slots), 0)
        key = iota((slots, slots), 1)
        for h in range(heads):
            here = slice(h * capacity, (h + 1) * capacity)
            keys = block_ref[:, here, :head_dim].reshape(slots, head_dim)
            values = block_ref[:, here, head_dim:].reshape(slots, head_dim)
            member = member_ref[h]
            same = lax.dot_general(
                member, member, (((0,), (0,)), ((), ())), preferred_element_type=F32
            )
            scores = lax.dot_general(
                keys, keys, (((1,), (1,)), ((), ())), preferred_element_type=F32
            )
            scores = jnp.where(query == key, -100000.0, scores * scale)
            scores = jnp.where((same > 0.5) & (key <= query), scores, -1e30)
            row_max = jnp.max(scores, axis=1, keepdims=True)
            weights = jnp.exp(scores - row_max)
            total = jnp.sum(weights, axis=1, keepdims=True)
            probabilities = (weights / total).astype(BF16)
            result = jnp.dot(probabilities, values, preferred_element_type=F32).astype(BF16)
            out_ref[:, here, :] = result.reshape(sources, capacity, head_dim)

    return vmem_call(
        kernel, jax.ShapeDtypeStruct((sources, rows, head_dim), BF16), (False, False)
    )(blocks, members)


def unpack(returned, slot_col, capacity):
    owners, height, head_dim = returned.shape
    rows, heads = slot_col.shape
    slots = owners * capacity

    def kernel(block_ref, slot_ref, out_ref):
        for h in range(heads):
            block = block_ref[:, h * capacity : (h + 1) * capacity, :].reshape(slots, head_dim)
            place = slot_ref[:, h : h + 1] == iota((rows, slots), 1)
            out_ref[:, h * head_dim : (h + 1) * head_dim] = jnp.dot(
                place.astype(BF16), block, preferred_element_type=F32
            ).astype(BF16)

    return vmem_call(
        kernel, jax.ShapeDtypeStruct((rows, heads * head_dim), BF16), (False, False)
    )(returned, slot_col)


CLU = ("zq", "zr")


def shifted(block, step, axis):
    size = lax.axis_size(axis)
    return lax.ppermute(block, axis, [(i, (i + step) % size) for i in range(size)])


def body(tokens, proj_weight, clusters):
    rows, depth = tokens.shape[1:]
    owners = lax.axis_size(CLU)
    me = lax.axis_index(CLU)
    heads = clusters.shape[2]
    shard = proj_weight.shape[0]
    width = 2 * proj_weight.shape[2]
    head_dim = proj_weight.shape[2] // heads
    capacity = 2 * rows // owners
    chips = lax.axis_size("x")

    pieces = cut_tokens(tokens[0], lax.axis_index("core"), chips)
    ids = clusters[0].T.astype(BF16).reshape(-1, 128)
    ids = jnp.pad(ids, ((0, shard - ids.shape[0]), (0, 0)))
    own = jnp.concatenate([proj_weight.reshape(shard, width), ids], axis=1)
    own, pieces = lax.optimization_barrier((own, pieces))
    pieces = lax.all_to_all(pieces, "x", split_axis=0, concat_axis=0, tiled=True)

    four = lax.all_gather(own, "zq", axis=0)
    below = shifted(four, 1, CLU)
    above = shifted(four, -1, CLU)
    low = shifted(four[:2], 2, CLU)
    later, pieces = lax.optimization_barrier((four[2:], pieces))
    high = shifted(later, -2, CLU)
    parts = [four, below, above, low, high]
    ring = assemble(parts, [(0, 0), (3, 0), (1, 0), (2, 0), (2, 2)], me, width)
    slot_row, slot_col = routing(clusters[0], owners, capacity)
    ring, slot_row = lax.optimization_barrier((ring, slot_row))
    other = lax.ppermute(ring, "core", [(0, 1), (1, 0)])
    steps = (2, 1, -1, 0)
    *sent, kept = project(pieces, ring, other, lax.axis_index("x"), steps)
    received, ready = exchange_x(sent, steps[:-1])
    outgoing = pack(
        kept, received, ready, slot_row, lax.axis_index("core"), owners, capacity, head_dim
    )
    incoming = lax.all_to_all(outgoing, CLU, split_axis=0, concat_axis=0, tiled=True)

    by_class = jnp.stack(
        [part[:, :16, width:] for part in (four, above, jnp.concatenate([low, high]), below)]
    )
    by_class = jnp.roll(by_class, lax.axis_index("zr"), axis=0)
    all_ids = by_class.transpose(1, 0, 2, 3).reshape((owners,) + by_class.shape[2:])
    members = owned_members(all_ids, me, heads, capacity)
    replies = attend(incoming, members, capacity)
    returned = lax.all_to_all(replies, CLU, split_axis=0, concat_axis=0, tiled=True)
    return unpack(returned, slot_col, capacity)[None]


def solution(mesh):
    ctx, clu, tp = (mesh.shape[name] for name in mesh.axis_names)
    fine = jax.sharding.Mesh(
        mesh.devices.reshape(ctx // 2, 2, clu // 4, 4, tp), ("x", "core") + CLU + ("tp",)
    )
    ctx_axes = ("x", "core")
    return jax.shard_map(
        body,
        mesh=fine,
        in_specs=(
            P(ctx_axes, CLU, None),
            P(ctx_axes + CLU, None, "tp"),
            P(ctx_axes, CLU, "tp"),
        ),
        out_specs=P(ctx_axes, CLU, "tp"),
        check_vma=False,
    )
```

```python
import jax
import jax.numpy as jnp
from jax import lax
from jax.experimental import pallas as pl
from jax.experimental.pallas import tpu as pltpu
from jax.sharding import PartitionSpec as P

CLUSTERS = 64
BF16 = jnp.bfloat16
F32 = jnp.float32
VMEM_LIMIT = 48 * 1024 * 1024
CUT_LIMIT = 62 * 1024 * 1024


def vmem_call(kernel, out_shape, in_smem, **kwargs):
    vmem = pl.BlockSpec(memory_space=pltpu.VMEM)
    smem = pl.BlockSpec(memory_space=pltpu.SMEM)
    return pl.pallas_call(
        kernel,
        out_shape=out_shape,
        in_specs=[smem if flag else vmem for flag in in_smem],
        out_specs=jax.tree.map(lambda _: vmem, out_shape),
        compiler_params=pltpu.CompilerParams(vmem_limit_bytes=VMEM_LIMIT),
        **kwargs,
    )


def scalar(value):
    return jnp.reshape(value, (1,)).astype(jnp.int32)


def iota(shape, dim):
    return lax.broadcasted_iota(jnp.int32, shape, dim)


def routing(ids, owners, capacity):
    rows, heads = ids.shape
    per_owner = CLUSTERS // owners

    def kernel(ids_ref, ids_t_ref, slot_row_ref, slot_col_ref):
        before_col = (iota((rows, rows), 1) < iota((rows, rows), 0)).astype(BF16)
        before_row = (iota((rows, rows), 0) < iota((rows, rows), 1)).astype(BF16)
        for h in range(heads):
            owner_col = ids_ref[:, h : h + 1] // per_owner
            hot = owner_col == iota((rows, owners), 1)
            count = jnp.dot(before_col, hot.astype(BF16), preferred_element_type=F32)
            rank = jnp.sum(jnp.where(hot, count, 0.0), axis=1, keepdims=True)
            slot_col_ref[:, h : h + 1] = owner_col * capacity + rank.astype(jnp.int32)
            owner_row = ids_t_ref[h : h + 1, :] // per_owner
            hot = owner_row == iota((owners, rows), 0)
            count = jnp.dot(hot.astype(BF16), before_row, preferred_element_type=F32)
            rank = jnp.sum(jnp.where(hot, count, 0.0), axis=0, keepdims=True)
            slot_row_ref[h : h + 1, :] = owner_row * capacity + rank.astype(jnp.int32)

    return vmem_call(
        kernel,
        (
            jax.ShapeDtypeStruct((heads, rows), jnp.int32),
            jax.ShapeDtypeStruct((rows, heads), jnp.int32),
        ),
        (False, False),
    )(ids, ids.T)


def owned_members(all_ids, me, heads, capacity):
    sources, id_rows, lanes = all_ids.shape
    rows = sources * capacity // 2
    per_head = rows // lanes
    per_owner = CLUSTERS // sources
    slots = sources * capacity

    def kernel(me_ref, ids_ref, out_ref):
        before = (iota((rows, rows), 0) < iota((rows, rows), 1)).astype(BF16)
        place = iota((sources, capacity, rows), 1)
        kinds = iota((16, slots), 0) + 1
        column = iota((slots, lanes), 1)
        tags = jnp.zeros((slots, lanes), jnp.int32)
        for h in range(heads):
            ids = jnp.concatenate(
                [ids_ref[:, h * per_head + j, :] for j in range(per_head)], axis=1
            )
            ids = ids.astype(F32).astype(jnp.int32)
            owner = ids // per_owner
            mine = owner == me_ref[0]
            rank = jnp.dot(mine.astype(BF16), before, preferred_element_type=F32)
            rank = jnp.where(mine, rank.astype(jnp.int32), -1)
            tag = ids - owner * per_owner + 1
            placed = jnp.where(rank[:, None, :] == place, tag[:, None, :], 0)
            tag = jnp.sum(placed.reshape(slots, rows), axis=1, keepdims=True)
            tags = jnp.where(column == h, tag, tags)
        same_slot = (iota((slots, slots), 0) == iota((slots, slots), 1)).astype(BF16)
        tags = lax.dot_general(
            tags.astype(BF16), same_slot, (((0,), (0,)), ((), ())), preferred_element_type=F32
        ).astype(jnp.int32)
        for h in range(heads):
            out_ref[h] = (tags[h : h + 1, :] == kinds).astype(BF16)

    return vmem_call(kernel, jax.ShapeDtypeStruct((heads, 16, slots), BF16), (True, False))(
        scalar(me), all_ids
    )


def cut_tokens(local_rows, core, chips):
    rows, depth = local_rows.shape
    half = depth // chips // 2

    def kernel(core_ref, in_ref, out_ref, block_ref, in_sems, out_sems):
        blocks = [(p, j) for p in range(chips) for j in range(2)]
        reads, writes = [], []
        for i, (p, j) in enumerate(blocks):
            first = (2 * p + lax.rem(core_ref[0] + j, 2)) * half
            reads.append(
                pltpu.make_async_copy(
                    in_ref.at[:, pl.ds(pl.multiple_of(first, half), half)],
                    block_ref.at[i],
                    in_sems.at[i],
                )
            )
            writes.append(
                pltpu.make_async_copy(
                    block_ref.at[i], out_ref.at[p, :, j * half : (j + 1) * half], out_sems.at[i]
                )
            )
        for read in reads:
            read.start()
        for read, write in zip(reads, writes):
            read.wait()
            write.start()
        for write in writes:
            write.wait()

    return pl.pallas_call(
        kernel,
        out_shape=jax.ShapeDtypeStruct((chips, rows, 2 * half), BF16),
        in_specs=[
            pl.BlockSpec(memory_space=pltpu.SMEM),
            pl.BlockSpec(memory_space=pl.ANY),
        ],
        out_specs=pl.BlockSpec(memory_space=pl.ANY),
        scratch_shapes=[
            pltpu.VMEM((2 * chips, rows, half), BF16),
            pltpu.SemaphoreType.DMA((2 * chips,)),
            pltpu.SemaphoreType.DMA((2 * chips,)),
        ],
        compiler_params=pltpu.CompilerParams(vmem_limit_bytes=CUT_LIMIT),
    )(scalar(core), local_rows)


def assemble(parts, places, me, width):
    shard = parts[0].shape[1]
    count = sum(part.shape[0] for part in parts)
    classes = 4

    def kernel(me_ref, *refs):
        out_ref = refs[-1]
        for ref, (kind, first) in zip(refs, places):
            device = lax.rem(me_ref[0] + kind, classes) + classes * first
            for j in range(ref.shape[0]):
                at = pl.multiple_of((device + classes * j) * shard, shard)
                out_ref[pl.ds(at, shard), :] = ref[j, :, :width]

    return vmem_call(
        kernel,
        jax.ShapeDtypeStruct((count * shard, width), BF16),
        (True,) + (False,) * len(parts),
    )(scalar(me), *parts)


def project(pieces, ring, other, x, steps):
    chips, rows, depth = pieces.shape
    half, width = ring.shape

    def kernel(x_ref, pieces_ref, ring_ref, other_ref, *out_refs):
        for step, out_ref in zip(steps, out_refs):
            p = lax.rem(x_ref[0] + step + chips, chips)
            total = jnp.dot(pieces_ref[p, :, :half], ring_ref[...], preferred_element_type=F32)
            total += jnp.dot(pieces_ref[p, :, half:], other_ref[...], preferred_element_type=F32)
            out_ref[...] = total.astype(BF16)

    return vmem_call(
        kernel,
        (jax.ShapeDtypeStruct((rows, width), BF16),) * len(steps),
        (True, False, False, False),
    )(scalar(x), pieces, ring, other)


def exchange_x(parts, steps):
    chips = lax.axis_size("x")
    received = []
    for core in (1, 0):
        for i, step in enumerate(steps):
            pairs = [(2 * x + core, (x + step) % chips * 2 + core) for x in range(chips)]
            received.append(lax.ppermute(parts[i], ("x", "core"), pairs))
        if core == 1:
            ready = sum(part[:16, :128] for part in received)
            ready = lax.ppermute(ready, "core", [(1, 0)])
            parts, ready = lax.optimization_barrier((parts, ready))
    return received, ready


def pack(own, received, ready, slot_row, core, owners, capacity, head_dim):
    rows, width = own.shape
    heads = slot_row.shape[0]
    slots = owners * capacity
    count = len(received) // 2

    def kernel(core_ref, slot_ref, own_ref, *refs):
        out_ref, part_ref, sems = refs[-3:]

        def copies(part_refs):
            return [
                pltpu.make_async_copy(ref, part_ref.at[i], sems.at[i])
                for i, ref in enumerate((own_ref,) + part_refs)
            ]

        for number, first in ((1, 0), (0, count)):

            @pl.when(core_ref[0] == number)
            def _():
                for copy in copies(refs[first : first + count]):
                    copy.start()
                for copy in copies(refs[first : first + count]):
                    copy.wait()

        for h in range(heads):
            place = iota((slots, rows), 0) == slot_ref[h : h + 1, :]
            place = place.astype(BF16)
            for m in range(2):
                cols = slice((m * heads + h) * head_dim, (m * heads + h + 1) * head_dim)
                total = part_ref[0, :, cols].astype(F32)
                for i in range(1, count + 1):
                    total += part_ref[i, :, cols].astype(F32)
                packed = jnp.dot(
                    place, total.astype(BF16), preferred_element_type=F32
                ).astype(BF16)
                out_ref[
                    :, h * capacity : (h + 1) * capacity, m * head_dim : (m + 1) * head_dim
                ] = packed.reshape(owners, capacity, head_dim)

    vmem = pl.BlockSpec(memory_space=pltpu.VMEM)
    whole = pl.BlockSpec(memory_space=pl.ANY)
    return pl.pallas_call(
        kernel,
        out_shape=jax.ShapeDtypeStruct((owners, heads * capacity, 2 * head_dim), BF16),
        in_specs=[pl.BlockSpec(memory_space=pltpu.SMEM), vmem] + [whole] * (len(received) + 2),
        out_specs=vmem,
        scratch_shapes=[
            pltpu.VMEM((count + 1, rows, width), BF16),
            pltpu.SemaphoreType.DMA((count + 1,)),
        ],
        compiler_params=pltpu.CompilerParams(vmem_limit_bytes=VMEM_LIMIT),
    )(scalar(core), slot_row, own, *received, ready)


def attend(blocks, members, capacity):
    sources, rows, width = blocks.shape
    head_dim = width // 2
    heads = rows // capacity
    slots = sources * capacity
    scale = head_dim ** (-0.5)

    def kernel(block_ref, member_ref, out_ref):
        query = iota((slots, slots), 0)
        key = iota((slots, slots), 1)
        for h in range(heads):
            here = slice(h * capacity, (h + 1) * capacity)
            keys = block_ref[:, here, :head_dim].reshape(slots, head_dim)
            values = block_ref[:, here, head_dim:].reshape(slots, head_dim)
            member = member_ref[h]
            same = lax.dot_general(
                member, member, (((0,), (0,)), ((), ())), preferred_element_type=F32
            )
            scores = lax.dot_general(
                keys, keys, (((1,), (1,)), ((), ())), preferred_element_type=F32
            )
            scores = jnp.where(query == key, -100000.0, scores * scale)
            scores = jnp.where((same > 0.5) & (key <= query), scores, -1e30)
            row_max = jnp.max(scores, axis=1, keepdims=True)
            weights = jnp.exp(scores - row_max)
            total = jnp.sum(weights, axis=1, keepdims=True)
            probabilities = (weights / total).astype(BF16)
            result = jnp.dot(probabilities, values, preferred_element_type=F32).astype(BF16)
            out_ref[:, here, :] = result.reshape(sources, capacity, head_dim)

    return vmem_call(
        kernel, jax.ShapeDtypeStruct((sources, rows, head_dim), BF16), (False, False)
    )(blocks, members)


def unpack(returned, slot_col, capacity):
    owners, height, head_dim = returned.shape
    rows, heads = slot_col.shape
    slots = owners * capacity

    def kernel(block_ref, slot_ref, out_ref):
        for h in range(heads):
            block = block_ref[:, h * capacity : (h + 1) * capacity, :].reshape(slots, head_dim)
            place = slot_ref[:, h : h + 1] == iota((rows, slots), 1)
            out_ref[:, h * head_dim : (h + 1) * head_dim] = jnp.dot(
                place.astype(BF16), block, preferred_element_type=F32
            ).astype(BF16)

    return vmem_call(
        kernel, jax.ShapeDtypeStruct((rows, heads * head_dim), BF16), (False, False)
    )(returned, slot_col)


CLU = ("zq", "zr")


def shifted(block, step, axis):
    size = lax.axis_size(axis)
    return lax.ppermute(block, axis, [(i, (i + step) % size) for i in range(size)])


def body(tokens, proj_weight, clusters):
    rows, depth = tokens.shape[1:]
    owners = lax.axis_size(CLU)
    me = lax.axis_index(CLU)
    heads = clusters.shape[2]
    shard = proj_weight.shape[0]
    width = 2 * proj_weight.shape[2]
    head_dim = proj_weight.shape[2] // heads
    capacity = 2 * rows // owners
    chips = lax.axis_size("x")

    pieces = cut_tokens(tokens[0], lax.axis_index("core"), chips)
    ids = clusters[0].T.astype(BF16).reshape(-1, 128)
    ids = jnp.pad(ids, ((0, shard - ids.shape[0]), (0, 0)))
    own = jnp.concatenate([proj_weight.reshape(shard, width), ids], axis=1)
    own, pieces = lax.optimization_barrier((own, pieces))
    pieces = lax.all_to_all(pieces, "x", split_axis=0, concat_axis=0, tiled=True)

    four = lax.all_gather(own, "zq", axis=0)
    below = shifted(four, 1, CLU)
    above = shifted(four, -1, CLU)
    low = shifted(four[:2], 2, CLU)
    later, pieces = lax.optimization_barrier((four[2:], pieces))
    high = shifted(later, -2, CLU)
    parts = [four, below, above, low, high]
    ring = assemble(parts, [(0, 0), (3, 0), (1, 0), (2, 0), (2, 2)], me, width)
    slot_row, slot_col = routing(clusters[0], owners, capacity)
    ring, slot_row = lax.optimization_barrier((ring, slot_row))
    other = lax.ppermute(ring, "core", [(0, 1), (1, 0)])
    steps = (2, -1, 1, 0)
    *sent, kept = project(pieces, ring, other, lax.axis_index("x"), steps)
    received, ready = exchange_x(sent, steps[:-1])
    outgoing = pack(
        kept, received, ready, slot_row, lax.axis_index("core"), owners, capacity, head_dim
    )
    incoming = lax.all_to_all(outgoing, CLU, split_axis=0, concat_axis=0, tiled=True)

    by_class = jnp.stack(
        [part[:, :16, width:] for part in (four, above, jnp.concatenate([low, high]), below)]
    )
    by_class = jnp.roll(by_class, lax.axis_index("zr"), axis=0)
    all_ids = by_class.transpose(1, 0, 2, 3).reshape((owners,) + by_class.shape[2:])
    members = owned_members(all_ids, me, heads, capacity)
    replies = attend(incoming, members, capacity)
    returned = lax.all_to_all(replies, CLU, split_axis=0, concat_axis=0, tiled=True)
    return unpack(returned, slot_col, capacity)[None]


def solution(mesh):
    ctx, clu, tp = (mesh.shape[name] for name in mesh.axis_names)
    fine = jax.sharding.Mesh(
        mesh.devices.reshape(ctx // 2, 2, clu // 4, 4, tp), ("x", "core") + CLU + ("tp",)
    )
    ctx_axes = ("x", "core")
    return jax.shard_map(
        body,
        mesh=fine,
        in_specs=(
            P(ctx_axes, CLU, None),
            P(ctx_axes + CLU, None, "tp"),
            P(ctx_axes, CLU, "tp"),
        ),
        out_specs=P(ctx_axes, CLU, "tp"),
        check_vma=False,
    )
```
